32 devices in a mesh: space: 16 (over z, y, x), batch: 2 (over core).
Axes of the slice: x: 2, y: 2, z: 4, core: 2. Of those that a mesh axis runs over, the one named last changes fastest.
Arguments:
- volume: bfloat16 [4, 2, 64, 128, 128], P(None, 'batch', 'space'), may hold values from -72 to 72
- kernel_one: bfloat16 [108, 32], replicated, may hold values from -0.625 to 0.625
- kernel_two: bfloat16 [864, 64], replicated, may hold values from -0.21875 to 0.21875
- cotangent: bfloat16 [64, 2, 16, 1024], P(None, 'batch', 'space'), may hold values from -6 to 6
Outputs:
- features: bfloat16 [64, 2, 16, 1024], P(None, 'batch', None, 'space')
- factor_in_one: float32 [108, 108], replicated
- factor_in_two: float32 [864, 864], replicated
- factor_out_one: float32 [32, 32], replicated
- factor_out_two: float32 [64, 64], replicated
- weight_grad_one: float32 [108, 32], replicated
- weight_grad_two: float32 [864, 64], replicated
The draws below stay inside these ranges and needn't reach their ends.
All inputs are finite; a program needn't handle non-finite values.
Results may differ from the reference program's by a relative error of at most 0.007.
Values may be sent and summed in bfloat16 or wider, within the bound.
No kernel may reach another device: no remote copies, remote signals or barrier semaphores. Data moves between devices by JAX's collectives and lax.ppermute only.
A program may use at most 128 MiB of HBM per device.

```python
import math
import jax
import jax.numpy as jnp
from jax import lax

C0 = 4
C1 = 32
C2 = 64
DZ = 4
PLANE = 128
BATCH = 2
NZ = 64
K1 = 108
K2 = 864
N_SPACE = 16


def draw_volume(key, part):
    key = jax.random.fold_in(key, 11)
    noise_key, plane_key, column_key = jax.random.split(key, 3)
    full_shape = (C0, BATCH, NZ, PLANE, PLANE)
    plane_scale = jnp.exp(jax.random.uniform(plane_key, (C0, BATCH, NZ, 1, 1), jnp.float32, math.log(0.3), math.log(3.0)))
    column_scale = jnp.exp(jax.random.uniform(column_key, (C0, 1, 1, 1, PLANE), jnp.float32, math.log(0.5), math.log(2.0)))
    rising = jnp.exp(math.log(3.0) * jnp.arange(NZ, dtype=jnp.float32) / (NZ - 1)).reshape(1, 1, NZ, 1, 1)
    values_raw = jax.random.truncated_normal(noise_key, -4.0, 4.0, full_shape, jnp.float32)
    return (values_raw * plane_scale * rising * column_scale).astype(jnp.bfloat16)


def steps_of(rng, extent, shards, low, largest):
    def one(axis_at, parts):
        heights = jax.random.uniform(jax.random.fold_in(jax.random.fold_in(rng, 6), axis_at), (parts,), jnp.float32, low / len(shards), largest / len(shards))
        return jnp.repeat(jnp.exp(heights), extent[axis_at] // parts).reshape((-1,) + (1,) * (len(extent) - axis_at - 1))

    level = one(*shards[0])
    for cut in shards[1:]:
        level = level * one(*cut)
    return level


def gaussian(key, extent, spread, limit, cuts=(), kind=jnp.bfloat16):
    level = steps_of(key, extent, cuts, -0.22, 0.18) if cuts else 1.0
    entries = jax.random.normal(key, extent, jnp.float32) * spread * level
    return jnp.minimum(jnp.maximum(entries, -limit), limit).astype(kind)


def setup_inputs(seed: int = 0) -> dict:
    seeds = jax.random.split(jax.random.key(seed), 5)
    return {
        "volume": draw_volume(jax.random.fold_in(seeds[4], 71), 0),
        "kernel_one": gaussian(seeds[1], (K1, C1), K1 ** -0.5, 0.625),
        "kernel_two": gaussian(seeds[2], (K2, C2), K2 ** -0.5, 0.21875),
        "cotangent": gaussian(seeds[3], (C2, BATCH, NZ // 4, (PLANE // 4) * (PLANE // 4)), 1.0, 6.0, ((1, 2), (2, 16))),
    }


def gelu_slope(value):
    inner = 0.7978845608028654 * (value + 0.044715 * value * value * value)
    tangent = jnp.tanh(inner)
    return 0.5 * (1.0 + tangent) + 0.5 * value * (1.0 - tangent * tangent) * 0.7978845608028654 * (1.0 + 3.0 * 0.044715 * value * value)

def build_patches(padded):
    plane_count = (padded.shape[2] - 1) // 2
    row_count = (padded.shape[3] - 1) // 2
    col_count = (padded.shape[4] - 1) // 2
    pieces = []
    for depth_off in range(3):
        for row_off in range(3):
            for col_off in range(3):
                pieces.append(padded[:, :, depth_off:depth_off + 2 * plane_count:2, row_off:row_off + 2 * row_count:2, col_off:col_off + 2 * col_count:2])
    return jnp.stack(pieces, axis=1).reshape(padded.shape[0] * 27, -1)

def gram(first_op, second_op):
    return lax.dot_general(first_op, second_op, (((1,), (1,)), ((), ())), preferred_element_type=jnp.float32)

def convolve(field, kernel):
    kernel_taps = kernel.astype(jnp.float32).reshape(field.shape[0], 3, 3, 3, kernel.shape[1])
    return lax.conv_general_dilated(field.astype(jnp.float32), kernel_taps, (2, 2, 2), ((1, 0), (1, 0), (1, 0)), dimension_numbers=('CNDHW', 'IDHWO', 'CNDHW'), precision=lax.Precision.HIGHEST)

def full_margin(field):
    return jnp.pad(field, ((0, 0), (0, 0), (1, 0), (1, 0), (1, 0)))

def factor_sums(padded, grads, plane_block, blocks):
    rows_k = padded.shape[0] * 27
    grad_chan = grads.shape[0]

    def accumulate(block_index, totals):
        first_plane = (block_index * (2 * plane_block)).astype(jnp.int32)
        slab = lax.dynamic_slice_in_dim(padded, first_plane, 2 * plane_block + 1, axis=2)
        patches = build_patches(slab)
        grad_first = (block_index * plane_block).astype(jnp.int32)
        grad_block = lax.dynamic_slice_in_dim(grads, grad_first, plane_block, axis=2).reshape(grad_chan, -1)
        return (totals[0] + gram(patches, patches), totals[1] + gram(grad_block, grad_block), totals[2] + gram(patches, grad_block))
    initial = (jnp.zeros((rows_k, rows_k), jnp.float32), jnp.zeros((grad_chan, grad_chan), jnp.float32), jnp.zeros((rows_k, grad_chan), jnp.float32))
    return lax.fori_loop(0, blocks, accumulate, initial)

def reference(volume, kernel_one, kernel_two, cotangent):
    pre_one = convolve(volume, kernel_one)
    hidden = jax.nn.gelu(pre_one, approximate=True).astype(jnp.bfloat16)
    pre_two, pullback = jax.vjp(lambda field: convolve(field, kernel_two), hidden.astype(jnp.float32))
    features = jax.nn.gelu(pre_two, approximate=True).astype(jnp.bfloat16).reshape(C2, BATCH, NZ // 4, -1)
    total_one = BATCH * (NZ // 2) * (PLANE // 2) * (PLANE // 2)
    total_two = BATCH * (NZ // 4) * (PLANE // 4) * (PLANE // 4)
    cot_field = cotangent.reshape(C2, BATCH, NZ // 4, PLANE // 4, PLANE // 4).astype(jnp.float32)
    grad_two = (cot_field * (1.0 / math.sqrt(total_two)) * gelu_slope(pre_two)).astype(jnp.bfloat16)
    grad_hidden = pullback(grad_two.astype(jnp.float32))[0]
    grad_one = (grad_hidden * gelu_slope(pre_one)).astype(jnp.bfloat16)
    in_one, out_one, weight_one = factor_sums(full_margin(volume), grad_one, DZ // 2, N_SPACE)
    in_two, out_two, weight_two = factor_sums(full_margin(hidden), grad_two, DZ // 4, N_SPACE)
    return (features, in_one / total_one, in_two / total_two, out_one, out_two, weight_one, weight_two)
```

```python
import functools
import math

import jax
import jax.numpy as jnp
import numpy as np
from jax import lax
from jax.experimental import pallas as pl
from jax.experimental.pallas import tpu as pltpu
from jax.sharding import PartitionSpec as P

F32 = jnp.float32
BF16 = jnp.bfloat16
LANES = 128
TAPS = 27
MIB = 1024 * 1024


def up_to(count, unit):
    return -(-count // unit) * unit


def split_columns(plane, quarter):
    table = np.zeros((4, plane, 5, 4, quarter), np.float32)
    for group in range(4):
        for q in range(5):
            for cell in range(quarter):
                x = 4 * cell + q - 1
                if 0 <= x < plane:
                    table[group, x, q, group, cell] = 1.0
    return table.reshape(4 * plane, 5 * 4 * quarter)


def patch_rows(channels, first, planes, hidden_planes, rows):
    width = up_to(25 * channels * planes, 16)
    table = np.zeros((len(hidden_planes), 2, 2, rows, width), np.float32)
    for at, j in enumerate(hidden_planes):
        for a in range(3):
            plane = 2 * j + a - first
            if not 0 <= plane < planes:
                continue
            for py, px, c, b, e in np.ndindex(2, 2, channels, 3, 3):
                source = (((2 * px + e) * channels + c) * planes + plane) * 5 + 2 * py + b
                table[at, py, px, c * TAPS + a * 9 + b * 3 + e, source] = 1.0
    return table.reshape(len(hidden_planes) * 4, rows, width)


def dot(first, second):
    return jnp.dot(first, second, preferred_element_type=F32)


def dot_nt(first, second):
    return lax.dot_general(first, second, (((1,), (1,)), ((), ())), preferred_element_type=F32)


def gelu_parts(value):
    square = value * value
    tangent = jnp.tanh(0.7978845608028654 * (value + 0.044715 * value * square))
    half = 0.5 * (1.0 + tangent)
    return value * half, half, tangent, square


def gelu_and_slope(value):
    act, half, tangent, square = gelu_parts(value)
    slope = half + 0.5 * value * (1.0 - tangent * tangent) * (
        0.7978845608028654 * (1.0 + 3.0 * 0.044715 * square)
    )
    return act, slope


def prepare_kernel(k1t_ref, k2t_ref, halo_rows_ref, own_rows_ref, halo_wide_ref, own_wide_ref, back_ref, k2_rows):
    hidden, rows_one = k1t_ref.shape
    rows_pad = halo_rows_ref.shape[1]
    k1t = jnp.pad(k1t_ref[...].astype(F32), ((0, 0), (0, rows_pad - rows_one))).astype(BF16)
    for rows_ref, wide_ref in ((halo_rows_ref, halo_wide_ref), (own_rows_ref, own_wide_ref)):
        for block in range(rows_ref.shape[0]):
            wide_ref[block * hidden : (block + 1) * hidden, :] = dot(k1t, rows_ref[block]).astype(BF16)
    out_chan, rows_two = k2t_ref.shape
    for at in range(0, rows_two, LANES):
        tall = min(LANES, rows_two - at)
        block = k2t_ref[:, at : at + tall].astype(F32)
        if tall < LANES:
            block = jnp.pad(block, ((0, 0), (0, LANES - tall)))
        k2_rows[at : at + tall, :out_chan] = block.T[:tall, :]
    taps = [k2_rows[pl.ds(tap, hidden, stride=TAPS), :][:, :out_chan] for tap in range(TAPS)]
    nothing = jnp.zeros_like(taps[0])

    def tap_for(parity, shift):
        if parity == 0:
            return 1 if shift == 0 else None
        return 2 if shift == 0 else 0

    for j in (1, 2):
        for py in range(2):
            for px in range(2):
                blocks = []
                for above in range(2):
                    a = {(1, 0): 1, (2, 0): 2, (2, 1): 0}.get((j, above))
                    for sy in range(2):
                        for sx in range(2):
                            b, e = tap_for(py, sy), tap_for(px, sx)
                            there = a is not None and b is not None and e is not None
                            blocks.append(taps[a * 9 + b * 3 + e] if there else nothing)
                start = ((j - 1) * 4 + py * 2 + px) * hidden
                back_ref[start : start + hidden, :] = jnp.concatenate(blocks, axis=1).astype(BF16)


def split_cells(planes, split_ref, cells_ref, rows_scr, lhs_scr, cells_scr):
    plane = planes[0].shape[0]
    pitch = plane + 8
    for at, source in enumerate(planes):
        start = at * pitch
        rows_scr[start : start + 8, :] = jnp.zeros((8, plane), F32)
        rows_scr[start + 8 : start + pitch, :] = source[...].astype(F32)
    for pair in range(len(planes) // 2):
        pieces = []
        for member in range(2):
            start = (pair * 2 + member) * pitch + 8
            tiles = [rows_scr[pl.ds(start + t, 8, stride=16), :] for t in range(-1, 16)]
            for q in range(5):
                pieces.append(jnp.concatenate([tiles[4 * group + q] for group in range(4)], axis=1))
        lhs_scr[pair * 80 : (pair + 1) * 80, :] = jnp.concatenate(pieces, axis=0).astype(BF16)
    total_rows = len(planes) * 40
    chunk = 160
    for part in range(total_rows // chunk):
        product = dot(lhs_scr[part * chunk : (part + 1) * chunk, :], split_ref[...])
        for q in range(5):
            start = q * total_rows + part * chunk
            cells_scr[start : start + chunk, :] = product[:, q * LANES : (q + 1) * LANES]
    filled = 5 * total_rows
    width = cells_ref.shape[0]
    if filled < 8 * width:
        cells_scr[filled : 8 * width, :] = jnp.zeros((8 * width - filled, LANES), F32)
    for yh in range(8):
        cells_ref[:, yh * LANES : (yh + 1) * LANES] = cells_scr[pl.ds(yh, width, stride=8), :].astype(BF16)


def own_kernel(
    vol_ref, wide_ref, split_ref, rows_ref,
    part_ref, act_ref, slope_ref, p1_ref, in_one_ref, rows_scr, lhs_scr, cells_scr, cells_ref,
):
    channels, own = vol_ref.shape[0], vol_ref.shape[1]
    planes = [vol_ref.at[c, z] for c in range(channels) for z in range(own)]
    split_cells(planes, split_ref, cells_ref, rows_scr, lhs_scr, cells_scr)
    pre = dot(wide_ref[...], cells_ref[...])
    tall = part_ref.shape[0]
    part_ref[...] = pre[:tall, :]
    quarter = tall // 4
    for at in range(0, tall, quarter):
        act, slope = gelu_and_slope(pre[tall + at : tall + at + quarter, :])
        act_ref[at : at + quarter, :] = act
        slope_ref[at : at + quarter, :] = slope
    blocks, rows_pad, width = rows_ref.shape
    p1 = dot(rows_ref[...].reshape(blocks * rows_pad, width), cells_ref[...]).astype(BF16)
    total = jnp.zeros((rows_pad, rows_pad), F32)
    for block in range(blocks):
        piece = p1[block * rows_pad : (block + 1) * rows_pad, :]
        p1_ref[block] = piece
        if block >= blocks // 2:
            total += dot_nt(piece, piece)
    in_one_ref[...] = total


def forward_kernel(
    scale, halo_ref, wide_ref, split_ref, part_ref, act_ref, k2t_ref, cot_ref,
    grad_ref, p2_ref, slope_ref, cells_ref, *rest,
):
    feat_refs, (rows_scr, lhs_scr, cells_scr, p2_scr, feat_scr) = rest[:-5], rest[-5:]
    channels, halo = halo_ref.shape[0], halo_ref.shape[1]
    planes = [halo_ref.at[c, z] for c in range(channels) for z in range(halo)]
    split_cells(planes, split_ref, cells_ref, rows_scr, lhs_scr, cells_scr)
    cells = cells_ref.shape[1]
    lane = lax.broadcasted_iota(jnp.int32, (1, cells), 1)
    side = math.isqrt(cells)
    not_left = (lane % side) != 0
    not_top = lane >= side
    tall = part_ref.shape[0]
    hidden = tall // 4
    rows_two = hidden * TAPS
    for j in (2, 1, 0):
        if j < 2:
            pre = dot(wide_ref[j * tall : (j + 1) * tall, :], cells_ref[...])
            if j == 1:
                pre = pre + part_ref[...]
        for parity in range(4):
            rows = slice(parity * hidden, (parity + 1) * hidden)
            if j == 2:
                act = act_ref[rows, :]
            elif j == 1:
                act, slope = gelu_and_slope(pre[rows, :])
                slope_ref[rows, :] = slope
            else:
                act = gelu_parts(pre[rows, :])[0]
            py, px = parity // 2, parity % 2
            for b in ((1,) if py == 0 else (2, 0)):
                for e in ((1,) if px == 0 else (2, 0)):
                    moved = act
                    distance = (side if b == 0 else 0) + (1 if e == 0 else 0)
                    if distance:
                        moved = pltpu.roll(act, distance, axis=1)
                    if b == 0:
                        moved = jnp.where(not_top, moved, 0.0)
                    if e == 0:
                        moved = jnp.where(not_left, moved, 0.0)
                    for k in range(cells // LANES):
                        start = k * rows_two + j * 9 + b * 3 + e
                        p2_scr[pl.ds(start, hidden, stride=TAPS), :] = moved[:, k * LANES : (k + 1) * LANES]
    for k in range(cells // LANES):
        p2_ref[:rows_two, k * LANES : (k + 1) * LANES] = p2_scr[k * rows_two : (k + 1) * rows_two, :].astype(BF16)
    p2_ref[rows_two:, :] = jnp.zeros((p2_ref.shape[0] - rows_two, cells), BF16)
    act, slope = gelu_and_slope(dot(k2t_ref[...], p2_ref[:rows_two, :]))
    grad_ref[...] = (cot_ref[...].astype(F32) * scale * slope).astype(BF16)
    owned = cells // feat_scr.shape[0]
    rows = act.shape[0] * owned // LANES
    count = LANES // owned
    place = lax.broadcasted_iota(jnp.int32, (1, LANES), 1) // owned
    for k in range(cells // LANES):
        tile = act[:, k * LANES : (k + 1) * LANES]
        for u in range(count):
            total = jnp.zeros((rows, LANES), F32)
            for m in range(count):
                block = tile[m * rows : (m + 1) * rows, :]
                if m != u:
                    block = pltpu.roll(block, ((m - u) * owned) % LANES, axis=1)
                total = jnp.where(place == m, block, total)
            if rows < feat_scr.shape[1]:
                total = jnp.pad(total, ((0, feat_scr.shape[1] - rows), (0, 0)))
            feat_scr[k * count + u] = total.astype(BF16)
    owners = feat_refs[0].shape[0]
    cube = lax.axis_index("space") // owners
    for change, feat_ref in enumerate(feat_refs):
        feat_ref[...] = feat_scr[pl.ds((cube ^ change) * owners, owners)]


def large_places(rows_two, out_chan):
    panels = -(-rows_two // LANES)
    pairs = (panels + 1) // 2
    middle = pairs // 2 * 2
    names = [("block", i, j) for j in range(middle, panels) for i in range(middle)]
    names += [("block", i, j) for j in range(middle) for i in range(j)]
    names += [("block", i, j) for j in range(middle, panels) for i in range(middle, j)]
    names += [("pair", p) for p in range(pairs)]
    cross = middle * (panels - middle)
    weights = [("weight_two", j) for j in range(panels - 1)]
    half = (len(names) * LANES + len(weights) * out_chan) // 2
    early = (half - cross * LANES) // out_chan
    order = [(name, LANES) for name in names[:cross]] + [(name, out_chan) for name in weights[:early]]
    order += [(name, LANES) for name in names[cross:]] + [(name, out_chan) for name in weights[early:]]
    places, at = {}, 0
    for name, rows in order:
        places[name] = at
        at += rows
    return panels, middle, places, at


def square_iotas():
    return (
        lax.broadcasted_iota(jnp.int32, (LANES, LANES), 0),
        lax.broadcasted_iota(jnp.int32, (LANES, LANES), 1),
    )


def diagonal_row(block):
    row, col = square_iotas()
    return jnp.sum(jnp.where(row == col, block, 0.0), axis=0, keepdims=True)


def two_in_one(upper, lower):
    row, col = square_iotas()
    return jnp.where(row <= col, upper, lower)


def first_of(block, turned):
    row, col = square_iotas()
    return jnp.where(row <= col, block, turned)


def second_of(block, turned, diagonal):
    row, col = square_iotas()
    return jnp.where(row > col, block, jnp.where(row == col, diagonal, turned))


def square(block):
    return jnp.pad(block, ((0, LANES - block.shape[0]), (0, LANES - block.shape[1])))


def padded_lanes(block):
    return jnp.pad(block, ((0, 0), (0, LANES - block.shape[1])))


def put(packed, at, block):
    half = packed.shape[1]
    done = 0
    while done < block.shape[0]:
        side, row = divmod(at + done, half)
        count = min(block.shape[0] - done, half - row)
        packed[side, row : row + count, :] = block[done : done + count, :].astype(BF16)
        done += count


def sums_kernel(
    places, rows_two, p2_ref, grad_ref, mine_ref, other_ref, done_ref, packed, product_scr, sems,
):
    done_ref[...] = jnp.zeros_like(done_ref)
    panels = p2_ref.shape[0] // LANES
    used = rows_two - (panels - 1) * LANES
    lane = lax.broadcasted_iota(jnp.int32, (1, LANES), 1)
    weight_two = dot_nt(grad_ref[...], p2_ref[...])
    out_chan = weight_two.shape[0]
    last = weight_two[:, (panels - 1) * LANES :]
    spare = LANES - used
    diagonals = []
    for j in range(0, panels, 2):
        wide = min(2, panels - j)
        tall = (j + wide) * LANES
        product = product_scr.at[(j // 2) % 2]
        product[:tall, : wide * LANES] = dot_nt(p2_ref[:tall, :], p2_ref[j * LANES : tall, :])
        for k in range(wide):
            columns = slice(k * LANES, (k + 1) * LANES)
            for i in range(j + k):
                block = product[i * LANES : (i + 1) * LANES, columns]
                if j + k == panels - 1 and i * spare < used:
                    piece = pltpu.roll(last, used - i * spare, axis=1)
                    top = jnp.where(lane >= used, piece, block[:out_chan, :])
                    block = jnp.concatenate([top, block[out_chan:, :]], axis=0)
                put(packed, places["block", i, j + k], block)
        first = product[j * LANES : (j + 1) * LANES, :LANES]
        if wide == 2:
            second = product[(j + 1) * LANES : tall, LANES:]
        else:
            second = square(dot_nt(grad_ref[...], grad_ref[...]))
        diagonals.append(diagonal_row(second))
        block = two_in_one(first, second)
        if wide == 1:
            row, _ = square_iotas()
            for at, diagonal in enumerate(diagonals):
                block = jnp.where(row == used + at, diagonal, block)
        put(packed, places["pair", j // 2], block)
    for j in range(panels - 1):
        put(packed, places["weight_two", j], weight_two[:, j * LANES : (j + 1) * LANES])
    core = lax.axis_index("batch")
    mine = pltpu.make_async_copy(packed.at[core], mine_ref, sems.at[0])
    other = pltpu.make_async_copy(packed.at[1 - core], other_ref, sems.at[1])
    other.start()
    mine.start()
    other.wait()
    mine.wait()


def shifted_up(source, scr):
    out_chan, cells = source.shape
    side = math.isqrt(cells)
    lane = lax.broadcasted_iota(jnp.int32, (1, cells), 1)
    value = source[...].astype(F32)
    for sy in range(2):
        for sx in range(2):
            moved = value
            distance = sy * side + sx
            if distance:
                moved = pltpu.roll(value, cells - distance, axis=1)
            if sy:
                moved = jnp.where(lane < cells - side, moved, 0.0)
            if sx:
                moved = jnp.where((lane % side) != side - 1, moved, 0.0)
            at = (2 * sy + sx) * out_chan
            scr[at : at + out_chan, :] = moved.astype(BF16)


def low_kernel(
    grad_ref, back_ref, slope_ref, p1_ref, cells_ref, rows_ref, in_one_ref, done_ref,
    in_one_out, low_out, high_ref, scr,
):
    _, rows_pad, _ = p1_ref.shape
    part, _, width = rows_ref.shape
    extra = dot(rows_ref[...].reshape(part * rows_pad, width), cells_ref[...])
    p1 = [
        (extra[at * rows_pad : (at + 1) * rows_pad, :] + p1_ref[at].astype(F32)).astype(BF16) for at in range(part)
    ]
    shifted_up(grad_ref, scr)
    tall = high_ref.shape[0]
    hidden = tall // part
    grad_hidden = dot(back_ref[:, : scr.shape[0]], scr[...])
    high_ref[...] = grad_hidden[tall:, :]
    in_one = in_one_ref[...]
    total = jnp.zeros((hidden, rows_pad + hidden), F32)
    for block in range(part):
        rows = slice(block * hidden, (block + 1) * hidden)
        piece = (grad_hidden[rows, :] * slope_ref[rows, :]).astype(BF16)
        in_one += dot_nt(p1[block], p1[block])
        total += dot_nt(piece, jnp.concatenate([p1[block], piece], axis=0))
    in_one_out[...] = in_one
    low_out[...] = total


def high_kernel(
    above_ref, back_ref, high_ref, slope_ref, p1_ref, in_one_ref, low_ref, out_ref, scr,
):
    shifted_up(above_ref, scr)
    blocks, rows_pad, _ = p1_ref.shape
    part = blocks // 2
    tall, reach = high_ref.shape[0], scr.shape[0]
    hidden = tall // part
    grad_hidden = high_ref[...] + dot(back_ref[tall:, reach:], scr[...])
    total = low_ref[...]
    for block in range(part):
        rows = slice(block * hidden, (block + 1) * hidden)
        piece = (grad_hidden[rows, :] * slope_ref[rows, :]).astype(BF16)
        total += dot_nt(piece, jnp.concatenate([p1_ref[part + block], piece], axis=0))
    weight_one, out_one = total[:, :rows_pad], total[:, rows_pad:]
    out_ref[...] = pack_small(in_one_ref[...], weight_one, out_one).astype(BF16)


SMALL_DIAGONAL = 108
SMALL_WEIGHT = 64
SMALL_REST = 112


def pack_small(in_one, weight_one, out_one):
    row, col = square_iotas()
    hidden = weight_one.shape[0]
    half = hidden // 2
    wide = padded_lanes(weight_one)
    out_square = square(out_one)
    block = jnp.where(row <= col, square(in_one), jnp.where(row < hidden, out_square, 0.0))
    block = jnp.where(row == SMALL_DIAGONAL, diagonal_row(out_square), block)
    first = jnp.pad(wide, ((SMALL_WEIGHT, LANES - SMALL_WEIGHT - hidden), (0, 0)))
    block = jnp.where((row >= SMALL_WEIGHT) & (row < SMALL_WEIGHT + hidden) & (col < SMALL_WEIGHT), first, block)
    turned = pltpu.roll(wide[half:, :], LANES - SMALL_WEIGHT, axis=1)
    lane = lax.broadcasted_iota(jnp.int32, (half, LANES), 1)
    rest = jnp.where(lane >= SMALL_WEIGHT, wide[:half, :], turned)
    return jnp.where(row >= SMALL_REST, jnp.pad(rest, ((SMALL_REST, 0), (0, 0))), block)


def unpack_small(block, rows_one, hidden):
    half = hidden // 2
    turned = block.T
    in_one = first_of(block, turned)[:rows_one, :rows_one]
    out_one = second_of(block, turned, block[SMALL_DIAGONAL : SMALL_DIAGONAL + 1, :])[:hidden, :hidden]
    rest = block[SMALL_REST:, :]
    lane = lax.broadcasted_iota(jnp.int32, (hidden, LANES), 1)
    high = jnp.concatenate([rest, pltpu.roll(rest, SMALL_WEIGHT, axis=1)], axis=0)
    weight_one = jnp.where(lane < SMALL_WEIGHT, block[SMALL_WEIGHT : SMALL_WEIGHT + hidden, :], high)
    return in_one, weight_one[:, :rows_one], out_one


def joined_kernel(mine_ref, came_ref, small_ref, *refs):
    feat_refs, out_ref = refs[:-1], refs[-1]
    owners = out_ref.shape[0]
    large, small = mine_ref.shape[0] // owners, small_ref.shape[0] // owners
    feat_rows = feat_refs[0].shape[1]
    for owner in range(owners):
        rows = slice(owner * large, (owner + 1) * large)
        out_ref[owner, :large, :] = (mine_ref[rows, :].astype(F32) + came_ref[rows, :].astype(F32)).astype(BF16)
        out_ref[owner, large : large + small, :] = small_ref[owner * small : (owner + 1) * small, :]
        for change, feat_ref in enumerate(feat_refs):
            start = large + small + change * feat_rows
            out_ref[owner, start : start + feat_rows, :] = feat_ref[owner]


def total_kernel(came_ref, out_ref, *feat_refs):
    owners, chunk = came_ref.shape[0], out_ref.shape[0]
    total = came_ref[0, :chunk, :].astype(F32)
    for owner in range(1, owners):
        total += came_ref[owner, :chunk, :].astype(F32)
    out_ref[...] = total.astype(BF16)
    for change, feat_ref in enumerate(feat_refs):
        rows = feat_ref.shape[1]
        start = chunk + change * rows
        for owner in range(owners):
            feat_ref[owner] = came_ref[owner, start : start + rows, :]


def pair_kernel(mine_ref, came_ref, out_ref):
    total = (mine_ref[...].astype(F32) + came_ref[...].astype(F32)).astype(BF16)
    for owner in range(out_ref.shape[0]):
        out_ref[owner] = total


def features_kernel(owned_rows, *refs):
    feat_refs, out_ref, scr = refs[:-2], refs[-2], refs[-1]
    owners, owned = out_ref.shape[1], out_ref.shape[2]
    members, rows, _ = feat_refs[0].shape
    cube = lax.axis_index("space") // members
    for change, feat_ref in enumerate(feat_refs):
        for member in range(members):
            start = pl.multiple_of(((cube ^ change) * members + member) * rows, 16)
            scr[pl.ds(start, rows), :] = feat_ref[member].astype(F32)
    for i in range(owned_rows):
        block = scr[pl.ds(i, owners, stride=rows), :]
        for m in range(LANES // owned):
            out_ref[m * owned_rows + i] = block[:, m * owned : (m + 1) * owned].astype(BF16)


def gathered_half(source_ref, half_scr):
    owners = source_ref.shape[0]
    tall = half_scr.shape[0] // owners
    for owner in range(owners):
        half_scr[owner * tall : (owner + 1) * tall, :] = source_ref[owner, :tall, :]


def unit_square():
    row, col = square_iotas()
    return jnp.where(row == col, 1.0, 0.0).astype(BF16)


def first_half_copies(middle, factor, out_ref, sems):
    rows_two, split = out_ref.shape[0], middle * LANES
    spots = [(slice(0, split), slice(split, rows_two)), (slice(split, rows_two), slice(0, split))]
    return [pltpu.make_async_copy(factor.at[spot], out_ref.at[spot], sems.at[at]) for at, spot in enumerate(spots)]


def second_half_copies(middle, factor, out_ref, sems):
    rows_two, split = out_ref.shape[0], middle * LANES
    spots = [(slice(0, split), slice(0, split)), (slice(split, rows_two), slice(split, rows_two))]
    return [pltpu.make_async_copy(factor.at[spot], out_ref.at[spot], sems.at[at]) for at, spot in enumerate(spots)]


def wait_for(copies):
    for copy in copies:
        copy.wait()


def write_first_half(places, panels, middle, scale, half_scr, factor, out_ref, sems):
    copies = first_half_copies(middle, factor, out_ref, sems)
    rows_two = out_ref.shape[0]
    split = middle * LANES
    unit = unit_square()
    for j in range(middle, panels):
        wide = min(LANES, rows_two - j * LANES)
        start = places["block", 0, j]
        panel = half_scr[start : start + split, :]
        columns = slice(j * LANES, j * LANES + wide)
        factor[:split, columns] = (panel.astype(F32) * scale)[:, :wide]
        factor[columns, :split] = (dot_nt(unit, panel) * scale)[:wide, :]
    for copy in copies:
        copy.start()


def write_second_half(places, panels, middle, scale, half_scr, factor, out_ref, sems):
    copies = second_half_copies(middle, factor, out_ref, sems)
    rows_two = out_ref.shape[0]
    half = half_scr.shape[0]
    unit = unit_square()
    used = rows_two - (panels - 1) * LANES
    pairs = (panels + 1) // 2
    start = places["pair", pairs - 1] - half
    holder = half_scr[start : start + LANES, :].astype(F32)
    for j in range(panels):
        first = middle if j >= middle else 0
        if j == middle:
            copies[0].start()
        if j % 2 == 0:
            start = places["pair", j // 2] - half
            block = half_scr[start : start + LANES, :]
            turned = dot_nt(unit, block)
            block = block.astype(F32)
            wide = min(LANES, rows_two - j * LANES)
            rows = slice(j * LANES, j * LANES + wide)
            factor[rows, rows] = (first_of(block, turned) * scale)[:wide, :wide]
            if j + 1 < panels:
                rows = slice((j + 1) * LANES, (j + 2) * LANES)
                diagonal = holder[used + j // 2 : used + j // 2 + 1, :]
                factor[rows, rows] = second_of(block, turned, diagonal) * scale
        if j == first:
            continue
        wide = min(LANES, rows_two - j * LANES)
        start = places["block", first, j] - half
        panel = half_scr[start : start + (j - first) * LANES, :]
        columns, rows = slice(j * LANES, j * LANES + wide), slice(first * LANES, j * LANES)
        factor[rows, columns] = (panel.astype(F32) * scale)[:, :wide]
        factor[columns, rows] = (dot_nt(unit, panel) * scale)[:wide, :]
    copies[1].start()


def own_half_kernel(places, panels, middle, scale, mine_ref, out_ref, half_scr, factor, sems):
    gathered_half(mine_ref, half_scr)
    core = lax.axis_index("batch")
    rest = (places, panels, middle, scale, half_scr, factor, out_ref, sems)
    pl.when(core == 0)(functools.partial(write_first_half, *rest))
    pl.when(core == 1)(functools.partial(write_second_half, *rest))
    where = (middle, factor, out_ref, sems)
    pl.when(core == 0)(lambda: wait_for(first_half_copies(*where)))
    pl.when(core == 1)(lambda: wait_for(second_half_copies(*where)))


def unpack_kernel(
    places, panels, middle, scale_one, scale_two, begun_ref, mine_ref, came_ref,
    in_one_out, in_two_ref, out_one_out, out_two_out, weight_one_out, weight_two_out,
    packed, small, factor, in_one_ref, out_one_ref, out_two_ref, weight_one_ref, weight_two_ref, sems,
):
    core = lax.axis_index("batch")
    gathered_half(mine_ref, packed.at[core])
    gathered_half(came_ref, packed.at[1 - core])
    rest = (places, panels, middle, scale_two)
    pl.when(core == 1)(functools.partial(write_first_half, *rest, packed.at[0], factor, in_two_ref, sems))
    pl.when(core == 0)(functools.partial(write_second_half, *rest, packed.at[1], factor, in_two_ref, sems))
    out_chan, rows_two = weight_two_ref.shape
    hidden, rows_one = weight_one_ref.shape
    owners = mine_ref.shape[0]
    tall_large, tall_small = packed.shape[1] // owners, small.shape[0] // owners
    for owner in range(owners):
        rows = slice(tall_large, tall_large + tall_small)
        small[owner * tall_small : (owner + 1) * tall_small, :] = mine_ref[owner, rows, :].astype(F32) + came_ref[
            owner, rows, :
        ].astype(F32)
    half = packed.shape[1]

    def get(name, count):
        side, row = divmod(places[name], half)
        return packed[side, row : row + count, :].astype(F32)

    used = rows_two - (panels - 1) * LANES
    spare = LANES - used
    lane = lax.broadcasted_iota(jnp.int32, (1, LANES), 1)
    last = jnp.zeros((out_chan, LANES), F32)
    for i in range(-(-used // spare)):
        piece = pltpu.roll(get(("block", i, panels - 1), out_chan), LANES - (used - i * spare), axis=1)
        last = jnp.where((lane >= i * spare) & (lane < (i + 1) * spare), piece, last)
    for j in range(panels - 1):
        weight_two_ref[:, j * LANES : (j + 1) * LANES] = get(("weight_two", j), out_chan)
    weight_two_ref[:, (panels - 1) * LANES :] = last[:, :used]
    copies = [pltpu.make_async_copy(weight_two_ref, weight_two_out, sems.at[2])]
    copies[0].start()
    pairs = (panels + 1) // 2
    block = get(("pair", pairs - 1), LANES)
    diagonal = block[used + pairs - 1 : used + pairs, :]
    out_two_ref[...] = second_of(block, block.T, diagonal)[:out_chan, :out_chan]
    in_one, weight_one, out_one = unpack_small(small[...], rows_one, hidden)
    in_one_ref[...] = in_one * scale_one
    weight_one_ref[...] = weight_one
    out_one_ref[...] = out_one
    results = ((in_one_ref, in_one_out), (out_one_ref, out_one_out), (out_two_ref, out_two_out))
    for at, (here, there) in enumerate(results + ((weight_one_ref, weight_one_out),)):
        copies.append(pltpu.make_async_copy(here, there, sems.at[3 + at]))
        copies[-1].start()
    wait_for(copies)
    where = (middle, factor, in_two_ref, sems)
    pl.when(core == 1)(lambda: wait_for(first_half_copies(*where)))
    pl.when(core == 0)(lambda: wait_for(second_half_copies(*where)))


def cube_size(space):
    return 8 if space % 8 == 0 else space


def exchange(parts, size):
    space = lax.axis_size("space")
    groups = [list(range(base, base + size)) for base in range(0, space, size)]
    return lax.all_to_all(parts, "space", split_axis=0, concat_axis=0, axis_index_groups=groups)


def from_partner(block, stride):
    return lax.ppermute(block, "space", [(i, i ^ stride) for i in range(lax.axis_size("space"))])


def call(kernel, out_shape, scratch=(), micros=3, mib=24, **more):
    return pl.pallas_call(
        kernel,
        out_shape=out_shape,
        scratch_shapes=list(scratch),
        cost_estimate=pl.CostEstimate(flops=int(micros * 1.1e9), bytes_accessed=1 << 20, transcendentals=0),
        compiler_params=pltpu.CompilerParams(vmem_limit_bytes=mib * MIB),
        **more,
    )


def passed_along(block, axis, distance):
    devices = range(lax.axis_size(axis))
    route = [(i - distance, i) for i in devices if i - distance in devices]
    return lax.ppermute(block, axis, route)


def swapped(block):
    return lax.ppermute(block, "batch", [(0, 1), (1, 0)])


def like(shape, kind=BF16):
    return jax.ShapeDtypeStruct(shape, kind)


def split_scratch(count, plane):
    return [
        pltpu.VMEM((count * (plane + 8), plane), F32),
        pltpu.VMEM((count * 40, 4 * plane), BF16),
        pltpu.VMEM((8 * up_to(25 * count, 16), LANES), F32),
    ]


def local(volume, kernel_one, kernel_two, cotangent):
    channels, _, own, plane, _ = volume.shape
    rows_one, hidden = kernel_one.shape
    rows_two, out_chan = kernel_two.shape
    cells = cotangent.shape[3]
    side = math.isqrt(cells)
    space = lax.axis_size("space")
    devices_all = space * lax.axis_size("batch")
    total_one = devices_all * 8 * cells
    total_two = devices_all * cells
    rows_pad = up_to(rows_one, 16)
    halo = own - 1
    halo_width = up_to(25 * channels * halo, 16)
    own_width = up_to(25 * channels * own, 16)
    tall = 4 * hidden

    vol = volume.reshape(channels, own, plane, plane)
    halo_block = passed_along(vol[:, own - halo :], "space", 1)
    halo_rows = jnp.asarray(patch_rows(channels, 0, halo, (0, 1), rows_pad), BF16)
    own_rows = jnp.asarray(patch_rows(channels, halo, own, (1, 2), rows_pad), BF16)
    split = jnp.asarray(split_columns(plane, side), BF16)
    halo_wide, own_wide, back = call(
        prepare_kernel,
        (like((2 * tall, halo_width)), like((2 * tall, own_width)), like((2 * tall, 8 * out_chan))),
        [pltpu.VMEM((rows_two, LANES), F32)],
        micros=3,
    )(kernel_one.T, kernel_two.T, halo_rows, own_rows)
    part, act_high, slope_high, p1, in_one_part = call(
        own_kernel,
        (
            like((tall, cells), F32),
            like((tall, cells), F32),
            like((tall, cells), F32),
            like((8, rows_pad, cells)),
            like((rows_pad, rows_pad), F32),
        ),
        split_scratch(channels * own, plane) + [pltpu.VMEM((own_width, cells), BF16)],
        micros=6,
    )(vol, own_wide, split, own_rows)
    panels, middle, places, large_rows = large_places(rows_two, out_chan)
    feat_rows = out_chan * cells // space // LANES
    feat_tall = up_to(feat_rows, 16)
    cube = cube_size(space)
    cubes = space // cube
    grad_two, p2, slope_low, spread, *feats = call(
        functools.partial(forward_kernel, 1.0 / math.sqrt(total_two)),
        (
            like((out_chan, cells)),
            like((panels * LANES, cells)),
            like((tall, cells), F32),
            like((halo_width, cells)),
        )
        + (like((cube, feat_tall, LANES)),) * cubes,
        split_scratch(channels * halo, plane)
        + [pltpu.VMEM((rows_two * (cells // LANES), LANES), F32), pltpu.VMEM((space, feat_tall, LANES), BF16)],
        micros=5,
    )(halo_block, halo_wide, split, part, act_high, kernel_two.T, cotangent.reshape(out_chan, cells))
    above = passed_along(grad_two, "space", -1)

    half = large_rows // 2
    small_rows = LANES
    chunk = (half + small_rows) // cube
    mine, other, done = call(
        functools.partial(sums_kernel, places, rows_two),
        (like((half, LANES)), like((half, LANES)), like((8, LANES), F32)),
        [
            pltpu.VMEM((2, half, LANES), BF16),
            pltpu.VMEM((2, panels * LANES, 2 * LANES), F32),
            pltpu.SemaphoreType.DMA((2,)),
        ],
        micros=5,
        out_specs=tuple(pl.BlockSpec(memory_space=pl.ANY if at < 2 else pltpu.VMEM) for at in range(3)),
    )(p2, grad_two)
    came = swapped(other)
    in_one_low, low, high = call(
        low_kernel,
        (like((rows_pad, rows_pad), F32), like((hidden, rows_pad + hidden), F32), like((tall, cells), F32)),
        [pltpu.VMEM((4 * out_chan, cells), BF16)],
        micros=0.1,
    )(grad_two, back, slope_low, p1, spread, halo_rows[4:], in_one_part, done)
    small = call(
        high_kernel,
        like((small_rows, LANES)),
        [pltpu.VMEM((4 * out_chan, cells), BF16)],
        micros=12,
    )(above, back, high, slope_high, p1, in_one_low, low)
    joined = call(joined_kernel, like((cube, chunk + cubes * feat_tall, LANES)), micros=1)(mine, came, small, *feats)
    total, *feats = call(
        total_kernel, (like((chunk, LANES)),) + (like((cube, feat_tall, LANES)),) * cubes, micros=1
    )(exchange(joined, cube))
    stride = cube
    while 2 * stride < space:
        total = (total.astype(F32) + from_partner(total, stride).astype(F32)).astype(BF16)
        stride *= 2
    other = from_partner(total, stride) if stride < space else jnp.zeros_like(total)
    copies = call(pair_kernel, like((cube, chunk, LANES)), micros=1)(total, other)
    mine = exchange(copies, cube)
    feats[1:] = [from_partner(feats[change], change * cube) for change in range(1, cubes)]
    mine, feats = lax.optimization_barrier((mine, feats))
    came = swapped(mine)
    features = call(
        functools.partial(features_kernel, feat_rows),
        like((out_chan, space, cells // space)),
        [pltpu.VMEM((space * feat_tall, LANES), F32)],
        micros=1,
    )(*feats)
    anywhere = pl.BlockSpec(memory_space=pl.ANY)
    begun = call(
        functools.partial(own_half_kernel, places, panels, middle, 1.0 / total_two),
        like((rows_two, rows_two), F32),
        [
            pltpu.VMEM((half, LANES), BF16),
            pltpu.VMEM((rows_two, rows_two), F32),
            pltpu.SemaphoreType.DMA((2,)),
        ],
        micros=2,
        out_specs=anywhere,
    )(mine)
    kinds = [
        like(shape, F32)
        for shape in (
            (rows_one, rows_one),
            (rows_two, rows_two),
            (hidden, hidden),
            (out_chan, out_chan),
            (hidden, rows_one),
            (out_chan, rows_two),
        )
    ]
    in_one, in_two, out_one, out_two, weight_one, weight_two = call(
        functools.partial(unpack_kernel, places, panels, middle, 1.0 / total_one, 1.0 / total_two),
        tuple(kinds),
        [
            pltpu.VMEM((2, half, LANES), BF16),
            pltpu.VMEM((small_rows, LANES), F32),
            pltpu.VMEM((rows_two, rows_two), F32),
        ]
        + [pltpu.VMEM(kind.shape, F32) for at, kind in enumerate(kinds) if at != 1]
        + [pltpu.SemaphoreType.DMA((7,))],
        micros=2,
        in_specs=[anywhere, pl.BlockSpec(memory_space=pltpu.VMEM), pl.BlockSpec(memory_space=pltpu.VMEM)],
        out_specs=(anywhere,) * 6,
        input_output_aliases={0: 1},
    )(begun, mine, came)
    features = features.reshape(out_chan, 1, space, cells // space)
    return features, in_one, in_two, out_one, out_two, weight_one.T, weight_two.T


def solution(mesh):
    placed = (P(None, "batch", "space", None, None), P(), P(), P(None, "batch", "space", None))
    return jax.shard_map(
        local,
        mesh=mesh,
        in_specs=placed,
        out_specs=(P(None, "batch", None, "space"), P(), P(), P(), P(), P(), P()),
        check_vma=False,
    )
```

```python
import functools
import math

import jax
import jax.numpy as jnp
import numpy as np
from jax import lax
from jax.experimental import pallas as pl
from jax.experimental.pallas import tpu as pltpu
from jax.sharding import PartitionSpec as P

F32 = jnp.float32
BF16 = jnp.bfloat16
LANES = 128
TAPS = 27
MIB = 1024 * 1024


def up_to(count, unit):
    return -(-count // unit) * unit


def split_columns(plane, quarter):
    table = np.zeros((4, plane, 5, 4, quarter), np.float32)
    for group in range(4):
        for q in range(5):
            for cell in range(quarter):
                x = 4 * cell + q - 1
                if 0 <= x < plane:
                    table[group, x, q, group, cell] = 1.0
    return table.reshape(4 * plane, 5 * 4 * quarter)


def patch_rows(channels, first, planes, hidden_planes, rows):
    width = up_to(25 * channels * planes, 16)
    table = np.zeros((len(hidden_planes), 2, 2, rows, width), np.float32)
    for at, j in enumerate(hidden_planes):
        for a in range(3):
            plane = 2 * j + a - first
            if not 0 <= plane < planes:
                continue
            for py, px, c, b, e in np.ndindex(2, 2, channels, 3, 3):
                source = (((2 * px + e) * channels + c) * planes + plane) * 5 + 2 * py + b
                table[at, py, px, c * TAPS + a * 9 + b * 3 + e, source] = 1.0
    return table.reshape(len(hidden_planes) * 4, rows, width)


def dot(first, second):
    return jnp.dot(first, second, preferred_element_type=F32)


def dot_nt(first, second):
    return lax.dot_general(first, second, (((1,), (1,)), ((), ())), preferred_element_type=F32)


def gelu_parts(value):
    square = value * value
    tangent = jnp.tanh(0.7978845608028654 * (value + 0.044715 * value * square))
    half = 0.5 * (1.0 + tangent)
    return value * half, half, tangent, square


def gelu_and_slope(value):
    act, half, tangent, square = gelu_parts(value)
    slope = half + 0.5 * value * (1.0 - tangent * tangent) * (
        0.7978845608028654 * (1.0 + 3.0 * 0.044715 * square)
    )
    return act, slope


def prepare_kernel(k1t_ref, k2t_ref, halo_rows_ref, own_rows_ref, halo_wide_ref, own_wide_ref, back_ref, k2_rows):
    hidden, rows_one = k1t_ref.shape
    rows_pad = halo_rows_ref.shape[1]
    k1t = jnp.pad(k1t_ref[...].astype(F32), ((0, 0), (0, rows_pad - rows_one))).astype(BF16)
    for rows_ref, wide_ref in ((halo_rows_ref, halo_wide_ref), (own_rows_ref, own_wide_ref)):
        for block in range(rows_ref.shape[0]):
            wide_ref[block * hidden : (block + 1) * hidden, :] = dot(k1t, rows_ref[block]).astype(BF16)
    out_chan, rows_two = k2t_ref.shape
    for at in range(0, rows_two, LANES):
        tall = min(LANES, rows_two - at)
        block = k2t_ref[:, at : at + tall].astype(F32)
        if tall < LANES:
            block = jnp.pad(block, ((0, 0), (0, LANES - tall)))
        k2_rows[at : at + tall, :out_chan] = block.T[:tall, :]
    taps = [k2_rows[pl.ds(tap, hidden, stride=TAPS), :][:, :out_chan] for tap in range(TAPS)]
    nothing = jnp.zeros_like(taps[0])

    def tap_for(parity, shift):
        if parity == 0:
            return 1 if shift == 0 else None
        return 2 if shift == 0 else 0

    for j in (1, 2):
        for py in range(2):
            for px in range(2):
                blocks = []
                for above in range(2):
                    a = {(1, 0): 1, (2, 0): 2, (2, 1): 0}.get((j, above))
                    for sy in range(2):
                        for sx in range(2):
                            b, e = tap_for(py, sy), tap_for(px, sx)
                            there = a is not None and b is not None and e is not None
                            blocks.append(taps[a * 9 + b * 3 + e] if there else nothing)
                start = ((j - 1) * 4 + py * 2 + px) * hidden
                back_ref[start : start + hidden, :] = jnp.concatenate(blocks, axis=1).astype(BF16)


def split_cells(planes, split_ref, cells_ref, rows_scr, lhs_scr, cells_scr):
    plane = planes[0].shape[0]
    pitch = plane + 8
    for at, source in enumerate(planes):
        start = at * pitch
        rows_scr[start : start + 8, :] = jnp.zeros((8, plane), F32)
        rows_scr[start + 8 : start + pitch, :] = source[...].astype(F32)
    for pair in range(len(planes) // 2):
        pieces = []
        for member in range(2):
            start = (pair * 2 + member) * pitch + 8
            tiles = [rows_scr[pl.ds(start + t, 8, stride=16), :] for t in range(-1, 16)]
            for q in range(5):
                pieces.append(jnp.concatenate([tiles[4 * group + q] for group in range(4)], axis=1))
        lhs_scr[pair * 80 : (pair + 1) * 80, :] = jnp.concatenate(pieces, axis=0).astype(BF16)
    total_rows = len(planes) * 40
    chunk = 160
    for part in range(total_rows // chunk):
        product = dot(lhs_scr[part * chunk : (part + 1) * chunk, :], split_ref[...])
        for q in range(5):
            start = q * total_rows + part * chunk
            cells_scr[start : start + chunk, :] = product[:, q * LANES : (q + 1) * LANES]
    filled = 5 * total_rows
    width = cells_ref.shape[0]
    if filled < 8 * width:
        cells_scr[filled : 8 * width, :] = jnp.zeros((8 * width - filled, LANES), F32)
    for yh in range(8):
        cells_ref[:, yh * LANES : (yh + 1) * LANES] = cells_scr[pl.ds(yh, width, stride=8), :].astype(BF16)


def own_kernel(
    vol_ref, wide_ref, split_ref, rows_ref,
    part_ref, act_ref, slope_ref, p1_ref, in_one_ref, rows_scr, lhs_scr, cells_scr, cells_ref,
):
    channels, own = vol_ref.shape[0], vol_ref.shape[1]
    planes = [vol_ref.at[c, z] for c in range(channels) for z in range(own)]
    split_cells(planes, split_ref, cells_ref, rows_scr, lhs_scr, cells_scr)
    pre = dot(wide_ref[...], cells_ref[...])
    tall = part_ref.shape[0]
    part_ref[...] = pre[:tall, :]
    quarter = tall // 4
    for at in range(0, tall, quarter):
        act, slope = gelu_and_slope(pre[tall + at : tall + at + quarter, :])
        act_ref[at : at + quarter, :] = act
        slope_ref[at : at + quarter, :] = slope
    blocks, rows_pad, width = rows_ref.shape
    p1 = dot(rows_ref[...].reshape(blocks * rows_pad, width), cells_ref[...]).astype(BF16)
    total = jnp.zeros((rows_pad, rows_pad), F32)
    for block in range(blocks):
        piece = p1[block * rows_pad : (block + 1) * rows_pad, :]
        p1_ref[block] = piece
        if block >= blocks // 2:
            total += dot_nt(piece, piece)
    in_one_ref[...] = total


def forward_kernel(
    scale, halo_ref, wide_ref, split_ref, part_ref, act_ref, k2t_ref, cot_ref,
    grad_ref, p2_ref, slope_ref, cells_ref, *rest,
):
    feat_refs, (rows_scr, lhs_scr, cells_scr, p2_scr, feat_scr) = rest[:-5], rest[-5:]
    channels, halo = halo_ref.shape[0], halo_ref.shape[1]
    planes = [halo_ref.at[c, z] for c in range(channels) for z in range(halo)]
    split_cells(planes, split_ref, cells_ref, rows_scr, lhs_scr, cells_scr)
    cells = cells_ref.shape[1]
    lane = lax.broadcasted_iota(jnp.int32, (1, cells), 1)
    side = math.isqrt(cells)
    not_left = (lane % side) != 0
    not_top = lane >= side
    tall = part_ref.shape[0]
    hidden = tall // 4
    rows_two = hidden * TAPS
    for j in (2, 1, 0):
        if j < 2:
            pre = dot(wide_ref[j * tall : (j + 1) * tall, :], cells_ref[...])
            if j == 1:
                pre = pre + part_ref[...]
        for parity in range(4):
            rows = slice(parity * hidden, (parity + 1) * hidden)
            if j == 2:
                act = act_ref[rows, :]
            elif j == 1:
                act, slope = gelu_and_slope(pre[rows, :])
                slope_ref[rows, :] = slope
            else:
                act = gelu_parts(pre[rows, :])[0]
            py, px = parity // 2, parity % 2
            for b in ((1,) if py == 0 else (2, 0)):
                for e in ((1,) if px == 0 else (2, 0)):
                    moved = act
                    distance = (side if b == 0 else 0) + (1 if e == 0 else 0)
                    if distance:
                        moved = pltpu.roll(act, distance, axis=1)
                    if b == 0:
                        moved = jnp.where(not_top, moved, 0.0)
                    if e == 0:
                        moved = jnp.where(not_left, moved, 0.0)
                    for k in range(cells // LANES):
                        start = k * rows_two + j * 9 + b * 3 + e
                        p2_scr[pl.ds(start, hidden, stride=TAPS), :] = moved[:, k * LANES : (k + 1) * LANES]
    for k in range(cells // LANES):
        p2_ref[:rows_two, k * LANES : (k + 1) * LANES] = p2_scr[k * rows_two : (k + 1) * rows_two, :].astype(BF16)
    p2_ref[rows_two:, :] = jnp.zeros((p2_ref.shape[0] - rows_two, cells), BF16)
    act, slope = gelu_and_slope(dot(k2t_ref[...], p2_ref[:rows_two, :]))
    grad_ref[...] = (cot_ref[...].astype(F32) * scale * slope).astype(BF16)
    owned = cells // feat_scr.shape[0]
    rows = act.shape[0] * owned // LANES
    count = LANES // owned
    place = lax.broadcasted_iota(jnp.int32, (1, LANES), 1) // owned
    for k in range(cells // LANES):
        tile = act[:, k * LANES : (k + 1) * LANES]
        for u in range(count):
            total = jnp.zeros((rows, LANES), F32)
            for m in range(count):
                block = tile[m * rows : (m + 1) * rows, :]
                if m != u:
                    block = pltpu.roll(block, ((m - u) * owned) % LANES, axis=1)
                total = jnp.where(place == m, block, total)
            if rows < feat_scr.shape[1]:
                total = jnp.pad(total, ((0, feat_scr.shape[1] - rows), (0, 0)))
            feat_scr[k * count + u] = total.astype(BF16)
    owners = feat_refs[0].shape[0]
    cube = lax.axis_index("space") // owners
    for change, feat_ref in enumerate(feat_refs):
        feat_ref[...] = feat_scr[pl.ds((cube ^ change) * owners, owners)]


def large_places(rows_two, out_chan):
    panels = -(-rows_two // LANES)
    pairs = (panels + 1) // 2
    middle = pairs // 2 * 2
    names = [("block", i, j) for j in range(middle, panels) for i in range(middle)]
    names += [("block", i, j) for j in range(middle) for i in range(j)]
    names += [("block", i, j) for j in range(middle, panels) for i in range(middle, j)]
    names += [("pair", p) for p in range(pairs)]
    cross = middle * (panels - middle)
    weights = [("weight_two", j) for j in range(panels - 1)]
    half = (len(names) * LANES + len(weights) * out_chan) // 2
    early = (half - cross * LANES) // out_chan
    order = [(name, LANES) for name in names[:cross]] + [(name, out_chan) for name in weights[:early]]
    order += [(name, LANES) for name in names[cross:]] + [(name, out_chan) for name in weights[early:]]
    places, at = {}, 0
    for name, rows in order:
        places[name] = at
        at += rows
    return panels, middle, places, at


def square_iotas():
    return (
        lax.broadcasted_iota(jnp.int32, (LANES, LANES), 0),
        lax.broadcasted_iota(jnp.int32, (LANES, LANES), 1),
    )


def diagonal_row(block):
    row, col = square_iotas()
    return jnp.sum(jnp.where(row == col, block, 0.0), axis=0, keepdims=True)


def two_in_one(upper, lower):
    row, col = square_iotas()
    return jnp.where(row <= col, upper, lower)


def first_of(block, turned):
    row, col = square_iotas()
    return jnp.where(row <= col, block, turned)


def second_of(block, turned, diagonal):
    row, col = square_iotas()
    return jnp.where(row > col, block, jnp.where(row == col, diagonal, turned))


def square(block):
    return jnp.pad(block, ((0, LANES - block.shape[0]), (0, LANES - block.shape[1])))


def padded_lanes(block):
    return jnp.pad(block, ((0, 0), (0, LANES - block.shape[1])))


def put(halves, at, block):
    half = halves[0].shape[0]
    done = 0
    while done < block.shape[0]:
        side, row = divmod(at + done, half)
        count = min(block.shape[0] - done, half - row)
        halves[side][row : row + count, :] = block[done : done + count, :].astype(BF16)
        done += count


def sums_kernel(
    places, rows_two, p2_ref, grad_ref, mine_ref, other_ref, done_ref, product_scr,
):
    done_ref[...] = jnp.zeros_like(done_ref)
    core = lax.axis_index("batch")
    rest = (places, rows_two, p2_ref, grad_ref, product_scr)
    pl.when(core == 0)(lambda: write_sums(*rest, (mine_ref, other_ref)))
    pl.when(core == 1)(lambda: write_sums(*rest, (other_ref, mine_ref)))


def write_sums(places, rows_two, p2_ref, grad_ref, product_scr, packed):
    panels = p2_ref.shape[0] // LANES
    used = rows_two - (panels - 1) * LANES
    lane = lax.broadcasted_iota(jnp.int32, (1, LANES), 1)
    weight_two = dot_nt(grad_ref[...], p2_ref[...])
    out_chan = weight_two.shape[0]
    last = weight_two[:, (panels - 1) * LANES :]
    spare = LANES - used
    diagonals = []
    for j in range(0, panels, 2):
        wide = min(2, panels - j)
        tall = (j + wide) * LANES
        product = product_scr.at[(j // 2) % 2]
        product[:tall, : wide * LANES] = dot_nt(p2_ref[:tall, :], p2_ref[j * LANES : tall, :])
        for k in range(wide):
            columns = slice(k * LANES, (k + 1) * LANES)
            for i in range(j + k):
                block = product[i * LANES : (i + 1) * LANES, columns]
                if j + k == panels - 1 and i * spare < used:
                    piece = pltpu.roll(last, used - i * spare, axis=1)
                    top = jnp.where(lane >= used, piece, block[:out_chan, :])
                    block = jnp.concatenate([top, block[out_chan:, :]], axis=0)
                put(packed, places["block", i, j + k], block)
        first = product[j * LANES : (j + 1) * LANES, :LANES]
        if wide == 2:
            second = product[(j + 1) * LANES : tall, LANES:]
        else:
            second = square(dot_nt(grad_ref[...], grad_ref[...]))
        diagonals.append(diagonal_row(second))
        block = two_in_one(first, second)
        if wide == 1:
            row, _ = square_iotas()
            for at, diagonal in enumerate(diagonals):
                block = jnp.where(row == used + at, diagonal, block)
        put(packed, places["pair", j // 2], block)
    for j in range(panels - 1):
        put(packed, places["weight_two", j], weight_two[:, j * LANES : (j + 1) * LANES])


def shifted_up(source, scr):
    out_chan, cells = source.shape
    side = math.isqrt(cells)
    lane = lax.broadcasted_iota(jnp.int32, (1, cells), 1)
    value = source[...].astype(F32)
    for sy in range(2):
        for sx in range(2):
            moved = value
            distance = sy * side + sx
            if distance:
                moved = pltpu.roll(value, cells - distance, axis=1)
            if sy:
                moved = jnp.where(lane < cells - side, moved, 0.0)
            if sx:
                moved = jnp.where((lane % side) != side - 1, moved, 0.0)
            at = (2 * sy + sx) * out_chan
            scr[at : at + out_chan, :] = moved.astype(BF16)


def low_kernel(
    grad_ref, back_ref, slope_ref, p1_ref, cells_ref, rows_ref, in_one_ref, done_ref,
    in_one_out, low_out, high_ref, scr,
):
    _, rows_pad, _ = p1_ref.shape
    part, _, width = rows_ref.shape
    extra = dot(rows_ref[...].reshape(part * rows_pad, width), cells_ref[...])
    p1 = [
        (extra[at * rows_pad : (at + 1) * rows_pad, :] + p1_ref[at].astype(F32)).astype(BF16) for at in range(part)
    ]
    shifted_up(grad_ref, scr)
    tall = high_ref.shape[0]
    hidden = tall // part
    grad_hidden = dot(back_ref[:, : scr.shape[0]], scr[...])
    high_ref[...] = grad_hidden[tall:, :]
    in_one = in_one_ref[...]
    total = jnp.zeros((hidden, rows_pad + hidden), F32)
    for block in range(part):
        rows = slice(block * hidden, (block + 1) * hidden)
        piece = (grad_hidden[rows, :] * slope_ref[rows, :]).astype(BF16)
        in_one += dot_nt(p1[block], p1[block])
        total += dot_nt(piece, jnp.concatenate([p1[block], piece], axis=0))
    in_one_out[...] = in_one
    low_out[...] = total


def high_kernel(
    above_ref, back_ref, high_ref, slope_ref, p1_ref, in_one_ref, low_ref, out_ref, scr,
):
    shifted_up(above_ref, scr)
    blocks, rows_pad, _ = p1_ref.shape
    part = blocks // 2
    tall, reach = high_ref.shape[0], scr.shape[0]
    hidden = tall // part
    grad_hidden = high_ref[...] + dot(back_ref[tall:, reach:], scr[...])
    total = low_ref[...]
    for block in range(part):
        rows = slice(block * hidden, (block + 1) * hidden)
        piece = (grad_hidden[rows, :] * slope_ref[rows, :]).astype(BF16)
        total += dot_nt(piece, jnp.concatenate([p1_ref[part + block], piece], axis=0))
    weight_one, out_one = total[:, :rows_pad], total[:, rows_pad:]
    out_ref[...] = pack_small(in_one_ref[...], weight_one, out_one).astype(BF16)


SMALL_DIAGONAL = 108
SMALL_WEIGHT = 64
SMALL_REST = 112


def pack_small(in_one, weight_one, out_one):
    row, col = square_iotas()
    hidden = weight_one.shape[0]
    half = hidden // 2
    wide = padded_lanes(weight_one)
    out_square = square(out_one)
    block = jnp.where(row <= col, square(in_one), jnp.where(row < hidden, out_square, 0.0))
    block = jnp.where(row == SMALL_DIAGONAL, diagonal_row(out_square), block)
    first = jnp.pad(wide, ((SMALL_WEIGHT, LANES - SMALL_WEIGHT - hidden), (0, 0)))
    block = jnp.where((row >= SMALL_WEIGHT) & (row < SMALL_WEIGHT + hidden) & (col < SMALL_WEIGHT), first, block)
    turned = pltpu.roll(wide[half:, :], LANES - SMALL_WEIGHT, axis=1)
    lane = lax.broadcasted_iota(jnp.int32, (half, LANES), 1)
    rest = jnp.where(lane >= SMALL_WEIGHT, wide[:half, :], turned)
    return jnp.where(row >= SMALL_REST, jnp.pad(rest, ((SMALL_REST, 0), (0, 0))), block)


def unpack_small(block, rows_one, hidden):
    half = hidden // 2
    turned = block.T
    in_one = first_of(block, turned)[:rows_one, :rows_one]
    out_one = second_of(block, turned, block[SMALL_DIAGONAL : SMALL_DIAGONAL + 1, :])[:hidden, :hidden]
    rest = block[SMALL_REST:, :]
    lane = lax.broadcasted_iota(jnp.int32, (hidden, LANES), 1)
    high = jnp.concatenate([rest, pltpu.roll(rest, SMALL_WEIGHT, axis=1)], axis=0)
    weight_one = jnp.where(lane < SMALL_WEIGHT, block[SMALL_WEIGHT : SMALL_WEIGHT + hidden, :], high)
    return in_one, weight_one[:, :rows_one], out_one


def joined_kernel(mine_ref, came_ref, small_ref, *refs):
    feat_refs, out_ref = refs[:-1], refs[-1]
    owners = out_ref.shape[0]
    large, small = mine_ref.shape[0] // owners, small_ref.shape[0] // owners
    feat_rows = feat_refs[0].shape[1]
    for owner in range(owners):
        rows = slice(owner * large, (owner + 1) * large)
        out_ref[owner, :large, :] = (mine_ref[rows, :].astype(F32) + came_ref[rows, :].astype(F32)).astype(BF16)
        out_ref[owner, large : large + small, :] = small_ref[owner * small : (owner + 1) * small, :]
        for change, feat_ref in enumerate(feat_refs):
            start = large + small + change * feat_rows
            out_ref[owner, start : start + feat_rows, :] = feat_ref[owner]


def total_kernel(came_ref, out_ref, feat_ref):
    owners, chunk = came_ref.shape[0], out_ref.shape[0]
    total = came_ref[0, :chunk, :].astype(F32)
    for owner in range(1, owners):
        total += came_ref[owner, :chunk, :].astype(F32)
    out_ref[...] = total.astype(BF16)
    for owner in range(owners):
        feat_ref[owner] = came_ref[owner, chunk:, :]


def pair_kernel(mine_ref, came_ref, out_ref):
    total = (mine_ref[...].astype(F32) + came_ref[...].astype(F32)).astype(BF16)
    for owner in range(out_ref.shape[0]):
        out_ref[owner] = total


def features_kernel(owned_rows, cubes, feat_ref, out_ref, scr):
    owners, owned = out_ref.shape[1], out_ref.shape[2]
    rows = feat_ref.shape[1] // cubes
    members = owners // cubes
    cube = lax.axis_index("space") // members
    for change in range(cubes):
        for member in range(members):
            start = pl.multiple_of(((cube ^ change) * members + member) * rows, 16)
            scr[pl.ds(start, rows), :] = feat_ref[member, change * rows : (change + 1) * rows, :].astype(F32)
    for i in range(owned_rows):
        block = scr[pl.ds(i, owners, stride=rows), :]
        for m in range(LANES // owned):
            out_ref[m * owned_rows + i] = block[:, m * owned : (m + 1) * owned].astype(BF16)


def gathered_half(source_ref, half_scr):
    owners = source_ref.shape[0]
    tall = half_scr.shape[0] // owners
    for owner in range(owners):
        half_scr[owner * tall : (owner + 1) * tall, :] = source_ref[owner, :tall, :]


def unit_square():
    row, col = square_iotas()
    return jnp.where(row == col, 1.0, 0.0).astype(BF16)


def first_half_copies(middle, factor, out_ref, sems):
    rows_two, split = out_ref.shape[0], middle * LANES
    spots = [(slice(0, split), slice(split, rows_two)), (slice(split, rows_two), slice(0, split))]
    return [pltpu.make_async_copy(factor.at[spot], out_ref.at[spot], sems.at[at]) for at, spot in enumerate(spots)]


def second_half_copies(middle, factor, out_ref, sems):
    rows_two, split = out_ref.shape[0], middle * LANES
    spots = [(slice(0, split), slice(0, split)), (slice(split, rows_two), slice(split, rows_two))]
    return [pltpu.make_async_copy(factor.at[spot], out_ref.at[spot], sems.at[at]) for at, spot in enumerate(spots)]


def wait_for(copies):
    for copy in copies:
        copy.wait()


def write_first_half(places, panels, middle, scale, half_scr, factor, out_ref, sems):
    copies = first_half_copies(middle, factor, out_ref, sems)
    rows_two = out_ref.shape[0]
    split = middle * LANES
    unit = unit_square()
    for j in range(middle, panels):
        wide = min(LANES, rows_two - j * LANES)
        start = places["block", 0, j]
        panel = half_scr[start : start + split, :]
        columns = slice(j * LANES, j * LANES + wide)
        factor[:split, columns] = (panel.astype(F32) * scale)[:, :wide]
        factor[columns, :split] = (dot_nt(unit, panel) * scale)[:wide, :]
    for copy in copies:
        copy.start()


def write_second_half(places, panels, middle, scale, half_scr, factor, out_ref, sems):
    copies = second_half_copies(middle, factor, out_ref, sems)
    rows_two = out_ref.shape[0]
    half = half_scr.shape[0]
    unit = unit_square()
    used = rows_two - (panels - 1) * LANES
    pairs = (panels + 1) // 2
    start = places["pair", pairs - 1] - half
    holder = half_scr[start : start + LANES, :].astype(F32)
    for j in range(panels):
        first = middle if j >= middle else 0
        if j == middle:
            copies[0].start()
        if j % 2 == 0:
            start = places["pair", j // 2] - half
            block = half_scr[start : start + LANES, :]
            turned = dot_nt(unit, block)
            block = block.astype(F32)
            wide = min(LANES, rows_two - j * LANES)
            rows = slice(j * LANES, j * LANES + wide)
            factor[rows, rows] = (first_of(block, turned) * scale)[:wide, :wide]
            if j + 1 < panels:
                rows = slice((j + 1) * LANES, (j + 2) * LANES)
                diagonal = holder[used + j // 2 : used + j // 2 + 1, :]
                factor[rows, rows] = second_of(block, turned, diagonal) * scale
        if j == first:
            continue
        wide = min(LANES, rows_two - j * LANES)
        start = places["block", first, j] - half
        panel = half_scr[start : start + (j - first) * LANES, :]
        columns, rows = slice(j * LANES, j * LANES + wide), slice(first * LANES, j * LANES)
        factor[rows, columns] = (panel.astype(F32) * scale)[:, :wide]
        factor[columns, rows] = (dot_nt(unit, panel) * scale)[:wide, :]
    copies[1].start()


def own_half_kernel(places, panels, middle, scale, mine_ref, out_ref, half_scr, factor, sems):
    gathered_half(mine_ref, half_scr)
    core = lax.axis_index("batch")
    rest = (places, panels, middle, scale, half_scr, factor, out_ref, sems)
    pl.when(core == 0)(functools.partial(write_first_half, *rest))
    pl.when(core == 1)(functools.partial(write_second_half, *rest))
    where = (middle, factor, out_ref, sems)
    pl.when(core == 0)(lambda: wait_for(first_half_copies(*where)))
    pl.when(core == 1)(lambda: wait_for(second_half_copies(*where)))


def unpack_kernel(
    places, panels, middle, scale_one, scale_two, begun_ref, mine_ref, came_ref,
    in_one_out, in_two_ref, out_one_out, out_two_out, weight_one_out, weight_two_out,
    packed, small, factor, in_one_ref, out_one_ref, out_two_ref, weight_one_ref, weight_two_ref, sems,
):
    core = lax.axis_index("batch")
    gathered_half(mine_ref, packed.at[core])
    gathered_half(came_ref, packed.at[1 - core])
    rest = (places, panels, middle, scale_two)
    pl.when(core == 1)(functools.partial(write_first_half, *rest, packed.at[0], factor, in_two_ref, sems))
    pl.when(core == 0)(functools.partial(write_second_half, *rest, packed.at[1], factor, in_two_ref, sems))
    out_chan, rows_two = weight_two_ref.shape
    hidden, rows_one = weight_one_ref.shape
    owners = mine_ref.shape[0]
    tall_large, tall_small = packed.shape[1] // owners, small.shape[0] // owners
    for owner in range(owners):
        rows = slice(tall_large, tall_large + tall_small)
        small[owner * tall_small : (owner + 1) * tall_small, :] = mine_ref[owner, rows, :].astype(F32) + came_ref[
            owner, rows, :
        ].astype(F32)
    half = packed.shape[1]

    def get(name, count):
        side, row = divmod(places[name], half)
        return packed[side, row : row + count, :].astype(F32)

    used = rows_two - (panels - 1) * LANES
    spare = LANES - used
    lane = lax.broadcasted_iota(jnp.int32, (1, LANES), 1)
    last = jnp.zeros((out_chan, LANES), F32)
    for i in range(-(-used // spare)):
        piece = pltpu.roll(get(("block", i, panels - 1), out_chan), LANES - (used - i * spare), axis=1)
        last = jnp.where((lane >= i * spare) & (lane < (i + 1) * spare), piece, last)
    for j in range(panels - 1):
        weight_two_ref[:, j * LANES : (j + 1) * LANES] = get(("weight_two", j), out_chan)
    weight_two_ref[:, (panels - 1) * LANES :] = last[:, :used]
    copies = [pltpu.make_async_copy(weight_two_ref, weight_two_out, sems.at[2])]
    copies[0].start()
    pairs = (panels + 1) // 2
    block = get(("pair", pairs - 1), LANES)
    diagonal = block[used + pairs - 1 : used + pairs, :]
    out_two_ref[...] = second_of(block, block.T, diagonal)[:out_chan, :out_chan]
    in_one, weight_one, out_one = unpack_small(small[...], rows_one, hidden)
    in_one_ref[...] = in_one * scale_one
    weight_one_ref[...] = weight_one
    out_one_ref[...] = out_one
    results = ((in_one_ref, in_one_out), (out_one_ref, out_one_out), (out_two_ref, out_two_out))
    for at, (here, there) in enumerate(results + ((weight_one_ref, weight_one_out),)):
        copies.append(pltpu.make_async_copy(here, there, sems.at[3 + at]))
        copies[-1].start()
    wait_for(copies)
    where = (middle, factor, in_two_ref, sems)
    pl.when(core == 1)(lambda: wait_for(first_half_copies(*where)))
    pl.when(core == 0)(lambda: wait_for(second_half_copies(*where)))


def cube_size(space):
    return 8 if space % 8 == 0 else space


def exchange(parts, size):
    space = lax.axis_size("space")
    groups = [list(range(base, base + size)) for base in range(0, space, size)]
    return lax.all_to_all(parts, "space", split_axis=0, concat_axis=0, axis_index_groups=groups)


def from_partner(block, stride):
    return lax.ppermute(block, "space", [(i, i ^ stride) for i in range(lax.axis_size("space"))])


def call(kernel, out_shape, scratch=(), micros=3, mib=24, **more):
    return pl.pallas_call(
        kernel,
        out_shape=out_shape,
        scratch_shapes=list(scratch),
        cost_estimate=pl.CostEstimate(flops=int(micros * 1.1e9), bytes_accessed=1 << 20, transcendentals=0),
        compiler_params=pltpu.CompilerParams(vmem_limit_bytes=mib * MIB),
        **more,
    )


def passed_along(block, axis, distance):
    devices = range(lax.axis_size(axis))
    route = [(i - distance, i) for i in devices if i - distance in devices]
    return lax.ppermute(block, axis, route)


def swapped(block):
    return lax.ppermute(block, "batch", [(0, 1), (1, 0)])


def like(shape, kind=BF16):
    return jax.ShapeDtypeStruct(shape, kind)


def split_scratch(count, plane):
    return [
        pltpu.VMEM((count * (plane + 8), plane), F32),
        pltpu.VMEM((count * 40, 4 * plane), BF16),
        pltpu.VMEM((8 * up_to(25 * count, 16), LANES), F32),
    ]


def local(volume, kernel_one, kernel_two, cotangent):
    channels, _, own, plane, _ = volume.shape
    rows_one, hidden = kernel_one.shape
    rows_two, out_chan = kernel_two.shape
    cells = cotangent.shape[3]
    side = math.isqrt(cells)
    space = lax.axis_size("space")
    devices_all = space * lax.axis_size("batch")
    total_one = devices_all * 8 * cells
    total_two = devices_all * cells
    rows_pad = up_to(rows_one, 16)
    halo = own - 1
    halo_width = up_to(25 * channels * halo, 16)
    own_width = up_to(25 * channels * own, 16)
    tall = 4 * hidden

    vol = volume.reshape(channels, own, plane, plane)
    halo_block = passed_along(vol[:, own - halo :], "space", 1)
    halo_rows = jnp.asarray(patch_rows(channels, 0, halo, (0, 1), rows_pad), BF16)
    own_rows = jnp.asarray(patch_rows(channels, halo, own, (1, 2), rows_pad), BF16)
    split = jnp.asarray(split_columns(plane, side), BF16)
    halo_wide, own_wide, back = call(
        prepare_kernel,
        (like((2 * tall, halo_width)), like((2 * tall, own_width)), like((2 * tall, 8 * out_chan))),
        [pltpu.VMEM((rows_two, LANES), F32)],
        micros=3,
    )(kernel_one.T, kernel_two.T, halo_rows, own_rows)
    part, act_high, slope_high, p1, in_one_part = call(
        own_kernel,
        (
            like((tall, cells), F32),
            like((tall, cells), F32),
            like((tall, cells), F32),
            like((8, rows_pad, cells)),
            like((rows_pad, rows_pad), F32),
        ),
        split_scratch(channels * own, plane) + [pltpu.VMEM((own_width, cells), BF16)],
        micros=6,
    )(vol, own_wide, split, own_rows)
    panels, middle, places, large_rows = large_places(rows_two, out_chan)
    feat_rows = out_chan * cells // space // LANES
    feat_tall = up_to(feat_rows, 16)
    cube = cube_size(space)
    cubes = space // cube
    grad_two, p2, slope_low, spread, *feats = call(
        functools.partial(forward_kernel, 1.0 / math.sqrt(total_two)),
        (
            like((out_chan, cells)),
            like((panels * LANES, cells)),
            like((tall, cells), F32),
            like((halo_width, cells)),
        )
        + (like((cube, feat_tall, LANES)),) * cubes,
        split_scratch(channels * halo, plane)
        + [pltpu.VMEM((rows_two * (cells // LANES), LANES), F32), pltpu.VMEM((space, feat_tall, LANES), BF16)],
        micros=5,
    )(halo_block, halo_wide, split, part, act_high, kernel_two.T, cotangent.reshape(out_chan, cells))
    feats = feats[:1] + [from_partner(feats[change], change * cube) for change in range(1, cubes)]
    above = passed_along(grad_two, "space", -1)
    feats, above = lax.optimization_barrier((feats, above))

    half = large_rows // 2
    small_rows = LANES
    chunk = (half + small_rows) // cube
    mine, other, done = call(
        functools.partial(sums_kernel, places, rows_two),
        (like((half, LANES)), like((half, LANES)), like((8, LANES), F32)),
        [pltpu.VMEM((2, panels * LANES, 2 * LANES), F32)],
        micros=0.1,
    )(p2, grad_two)
    came = swapped(other)
    in_one_low, low, high = call(
        low_kernel,
        (like((rows_pad, rows_pad), F32), like((hidden, rows_pad + hidden), F32), like((tall, cells), F32)),
        [pltpu.VMEM((4 * out_chan, cells), BF16)],
        micros=0.1,
    )(grad_two, back, slope_low, p1, spread, halo_rows[4:], in_one_part, done)
    small = call(
        high_kernel,
        like((small_rows, LANES)),
        [pltpu.VMEM((4 * out_chan, cells), BF16)],
        micros=12,
    )(above, back, high, slope_high, p1, in_one_low, low)
    joined = call(joined_kernel, like((cube, chunk + cubes * feat_tall, LANES)), micros=1)(mine, came, small, *feats)
    total, feat = call(
        total_kernel, (like((chunk, LANES)), like((cube, cubes * feat_tall, LANES))), micros=1
    )(exchange(joined, cube))
    stride = cube
    while 2 * stride < space:
        total = (total.astype(F32) + from_partner(total, stride).astype(F32)).astype(BF16)
        stride *= 2
    features = call(
        functools.partial(features_kernel, feat_rows, cubes),
        like((out_chan, space, cells // space)),
        [pltpu.VMEM((space * feat_tall, LANES), F32)],
        micros=1,
    )(feat)
    other = from_partner(total, stride) if stride < space else jnp.zeros_like(total)
    other, features = lax.optimization_barrier((other, features))
    copies = call(pair_kernel, like((cube, chunk, LANES)), micros=1)(total, other)
    mine = exchange(copies, cube)
    came = swapped(mine)
    anywhere = pl.BlockSpec(memory_space=pl.ANY)
    begun = call(
        functools.partial(own_half_kernel, places, panels, middle, 1.0 / total_two),
        like((rows_two, rows_two), F32),
        [
            pltpu.VMEM((half, LANES), BF16),
            pltpu.VMEM((rows_two, rows_two), F32),
            pltpu.SemaphoreType.DMA((2,)),
        ],
        micros=2,
        out_specs=anywhere,
    )(mine)
    kinds = [
        like(shape, F32)
        for shape in (
            (rows_one, rows_one),
            (rows_two, rows_two),
            (hidden, hidden),
            (out_chan, out_chan),
            (hidden, rows_one),
            (out_chan, rows_two),
        )
    ]
    in_one, in_two, out_one, out_two, weight_one, weight_two = call(
        functools.partial(unpack_kernel, places, panels, middle, 1.0 / total_one, 1.0 / total_two),
        tuple(kinds),
        [
            pltpu.VMEM((2, half, LANES), BF16),
            pltpu.VMEM((small_rows, LANES), F32),
            pltpu.VMEM((rows_two, rows_two), F32),
        ]
        + [pltpu.VMEM(kind.shape, F32) for at, kind in enumerate(kinds) if at != 1]
        + [pltpu.SemaphoreType.DMA((7,))],
        micros=2,
        in_specs=[anywhere, pl.BlockSpec(memory_space=pltpu.VMEM), pl.BlockSpec(memory_space=pltpu.VMEM)],
        out_specs=(anywhere,) * 6,
        input_output_aliases={0: 1},
    )(begun, mine, came)
    features = features.reshape(out_chan, 1, space, cells // space)
    return features, in_one, in_two, out_one, out_two, weight_one.T, weight_two.T


def solution(mesh):
    placed = (P(None, "batch", "space", None, None), P(), P(), P(None, "batch", "space", None))
    return jax.shard_map(
        local,
        mesh=mesh,
        in_specs=placed,
        out_specs=(P(None, "batch", None, "space"), P(), P(), P(), P(), P(), P()),
        check_vma=False,
    )
```

```python
import functools
import math

import jax
import jax.numpy as jnp
import numpy as np
from jax import lax
from jax.experimental import pallas as pl
from jax.experimental.pallas import tpu as pltpu
from jax.sharding import PartitionSpec as P

F32 = jnp.float32
BF16 = jnp.bfloat16
LANES = 128
TAPS = 27
MIB = 1024 * 1024


def up_to(count, unit):
    return -(-count // unit) * unit


def split_columns(plane, quarter):
    table = np.zeros((4, plane, 5, 4, quarter), np.float32)
    for group in range(4):
        for q in range(5):
            for cell in range(quarter):
                x = 4 * cell + q - 1
                if 0 <= x < plane:
                    table[group, x, q, group, cell] = 1.0
    return table.reshape(4 * plane, 5 * 4 * quarter)


def patch_rows(channels, first, planes, hidden_planes, rows):
    width = up_to(25 * channels * planes, 16)
    table = np.zeros((len(hidden_planes), 2, 2, rows, width), np.float32)
    for at, j in enumerate(hidden_planes):
        for a in range(3):
            plane = 2 * j + a - first
            if not 0 <= plane < planes:
                continue
            for py, px, c, b, e in np.ndindex(2, 2, channels, 3, 3):
                source = (((2 * px + e) * channels + c) * planes + plane) * 5 + 2 * py + b
                table[at, py, px, c * TAPS + a * 9 + b * 3 + e, source] = 1.0
    return table.reshape(len(hidden_planes) * 4, rows, width)


def dot(first, second):
    return jnp.dot(first, second, preferred_element_type=F32)


def dot_nt(first, second):
    return lax.dot_general(first, second, (((1,), (1,)), ((), ())), preferred_element_type=F32)


def gelu_parts(value):
    square = value * value
    tangent = jnp.tanh(0.7978845608028654 * (value + 0.044715 * value * square))
    half = 0.5 * (1.0 + tangent)
    return value * half, half, tangent, square


def gelu_and_slope(value):
    act, half, tangent, square = gelu_parts(value)
    slope = half + 0.5 * value * (1.0 - tangent * tangent) * (
        0.7978845608028654 * (1.0 + 3.0 * 0.044715 * square)
    )
    return act, slope


def prepare_kernel(k1t_ref, k2t_ref, halo_rows_ref, own_rows_ref, halo_wide_ref, own_wide_ref, back_ref, k2_rows):
    hidden, rows_one = k1t_ref.shape
    rows_pad = halo_rows_ref.shape[1]
    k1t = jnp.pad(k1t_ref[...].astype(F32), ((0, 0), (0, rows_pad - rows_one))).astype(BF16)
    for rows_ref, wide_ref in ((halo_rows_ref, halo_wide_ref), (own_rows_ref, own_wide_ref)):
        for block in range(rows_ref.shape[0]):
            wide_ref[block * hidden : (block + 1) * hidden, :] = dot(k1t, rows_ref[block]).astype(BF16)
    out_chan, rows_two = k2t_ref.shape
    for at in range(0, rows_two, LANES):
        tall = min(LANES, rows_two - at)
        block = k2t_ref[:, at : at + tall].astype(F32)
        if tall < LANES:
            block = jnp.pad(block, ((0, 0), (0, LANES - tall)))
        k2_rows[at : at + tall, :out_chan] = block.T[:tall, :]
    taps = [k2_rows[pl.ds(tap, hidden, stride=TAPS), :][:, :out_chan] for tap in range(TAPS)]
    nothing = jnp.zeros_like(taps[0])

    def tap_for(parity, shift):
        if parity == 0:
            return 1 if shift == 0 else None
        return 2 if shift == 0 else 0

    for j in (1, 2):
        for py in range(2):
            for px in range(2):
                blocks = []
                for above in range(2):
                    a = {(1, 0): 1, (2, 0): 2, (2, 1): 0}.get((j, above))
                    for sy in range(2):
                        for sx in range(2):
                            b, e = tap_for(py, sy), tap_for(px, sx)
                            there = a is not None and b is not None and e is not None
                            blocks.append(taps[a * 9 + b * 3 + e] if there else nothing)
                start = ((j - 1) * 4 + py * 2 + px) * hidden
                back_ref[start : start + hidden, :] = jnp.concatenate(blocks, axis=1).astype(BF16)


def split_cells(planes, split_ref, cells_ref, rows_scr, lhs_scr, cells_scr):
    plane = planes[0].shape[0]
    pitch = plane + 8
    for at, source in enumerate(planes):
        start = at * pitch
        rows_scr[start : start + 8, :] = jnp.zeros((8, plane), F32)
        rows_scr[start + 8 : start + pitch, :] = source[...].astype(F32)
    for pair in range(len(planes) // 2):
        pieces = []
        for member in range(2):
            start = (pair * 2 + member) * pitch + 8
            tiles = [rows_scr[pl.ds(start + t, 8, stride=16), :] for t in range(-1, 16)]
            for q in range(5):
                pieces.append(jnp.concatenate([tiles[4 * group + q] for group in range(4)], axis=1))
        lhs_scr[pair * 80 : (pair + 1) * 80, :] = jnp.concatenate(pieces, axis=0).astype(BF16)
    total_rows = len(planes) * 40
    chunk = 160
    for part in range(total_rows // chunk):
        product = dot(lhs_scr[part * chunk : (part + 1) * chunk, :], split_ref[...])
        for q in range(5):
            start = q * total_rows + part * chunk
            cells_scr[start : start + chunk, :] = product[:, q * LANES : (q + 1) * LANES]
    filled = 5 * total_rows
    width = cells_ref.shape[0]
    if filled < 8 * width:
        cells_scr[filled : 8 * width, :] = jnp.zeros((8 * width - filled, LANES), F32)
    for yh in range(8):
        cells_ref[:, yh * LANES : (yh + 1) * LANES] = cells_scr[pl.ds(yh, width, stride=8), :].astype(BF16)


def own_kernel(
    vol_ref, wide_ref, split_ref, rows_ref,
    part_ref, act_ref, slope_ref, p1_ref, in_one_ref, rows_scr, lhs_scr, cells_scr, cells_ref,
):
    channels, own = vol_ref.shape[0], vol_ref.shape[1]
    planes = [vol_ref.at[c, z] for c in range(channels) for z in range(own)]
    split_cells(planes, split_ref, cells_ref, rows_scr, lhs_scr, cells_scr)
    pre = dot(wide_ref[...], cells_ref[...])
    tall = part_ref.shape[0]
    part_ref[...] = pre[:tall, :]
    quarter = tall // 4
    for at in range(0, tall, quarter):
        act, slope = gelu_and_slope(pre[tall + at : tall + at + quarter, :])
        act_ref[at : at + quarter, :] = act
        slope_ref[at : at + quarter, :] = slope
    blocks, rows_pad, width = rows_ref.shape
    p1 = dot(rows_ref[...].reshape(blocks * rows_pad, width), cells_ref[...]).astype(BF16)
    total = jnp.zeros((rows_pad, rows_pad), F32)
    for block in range(blocks):
        piece = p1[block * rows_pad : (block + 1) * rows_pad, :]
        p1_ref[block] = piece
        if block >= blocks // 2:
            total += dot_nt(piece, piece)
    in_one_ref[...] = total


def forward_kernel(
    scale, halo_ref, wide_ref, split_ref, part_ref, act_ref, k2t_ref, cot_ref,
    grad_ref, p2_ref, slope_ref, cells_ref, *rest,
):
    feat_refs, (rows_scr, lhs_scr, cells_scr, p2_scr, feat_scr) = rest[:-5], rest[-5:]
    channels, halo = halo_ref.shape[0], halo_ref.shape[1]
    planes = [halo_ref.at[c, z] for c in range(channels) for z in range(halo)]
    split_cells(planes, split_ref, cells_ref, rows_scr, lhs_scr, cells_scr)
    cells = cells_ref.shape[1]
    lane = lax.broadcasted_iota(jnp.int32, (1, cells), 1)
    side = math.isqrt(cells)
    not_left = (lane % side) != 0
    not_top = lane >= side
    tall = part_ref.shape[0]
    hidden = tall // 4
    rows_two = hidden * TAPS
    for j in (2, 1, 0):
        if j < 2:
            pre = dot(wide_ref[j * tall : (j + 1) * tall, :], cells_ref[...])
            if j == 1:
                pre = pre + part_ref[...]
        for parity in range(4):
            rows = slice(parity * hidden, (parity + 1) * hidden)
            if j == 2:
                act = act_ref[rows, :]
            elif j == 1:
                act, slope = gelu_and_slope(pre[rows, :])
                slope_ref[rows, :] = slope
            else:
                act = gelu_parts(pre[rows, :])[0]
            py, px = parity // 2, parity % 2
            for b in ((1,) if py == 0 else (2, 0)):
                for e in ((1,) if px == 0 else (2, 0)):
                    moved = act
                    distance = (side if b == 0 else 0) + (1 if e == 0 else 0)
                    if distance:
                        moved = pltpu.roll(act, distance, axis=1)
                    if b == 0:
                        moved = jnp.where(not_top, moved, 0.0)
                    if e == 0:
                        moved = jnp.where(not_left, moved, 0.0)
                    for k in range(cells // LANES):
                        start = k * rows_two + j * 9 + b * 3 + e
                        p2_scr[pl.ds(start, hidden, stride=TAPS), :] = moved[:, k * LANES : (k + 1) * LANES]
    for k in range(cells // LANES):
        p2_ref[:rows_two, k * LANES : (k + 1) * LANES] = p2_scr[k * rows_two : (k + 1) * rows_two, :].astype(BF16)
    p2_ref[rows_two:, :] = jnp.zeros((p2_ref.shape[0] - rows_two, cells), BF16)
    act, slope = gelu_and_slope(dot(k2t_ref[...], p2_ref[:rows_two, :]))
    grad_ref[...] = (cot_ref[...].astype(F32) * scale * slope).astype(BF16)
    owned = cells // feat_scr.shape[0]
    rows = act.shape[0] * owned // LANES
    count = LANES // owned
    place = lax.broadcasted_iota(jnp.int32, (1, LANES), 1) // owned
    for k in range(cells // LANES):
        tile = act[:, k * LANES : (k + 1) * LANES]
        for u in range(count):
            total = jnp.zeros((rows, LANES), F32)
            for m in range(count):
                block = tile[m * rows : (m + 1) * rows, :]
                if m != u:
                    block = pltpu.roll(block, ((m - u) * owned) % LANES, axis=1)
                total = jnp.where(place == m, block, total)
            if rows < feat_scr.shape[1]:
                total = jnp.pad(total, ((0, feat_scr.shape[1] - rows), (0, 0)))
            feat_scr[k * count + u] = total.astype(BF16)
    owners = feat_refs[0].shape[0]
    cube = lax.axis_index("space") // owners
    for change, feat_ref in enumerate(feat_refs):
        feat_ref[...] = feat_scr[pl.ds((cube ^ change) * owners, owners)]


def large_places(rows_two, out_chan):
    panels = -(-rows_two // LANES)
    pairs = (panels + 1) // 2
    middle = pairs // 2 * 2
    names = [("block", i, j) for j in range(middle, panels) for i in range(middle)]
    names += [("block", i, j) for j in range(middle) for i in range(j)]
    names += [("block", i, j) for j in range(middle, panels) for i in range(middle, j)]
    names += [("pair", p) for p in range(pairs)]
    cross = middle * (panels - middle)
    weights = [("weight_two", j) for j in range(panels - 1)]
    half = (len(names) * LANES + len(weights) * out_chan) // 2
    early = (half - cross * LANES) // out_chan
    order = [(name, LANES) for name in names[:cross]] + [(name, out_chan) for name in weights[:early]]
    order += [(name, LANES) for name in names[cross:]] + [(name, out_chan) for name in weights[early:]]
    places, at = {}, 0
    for name, rows in order:
        places[name] = at
        at += rows
    return panels, middle, places, at


def square_iotas():
    return (
        lax.broadcasted_iota(jnp.int32, (LANES, LANES), 0),
        lax.broadcasted_iota(jnp.int32, (LANES, LANES), 1),
    )


def diagonal_row(block):
    row, col = square_iotas()
    return jnp.sum(jnp.where(row == col, block, 0.0), axis=0, keepdims=True)


def two_in_one(upper, lower):
    row, col = square_iotas()
    return jnp.where(row <= col, upper, lower)


def first_of(block, turned):
    row, col = square_iotas()
    return jnp.where(row <= col, block, turned)


def second_of(block, turned, diagonal):
    row, col = square_iotas()
    return jnp.where(row > col, block, jnp.where(row == col, diagonal, turned))


def square(block):
    return jnp.pad(block, ((0, LANES - block.shape[0]), (0, LANES - block.shape[1])))


def padded_lanes(block):
    return jnp.pad(block, ((0, 0), (0, LANES - block.shape[1])))


def put(halves, at, block):
    half = halves[0].shape[0]
    done = 0
    while done < block.shape[0]:
        side, row = divmod(at + done, half)
        count = min(block.shape[0] - done, half - row)
        halves[side][row : row + count, :] = block[done : done + count, :].astype(BF16)
        done += count


def sums_kernel(
    places, rows_two, p2_ref, grad_ref, mine_ref, other_ref, done_ref, product_scr,
):
    done_ref[...] = jnp.zeros_like(done_ref)
    core = lax.axis_index("batch")
    rest = (places, rows_two, p2_ref, grad_ref, product_scr)
    pl.when(core == 0)(lambda: write_sums(*rest, (mine_ref, other_ref)))
    pl.when(core == 1)(lambda: write_sums(*rest, (other_ref, mine_ref)))


def write_sums(places, rows_two, p2_ref, grad_ref, product_scr, packed):
    panels = p2_ref.shape[0] // LANES
    used = rows_two - (panels - 1) * LANES
    lane = lax.broadcasted_iota(jnp.int32, (1, LANES), 1)
    weight_two = dot_nt(grad_ref[...], p2_ref[...])
    out_chan = weight_two.shape[0]
    last = weight_two[:, (panels - 1) * LANES :]
    spare = LANES - used
    diagonals = []
    for j in range(0, panels, 2):
        wide = min(2, panels - j)
        tall = (j + wide) * LANES
        product = product_scr.at[(j // 2) % 2]
        product[:tall, : wide * LANES] = dot_nt(p2_ref[:tall, :], p2_ref[j * LANES : tall, :])
        for k in range(wide):
            columns = slice(k * LANES, (k + 1) * LANES)
            for i in range(j + k):
                block = product[i * LANES : (i + 1) * LANES, columns]
                if j + k == panels - 1 and i * spare < used:
                    piece = pltpu.roll(last, used - i * spare, axis=1)
                    top = jnp.where(lane >= used, piece, block[:out_chan, :])
                    block = jnp.concatenate([top, block[out_chan:, :]], axis=0)
                put(packed, places["block", i, j + k], block)
        first = product[j * LANES : (j + 1) * LANES, :LANES]
        if wide == 2:
            second = product[(j + 1) * LANES : tall, LANES:]
        else:
            second = square(dot_nt(grad_ref[...], grad_ref[...]))
        diagonals.append(diagonal_row(second))
        block = two_in_one(first, second)
        if wide == 1:
            row, _ = square_iotas()
            for at, diagonal in enumerate(diagonals):
                block = jnp.where(row == used + at, diagonal, block)
        put(packed, places["pair", j // 2], block)
    for j in range(panels - 1):
        put(packed, places["weight_two", j], weight_two[:, j * LANES : (j + 1) * LANES])


def shifted_up(source, scr):
    out_chan, cells = source.shape
    side = math.isqrt(cells)
    lane = lax.broadcasted_iota(jnp.int32, (1, cells), 1)
    value = source[...].astype(F32)
    for sy in range(2):
        for sx in range(2):
            moved = value
            distance = sy * side + sx
            if distance:
                moved = pltpu.roll(value, cells - distance, axis=1)
            if sy:
                moved = jnp.where(lane < cells - side, moved, 0.0)
            if sx:
                moved = jnp.where((lane % side) != side - 1, moved, 0.0)
            at = (2 * sy + sx) * out_chan
            scr[at : at + out_chan, :] = moved.astype(BF16)


def low_kernel(
    grad_ref, back_ref, slope_ref, p1_ref, cells_ref, rows_ref, in_one_ref, done_ref,
    in_one_out, low_out, high_ref, scr,
):
    _, rows_pad, _ = p1_ref.shape
    part, _, width = rows_ref.shape
    extra = dot(rows_ref[...].reshape(part * rows_pad, width), cells_ref[...])
    p1 = [
        (extra[at * rows_pad : (at + 1) * rows_pad, :] + p1_ref[at].astype(F32)).astype(BF16) for at in range(part)
    ]
    shifted_up(grad_ref, scr)
    tall = high_ref.shape[0]
    hidden = tall // part
    grad_hidden = dot(back_ref[:, : scr.shape[0]], scr[...])
    high_ref[...] = grad_hidden[tall:, :]
    in_one = in_one_ref[...]
    total = jnp.zeros((hidden, rows_pad + hidden), F32)
    for block in range(part):
        rows = slice(block * hidden, (block + 1) * hidden)
        piece = (grad_hidden[rows, :] * slope_ref[rows, :]).astype(BF16)
        in_one += dot_nt(p1[block], p1[block])
        total += dot_nt(piece, jnp.concatenate([p1[block], piece], axis=0))
    in_one_out[...] = in_one
    low_out[...] = total


def high_kernel(
    above_ref, back_ref, high_ref, slope_ref, p1_ref, in_one_ref, low_ref, out_ref, scr,
):
    shifted_up(above_ref, scr)
    blocks, rows_pad, _ = p1_ref.shape
    part = blocks // 2
    tall, reach = high_ref.shape[0], scr.shape[0]
    hidden = tall // part
    grad_hidden = high_ref[...] + dot(back_ref[tall:, reach:], scr[...])
    total = low_ref[...]
    for block in range(part):
        rows = slice(block * hidden, (block + 1) * hidden)
        piece = (grad_hidden[rows, :] * slope_ref[rows, :]).astype(BF16)
        total += dot_nt(piece, jnp.concatenate([p1_ref[part + block], piece], axis=0))
    weight_one, out_one = total[:, :rows_pad], total[:, rows_pad:]
    out_ref[...] = pack_small(in_one_ref[...], weight_one, out_one).astype(BF16)


SMALL_DIAGONAL = 108
SMALL_WEIGHT = 64
SMALL_REST = 112


def pack_small(in_one, weight_one, out_one):
    row, col = square_iotas()
    hidden = weight_one.shape[0]
    half = hidden // 2
    wide = padded_lanes(weight_one)
    out_square = square(out_one)
    block = jnp.where(row <= col, square(in_one), jnp.where(row < hidden, out_square, 0.0))
    block = jnp.where(row == SMALL_DIAGONAL, diagonal_row(out_square), block)
    first = jnp.pad(wide, ((SMALL_WEIGHT, LANES - SMALL_WEIGHT - hidden), (0, 0)))
    block = jnp.where((row >= SMALL_WEIGHT) & (row < SMALL_WEIGHT + hidden) & (col < SMALL_WEIGHT), first, block)
    turned = pltpu.roll(wide[half:, :], LANES - SMALL_WEIGHT, axis=1)
    lane = lax.broadcasted_iota(jnp.int32, (half, LANES), 1)
    rest = jnp.where(lane >= SMALL_WEIGHT, wide[:half, :], turned)
    return jnp.where(row >= SMALL_REST, jnp.pad(rest, ((SMALL_REST, 0), (0, 0))), block)


def unpack_small(block, rows_one, hidden):
    half = hidden // 2
    turned = block.T
    in_one = first_of(block, turned)[:rows_one, :rows_one]
    out_one = second_of(block, turned, block[SMALL_DIAGONAL : SMALL_DIAGONAL + 1, :])[:hidden, :hidden]
    rest = block[SMALL_REST:, :]
    lane = lax.broadcasted_iota(jnp.int32, (hidden, LANES), 1)
    high = jnp.concatenate([rest, pltpu.roll(rest, SMALL_WEIGHT, axis=1)], axis=0)
    weight_one = jnp.where(lane < SMALL_WEIGHT, block[SMALL_WEIGHT : SMALL_WEIGHT + hidden, :], high)
    return in_one, weight_one[:, :rows_one], out_one


def joined_kernel(mine_ref, came_ref, small_ref, *refs):
    feat_refs, out_ref = refs[:-1], refs[-1]
    owners = out_ref.shape[0]
    large, small = mine_ref.shape[0] // owners, small_ref.shape[0] // owners
    feat_rows = feat_refs[0].shape[1]
    for owner in range(owners):
        rows = slice(owner * large, (owner + 1) * large)
        out_ref[owner, :large, :] = (mine_ref[rows, :].astype(F32) + came_ref[rows, :].astype(F32)).astype(BF16)
        out_ref[owner, large : large + small, :] = small_ref[owner * small : (owner + 1) * small, :]
        for change, feat_ref in enumerate(feat_refs):
            start = large + small + change * feat_rows
            out_ref[owner, start : start + feat_rows, :] = feat_ref[walk(owners)[owner]]


def total_kernel(came_ref, out_ref, feat_ref):
    owners, chunk = came_ref.shape[0], out_ref.shape[0]
    total = came_ref[0, :chunk, :].astype(F32)
    for owner in range(1, owners):
        total += came_ref[owner, :chunk, :].astype(F32)
    out_ref[...] = total.astype(BF16)
    for owner in range(owners):
        feat_ref[owner] = came_ref[owner, chunk:, :]


def pair_kernel(mine_ref, came_ref, out_ref):
    total = (mine_ref[...].astype(F32) + came_ref[...].astype(F32)).astype(BF16)
    for owner in range(out_ref.shape[0]):
        out_ref[owner] = total


def features_kernel(owned_rows, cubes, feat_ref, out_ref, scr):
    owners, owned = out_ref.shape[1], out_ref.shape[2]
    rows = feat_ref.shape[1] // cubes
    members = owners // cubes
    cube = lax.axis_index("space") // members
    for change in range(cubes):
        for member in range(members):
            start = pl.multiple_of(((cube ^ change) * members + walk(members)[member]) * rows, 16)
            scr[pl.ds(start, rows), :] = feat_ref[member, change * rows : (change + 1) * rows, :].astype(F32)
    for i in range(owned_rows):
        block = scr[pl.ds(i, owners, stride=rows), :]
        for m in range(LANES // owned):
            out_ref[m * owned_rows + i] = block[:, m * owned : (m + 1) * owned].astype(BF16)


def gathered_half(source_ref, half_scr):
    owners = source_ref.shape[0]
    tall = half_scr.shape[0] // owners
    for owner in range(owners):
        half_scr[owner * tall : (owner + 1) * tall, :] = source_ref[owner, :tall, :]


def unit_square():
    row, col = square_iotas()
    return jnp.where(row == col, 1.0, 0.0).astype(BF16)


def first_half_copies(middle, factor, out_ref, sems):
    rows_two, split = out_ref.shape[0], middle * LANES
    spots = [(slice(0, split), slice(split, rows_two)), (slice(split, rows_two), slice(0, split))]
    return [pltpu.make_async_copy(factor.at[spot], out_ref.at[spot], sems.at[at]) for at, spot in enumerate(spots)]


def second_half_copies(middle, factor, out_ref, sems):
    rows_two, split = out_ref.shape[0], middle * LANES
    spots = [(slice(0, split), slice(0, split)), (slice(split, rows_two), slice(split, rows_two))]
    return [pltpu.make_async_copy(factor.at[spot], out_ref.at[spot], sems.at[at]) for at, spot in enumerate(spots)]


def wait_for(copies):
    for copy in copies:
        copy.wait()


def write_first_half(places, panels, middle, scale, half_scr, factor, out_ref, sems):
    copies = first_half_copies(middle, factor, out_ref, sems)
    rows_two = out_ref.shape[0]
    split = middle * LANES
    unit = unit_square()
    for j in range(middle, panels):
        wide = min(LANES, rows_two - j * LANES)
        start = places["block", 0, j]
        panel = half_scr[start : start + split, :]
        columns = slice(j * LANES, j * LANES + wide)
        factor[:split, columns] = (panel.astype(F32) * scale)[:, :wide]
        factor[columns, :split] = (dot_nt(unit, panel) * scale)[:wide, :]
    for copy in copies:
        copy.start()


def write_second_half(places, panels, middle, scale, half_scr, factor, out_ref, sems):
    copies = second_half_copies(middle, factor, out_ref, sems)
    rows_two = out_ref.shape[0]
    half = half_scr.shape[0]
    unit = unit_square()
    used = rows_two - (panels - 1) * LANES
    pairs = (panels + 1) // 2
    start = places["pair", pairs - 1] - half
    holder = half_scr[start : start + LANES, :].astype(F32)
    for j in range(panels):
        first = middle if j >= middle else 0
        if j == middle:
            copies[0].start()
        if j % 2 == 0:
            start = places["pair", j // 2] - half
            block = half_scr[start : start + LANES, :]
            turned = dot_nt(unit, block)
            block = block.astype(F32)
            wide = min(LANES, rows_two - j * LANES)
            rows = slice(j * LANES, j * LANES + wide)
            factor[rows, rows] = (first_of(block, turned) * scale)[:wide, :wide]
            if j + 1 < panels:
                rows = slice((j + 1) * LANES, (j + 2) * LANES)
                diagonal = holder[used + j // 2 : used + j // 2 + 1, :]
                factor[rows, rows] = second_of(block, turned, diagonal) * scale
        if j == first:
            continue
        wide = min(LANES, rows_two - j * LANES)
        start = places["block", first, j] - half
        panel = half_scr[start : start + (j - first) * LANES, :]
        columns, rows = slice(j * LANES, j * LANES + wide), slice(first * LANES, j * LANES)
        factor[rows, columns] = (panel.astype(F32) * scale)[:, :wide]
        factor[columns, rows] = (dot_nt(unit, panel) * scale)[:wide, :]
    copies[1].start()


def own_half_kernel(places, panels, middle, scale, mine_ref, out_ref, half_scr, factor, sems):
    gathered_half(mine_ref, half_scr)
    core = lax.axis_index("batch")
    rest = (places, panels, middle, scale, half_scr, factor, out_ref, sems)
    pl.when(core == 0)(functools.partial(write_first_half, *rest))
    pl.when(core == 1)(functools.partial(write_second_half, *rest))
    where = (middle, factor, out_ref, sems)
    pl.when(core == 0)(lambda: wait_for(first_half_copies(*where)))
    pl.when(core == 1)(lambda: wait_for(second_half_copies(*where)))


def unpack_kernel(
    places, panels, middle, scale_one, scale_two, begun_ref, mine_ref, came_ref,
    in_one_out, in_two_ref, out_one_out, out_two_out, weight_one_out, weight_two_out,
    packed, small, factor, in_one_ref, out_one_ref, out_two_ref, weight_one_ref, weight_two_ref, sems,
):
    core = lax.axis_index("batch")
    gathered_half(mine_ref, packed.at[core])
    gathered_half(came_ref, packed.at[1 - core])
    rest = (places, panels, middle, scale_two)
    pl.when(core == 1)(functools.partial(write_first_half, *rest, packed.at[0], factor, in_two_ref, sems))
    pl.when(core == 0)(functools.partial(write_second_half, *rest, packed.at[1], factor, in_two_ref, sems))
    out_chan, rows_two = weight_two_ref.shape
    hidden, rows_one = weight_one_ref.shape
    owners = mine_ref.shape[0]
    tall_large, tall_small = packed.shape[1] // owners, small.shape[0] // owners
    for owner in range(owners):
        rows = slice(tall_large, tall_large + tall_small)
        small[owner * tall_small : (owner + 1) * tall_small, :] = mine_ref[owner, rows, :].astype(F32) + came_ref[
            owner, rows, :
        ].astype(F32)
    half = packed.shape[1]

    def get(name, count):
        side, row = divmod(places[name], half)
        return packed[side, row : row + count, :].astype(F32)

    used = rows_two - (panels - 1) * LANES
    spare = LANES - used
    lane = lax.broadcasted_iota(jnp.int32, (1, LANES), 1)
    last = jnp.zeros((out_chan, LANES), F32)
    for i in range(-(-used // spare)):
        piece = pltpu.roll(get(("block", i, panels - 1), out_chan), LANES - (used - i * spare), axis=1)
        last = jnp.where((lane >= i * spare) & (lane < (i + 1) * spare), piece, last)
    for j in range(panels - 1):
        weight_two_ref[:, j * LANES : (j + 1) * LANES] = get(("weight_two", j), out_chan)
    weight_two_ref[:, (panels - 1) * LANES :] = last[:, :used]
    copies = [pltpu.make_async_copy(weight_two_ref, weight_two_out, sems.at[2])]
    copies[0].start()
    pairs = (panels + 1) // 2
    block = get(("pair", pairs - 1), LANES)
    diagonal = block[used + pairs - 1 : used + pairs, :]
    out_two_ref[...] = second_of(block, block.T, diagonal)[:out_chan, :out_chan]
    in_one, weight_one, out_one = unpack_small(small[...], rows_one, hidden)
    in_one_ref[...] = in_one * scale_one
    weight_one_ref[...] = weight_one
    out_one_ref[...] = out_one
    results = ((in_one_ref, in_one_out), (out_one_ref, out_one_out), (out_two_ref, out_two_out))
    for at, (here, there) in enumerate(results + ((weight_one_ref, weight_one_out),)):
        copies.append(pltpu.make_async_copy(here, there, sems.at[3 + at]))
        copies[-1].start()
    wait_for(copies)
    where = (middle, factor, in_two_ref, sems)
    pl.when(core == 1)(lambda: wait_for(first_half_copies(*where)))
    pl.when(core == 0)(lambda: wait_for(second_half_copies(*where)))


def cube_size(space):
    return 8 if space % 8 == 0 else space


def walk(size):
    return [at ^ (at >> 1) for at in range(size)]


def exchange(parts, size):
    space = lax.axis_size("space")
    groups = [[base + at for at in walk(size)] for base in range(0, space, size)]
    return lax.all_to_all(parts, "space", split_axis=0, concat_axis=0, axis_index_groups=groups)


def from_partner(block, stride):
    return lax.ppermute(block, "space", [(i, i ^ stride) for i in range(lax.axis_size("space"))])


def call(kernel, out_shape, scratch=(), micros=3, mib=24, **more):
    return pl.pallas_call(
        kernel,
        out_shape=out_shape,
        scratch_shapes=list(scratch),
        cost_estimate=pl.CostEstimate(flops=int(micros * 1.1e9), bytes_accessed=1 << 20, transcendentals=0),
        compiler_params=pltpu.CompilerParams(vmem_limit_bytes=mib * MIB),
        **more,
    )


def passed_along(block, axis, distance):
    devices = range(lax.axis_size(axis))
    route = [(i - distance, i) for i in devices if i - distance in devices]
    return lax.ppermute(block, axis, route)


def swapped(block):
    return lax.ppermute(block, "batch", [(0, 1), (1, 0)])


def like(shape, kind=BF16):
    return jax.ShapeDtypeStruct(shape, kind)


def split_scratch(count, plane):
    return [
        pltpu.VMEM((count * (plane + 8) + 16, plane), F32),
        pltpu.VMEM((count * 40, 4 * plane), BF16),
        pltpu.VMEM((8 * up_to(25 * count, 16) + 8, LANES), F32),
    ]


def local(volume, kernel_one, kernel_two, cotangent):
    channels, _, own, plane, _ = volume.shape
    rows_one, hidden = kernel_one.shape
    rows_two, out_chan = kernel_two.shape
    cells = cotangent.shape[3]
    side = math.isqrt(cells)
    space = lax.axis_size("space")
    devices_all = space * lax.axis_size("batch")
    total_one = devices_all * 8 * cells
    total_two = devices_all * cells
    rows_pad = up_to(rows_one, 16)
    halo = own - 1
    halo_width = up_to(25 * channels * halo, 16)
    own_width = up_to(25 * channels * own, 16)
    tall = 4 * hidden

    vol = volume.reshape(channels, own, plane, plane)
    halo_block = passed_along(vol[:, own - halo :], "space", 1)
    halo_rows = jnp.asarray(patch_rows(channels, 0, halo, (0, 1), rows_pad), BF16)
    own_rows = jnp.asarray(patch_rows(channels, halo, own, (1, 2), rows_pad), BF16)
    split = jnp.asarray(split_columns(plane, side), BF16)
    halo_wide, own_wide, back = call(
        prepare_kernel,
        (like((2 * tall, halo_width)), like((2 * tall, own_width)), like((2 * tall, 8 * out_chan))),
        [pltpu.VMEM((rows_two + 32, LANES), F32)],
        micros=3,
    )(kernel_one.T, kernel_two.T, halo_rows, own_rows)
    part, act_high, slope_high, p1, in_one_part = call(
        own_kernel,
        (
            like((tall, cells), F32),
            like((tall, cells), F32),
            like((tall, cells), F32),
            like((8, rows_pad, cells)),
            like((rows_pad, rows_pad), F32),
        ),
        split_scratch(channels * own, plane) + [pltpu.VMEM((own_width, cells), BF16)],
        micros=6,
    )(vol, own_wide, split, own_rows)
    panels, middle, places, large_rows = large_places(rows_two, out_chan)
    feat_rows = out_chan * cells // space // LANES
    feat_tall = up_to(feat_rows, 16)
    cube = cube_size(space)
    cubes = space // cube
    grad_two, p2, slope_low, spread, *feats = call(
        functools.partial(forward_kernel, 1.0 / math.sqrt(total_two)),
        (
            like((out_chan, cells)),
            like((panels * LANES, cells)),
            like((tall, cells), F32),
            like((halo_width, cells)),
        )
        + (like((cube, feat_tall, LANES)),) * cubes,
        split_scratch(channels * halo, plane)
        + [pltpu.VMEM((rows_two * (cells // LANES) + 32, LANES), F32), pltpu.VMEM((space, feat_tall, LANES), BF16)],
        micros=5,
    )(halo_block, halo_wide, split, part, act_high, kernel_two.T, cotangent.reshape(out_chan, cells))
    feats = feats[:1] + [from_partner(feats[change], change * cube) for change in range(1, cubes)]
    above = passed_along(grad_two, "space", -1)
    feats, above = lax.optimization_barrier((feats, above))

    half = large_rows // 2
    small_rows = LANES
    chunk = (half + small_rows) // cube
    mine, other, done = call(
        functools.partial(sums_kernel, places, rows_two),
        (like((half, LANES)), like((half, LANES)), like((8, LANES), F32)),
        [pltpu.VMEM((2, panels * LANES, 2 * LANES), F32)],
        micros=0.1,
    )(p2, grad_two)
    came = swapped(other)
    in_one_low, low, high = call(
        low_kernel,
        (like((rows_pad, rows_pad), F32), like((hidden, rows_pad + hidden), F32), like((tall, cells), F32)),
        [pltpu.VMEM((4 * out_chan, cells), BF16)],
        micros=0.1,
    )(grad_two, back, slope_low, p1, spread, halo_rows[4:], in_one_part, done)
    small = call(
        high_kernel,
        like((small_rows, LANES)),
        [pltpu.VMEM((4 * out_chan, cells), BF16)],
        micros=12,
    )(above, back, high, slope_high, p1, in_one_low, low)
    joined = call(joined_kernel, like((cube, chunk + cubes * feat_tall, LANES)), micros=1)(mine, came, small, *feats)
    total, feat = call(
        total_kernel, (like((chunk, LANES)), like((cube, cubes * feat_tall, LANES))), micros=1
    )(exchange(joined, cube))
    stride = cube
    while 2 * stride < space:
        total = (total.astype(F32) + from_partner(total, stride).astype(F32)).astype(BF16)
        stride *= 2
    features = call(
        functools.partial(features_kernel, feat_rows, cubes),
        like((out_chan, space, cells // space)),
        [pltpu.VMEM(((space + 1) * feat_tall, LANES), F32)],
        micros=1,
    )(feat)
    other = from_partner(total, stride) if stride < space else jnp.zeros_like(total)
    other, features = lax.optimization_barrier((other, features))
    copies = call(pair_kernel, like((cube, chunk, LANES)), micros=1)(total, other)
    mine = exchange(copies, cube)
    came = swapped(mine)
    anywhere = pl.BlockSpec(memory_space=pl.ANY)
    begun = call(
        functools.partial(own_half_kernel, places, panels, middle, 1.0 / total_two),
        like((rows_two, rows_two), F32),
        [
            pltpu.VMEM((half, LANES), BF16),
            pltpu.VMEM((rows_two, rows_two), F32),
            pltpu.SemaphoreType.DMA((2,)),
        ],
        micros=2,
        out_specs=anywhere,
    )(mine)
    kinds = [
        like(shape, F32)
        for shape in (
            (rows_one, rows_one),
            (rows_two, rows_two),
            (hidden, hidden),
            (out_chan, out_chan),
            (hidden, rows_one),
            (out_chan, rows_two),
        )
    ]
    in_one, in_two, out_one, out_two, weight_one, weight_two = call(
        functools.partial(unpack_kernel, places, panels, middle, 1.0 / total_one, 1.0 / total_two),
        tuple(kinds),
        [
            pltpu.VMEM((2, half, LANES), BF16),
            pltpu.VMEM((small_rows, LANES), F32),
            pltpu.VMEM((rows_two, rows_two), F32),
        ]
        + [pltpu.VMEM(kind.shape, F32) for at, kind in enumerate(kinds) if at != 1]
        + [pltpu.SemaphoreType.DMA((7,))],
        micros=2,
        in_specs=[anywhere, pl.BlockSpec(memory_space=pltpu.VMEM), pl.BlockSpec(memory_space=pltpu.VMEM)],
        out_specs=(anywhere,) * 6,
        input_output_aliases={0: 1},
    )(begun, mine, came)
    features = features.reshape(out_chan, 1, space, cells // space)
    return features, in_one, in_two, out_one, out_two, weight_one.T, weight_two.T


def solution(mesh):
    placed = (P(None, "batch", "space", None, None), P(), P(), P(None, "batch", "space", None))
    return jax.shard_map(
        local,
        mesh=mesh,
        in_specs=placed,
        out_specs=(P(None, "batch", None, "space"), P(), P(), P(), P(), P(), P()),
        check_vma=False,
    )
```

```python
import functools
import math

import jax
import jax.numpy as jnp
import numpy as np
from jax import lax
from jax.experimental import pallas as pl
from jax.experimental.pallas import tpu as pltpu
from jax.sharding import PartitionSpec as P

F32 = jnp.float32
BF16 = jnp.bfloat16
LANES = 128
TAPS = 27
MIB = 1024 * 1024


def up_to(count, unit):
    return -(-count // unit) * unit


def split_columns(plane, quarter):
    table = np.zeros((4, plane, 5, 4, quarter), np.float32)
    for group in range(4):
        for q in range(5):
            for cell in range(quarter):
                x = 4 * cell + q - 1
                if 0 <= x < plane:
                    table[group, x, q, group, cell] = 1.0
    return table.reshape(4 * plane, 5 * 4 * quarter)


def patch_rows(channels, first, planes, hidden_planes, rows):
    width = up_to(25 * channels * planes, 16)
    table = np.zeros((len(hidden_planes), 2, 2, rows, width), np.float32)
    for at, j in enumerate(hidden_planes):
        for a in range(3):
            plane = 2 * j + a - first
            if not 0 <= plane < planes:
                continue
            for py, px, c, b, e in np.ndindex(2, 2, channels, 3, 3):
                source = (((2 * px + e) * channels + c) * planes + plane) * 5 + 2 * py + b
                table[at, py, px, c * TAPS + a * 9 + b * 3 + e, source] = 1.0
    return table.reshape(len(hidden_planes) * 4, rows, width)


def dot(first, second):
    return jnp.dot(first, second, preferred_element_type=F32)


def dot_nt(first, second):
    return lax.dot_general(first, second, (((1,), (1,)), ((), ())), preferred_element_type=F32)


def gelu_parts(value):
    square = value * value
    tangent = jnp.tanh(0.7978845608028654 * (value + 0.044715 * value * square))
    half = 0.5 * (1.0 + tangent)
    return value * half, half, tangent, square


def gelu_and_slope(value):
    act, half, tangent, square = gelu_parts(value)
    slope = half + 0.5 * value * (1.0 - tangent * tangent) * (
        0.7978845608028654 * (1.0 + 3.0 * 0.044715 * square)
    )
    return act, slope


def prepare_kernel(k1t_ref, k2t_ref, halo_rows_ref, own_rows_ref, halo_wide_ref, own_wide_ref, back_ref, k2_rows):
    hidden, rows_one = k1t_ref.shape
    rows_pad = halo_rows_ref.shape[1]
    k1t = jnp.pad(k1t_ref[...].astype(F32), ((0, 0), (0, rows_pad - rows_one))).astype(BF16)
    for rows_ref, wide_ref in ((halo_rows_ref, halo_wide_ref), (own_rows_ref, own_wide_ref)):
        for block in range(rows_ref.shape[0]):
            wide_ref[block * hidden : (block + 1) * hidden, :] = dot(k1t, rows_ref[block]).astype(BF16)
    out_chan, rows_two = k2t_ref.shape
    for at in range(0, rows_two, LANES):
        tall = min(LANES, rows_two - at)
        block = k2t_ref[:, at : at + tall].astype(F32)
        if tall < LANES:
            block = jnp.pad(block, ((0, 0), (0, LANES - tall)))
        k2_rows[at : at + tall, :out_chan] = block.T[:tall, :]
    taps = [k2_rows[pl.ds(tap, hidden, stride=TAPS), :][:, :out_chan] for tap in range(TAPS)]
    nothing = jnp.zeros_like(taps[0])

    def tap_for(parity, shift):
        if parity == 0:
            return 1 if shift == 0 else None
        return 2 if shift == 0 else 0

    for j in (1, 2):
        for py in range(2):
            for px in range(2):
                blocks = []
                for above in range(2):
                    a = {(1, 0): 1, (2, 0): 2, (2, 1): 0}.get((j, above))
                    for sy in range(2):
                        for sx in range(2):
                            b, e = tap_for(py, sy), tap_for(px, sx)
                            there = a is not None and b is not None and e is not None
                            blocks.append(taps[a * 9 + b * 3 + e] if there else nothing)
                start = ((j - 1) * 4 + py * 2 + px) * hidden
                back_ref[start : start + hidden, :] = jnp.concatenate(blocks, axis=1).astype(BF16)


def split_cells(planes, split_ref, cells_ref, rows_scr, lhs_scr, cells_scr):
    plane = planes[0].shape[0]
    pitch = plane + 8
    for at, source in enumerate(planes):
        start = at * pitch
        rows_scr[start : start + 8, :] = jnp.zeros((8, plane), F32)
        rows_scr[start + 8 : start + pitch, :] = source[...].astype(F32)
    for pair in range(len(planes) // 2):
        pieces = []
        for member in range(2):
            start = (pair * 2 + member) * pitch + 8
            tiles = [rows_scr[pl.ds(start + t, 8, stride=16), :] for t in range(-1, 16)]
            for q in range(5):
                pieces.append(jnp.concatenate([tiles[4 * group + q] for group in range(4)], axis=1))
        lhs_scr[pair * 80 : (pair + 1) * 80, :] = jnp.concatenate(pieces, axis=0).astype(BF16)
    total_rows = len(planes) * 40
    chunk = 160
    for part in range(total_rows // chunk):
        product = dot(lhs_scr[part * chunk : (part + 1) * chunk, :], split_ref[...])
        for q in range(5):
            start = q * total_rows + part * chunk
            cells_scr[start : start + chunk, :] = product[:, q * LANES : (q + 1) * LANES]
    filled = 5 * total_rows
    width = cells_ref.shape[0]
    if filled < 8 * width:
        cells_scr[filled : 8 * width, :] = jnp.zeros((8 * width - filled, LANES), F32)
    for yh in range(8):
        cells_ref[:, yh * LANES : (yh + 1) * LANES] = cells_scr[pl.ds(yh, width, stride=8), :].astype(BF16)


def own_kernel(
    vol_ref, wide_ref, split_ref, rows_ref,
    part_ref, act_ref, slope_ref, p1_ref, in_one_ref, rows_scr, lhs_scr, cells_scr, cells_ref,
):
    channels, own = vol_ref.shape[0], vol_ref.shape[1]
    planes = [vol_ref.at[c, z] for c in range(channels) for z in range(own)]
    split_cells(planes, split_ref, cells_ref, rows_scr, lhs_scr, cells_scr)
    pre = dot(wide_ref[...], cells_ref[...])
    tall = part_ref.shape[0]
    part_ref[...] = pre[:tall, :]
    quarter = tall // 4
    for at in range(0, tall, quarter):
        act, slope = gelu_and_slope(pre[tall + at : tall + at + quarter, :])
        act_ref[at : at + quarter, :] = act
        slope_ref[at : at + quarter, :] = slope
    blocks, rows_pad, width = rows_ref.shape
    p1 = dot(rows_ref[...].reshape(blocks * rows_pad, width), cells_ref[...]).astype(BF16)
    total = jnp.zeros((rows_pad, rows_pad), F32)
    for block in range(blocks):
        piece = p1[block * rows_pad : (block + 1) * rows_pad, :]
        p1_ref[block] = piece
        if block >= blocks // 2:
            total += dot_nt(piece, piece)
    in_one_ref[...] = total


def forward_kernel(
    scale, halo_ref, wide_ref, split_ref, part_ref, act_ref, k2t_ref, cot_ref, rows_ref, p1_ref,
    grad_ref, p2_ref, slope_ref, low_ref, *rest,
):
    feat_refs, (rows_scr, lhs_scr, cells_scr, cells_ref, p2_scr, feat_scr) = rest[:-6], rest[-6:]
    channels, halo = halo_ref.shape[0], halo_ref.shape[1]
    planes = [halo_ref.at[c, z] for c in range(channels) for z in range(halo)]
    split_cells(planes, split_ref, cells_ref, rows_scr, lhs_scr, cells_scr)
    cells = cells_ref.shape[1]
    lane = lax.broadcasted_iota(jnp.int32, (1, cells), 1)
    side = math.isqrt(cells)
    not_left = (lane % side) != 0
    not_top = lane >= side
    tall = part_ref.shape[0]
    hidden = tall // 4
    rows_two = hidden * TAPS
    part, rows_pad, width = rows_ref.shape
    both = jnp.concatenate([wide_ref[...], rows_ref[...].reshape(part * rows_pad, width)], axis=0)
    product = dot(both, cells_ref[...])
    for at in range(part):
        start = 2 * tall + at * rows_pad
        low_ref[at] = (product[start : start + rows_pad, :] + p1_ref[at].astype(F32)).astype(BF16)
    for j in (2, 1, 0):
        if j < 2:
            pre = product[j * tall : (j + 1) * tall, :]
            if j == 1:
                pre = pre + part_ref[...]
        for parity in range(4):
            rows = slice(parity * hidden, (parity + 1) * hidden)
            if j == 2:
                act = act_ref[rows, :]
            elif j == 1:
                act, slope = gelu_and_slope(pre[rows, :])
                slope_ref[rows, :] = slope
            else:
                act = gelu_parts(pre[rows, :])[0]
            py, px = parity // 2, parity % 2
            for b in ((1,) if py == 0 else (2, 0)):
                for e in ((1,) if px == 0 else (2, 0)):
                    moved = act
                    distance = (side if b == 0 else 0) + (1 if e == 0 else 0)
                    if distance:
                        moved = pltpu.roll(act, distance, axis=1)
                    if b == 0:
                        moved = jnp.where(not_top, moved, 0.0)
                    if e == 0:
                        moved = jnp.where(not_left, moved, 0.0)
                    for k in range(cells // LANES):
                        start = k * rows_two + j * 9 + b * 3 + e
                        p2_scr[pl.ds(start, hidden, stride=TAPS), :] = moved[:, k * LANES : (k + 1) * LANES]
    for k in range(cells // LANES):
        p2_ref[:rows_two, k * LANES : (k + 1) * LANES] = p2_scr[k * rows_two : (k + 1) * rows_two, :].astype(BF16)
    p2_ref[rows_two:, :] = jnp.zeros((p2_ref.shape[0] - rows_two, cells), BF16)
    act, slope = gelu_and_slope(dot(k2t_ref[...], p2_ref[:rows_two, :]))
    grad_ref[...] = (cot_ref[...].astype(F32) * scale * slope).astype(BF16)
    owned = cells // feat_scr.shape[0]
    rows = act.shape[0] * owned // LANES
    count = LANES // owned
    place = lax.broadcasted_iota(jnp.int32, (1, LANES), 1) // owned
    for k in range(cells // LANES):
        tile = act[:, k * LANES : (k + 1) * LANES]
        for u in range(count):
            total = jnp.zeros((rows, LANES), F32)
            for m in range(count):
                block = tile[m * rows : (m + 1) * rows, :]
                if m != u:
                    block = pltpu.roll(block, ((m - u) * owned) % LANES, axis=1)
                total = jnp.where(place == m, block, total)
            if rows < feat_scr.shape[1]:
                total = jnp.pad(total, ((0, feat_scr.shape[1] - rows), (0, 0)))
            feat_scr[k * count + u] = total.astype(BF16)
    owners = feat_refs[0].shape[0]
    cube = lax.axis_index("space") // owners
    for change, feat_ref in enumerate(feat_refs):
        feat_ref[...] = feat_scr[pl.ds((cube ^ change) * owners, owners)]


def large_places(rows_two, out_chan):
    panels = -(-rows_two // LANES)
    pairs = (panels + 1) // 2
    middle = pairs // 2 * 2
    names = [("block", i, j) for j in range(middle, panels) for i in range(middle)]
    names += [("block", i, j) for j in range(middle) for i in range(j)]
    names += [("block", i, j) for j in range(middle, panels) for i in range(middle, j)]
    names += [("pair", p) for p in range(pairs)]
    cross = middle * (panels - middle)
    weights = [("weight_two", j) for j in range(panels - 1)]
    half = (len(names) * LANES + len(weights) * out_chan) // 2
    early = (half - cross * LANES) // out_chan
    order = [(name, LANES) for name in names[:cross]] + [(name, out_chan) for name in weights[:early]]
    order += [(name, LANES) for name in names[cross:]] + [(name, out_chan) for name in weights[early:]]
    places, at = {}, 0
    for name, rows in order:
        places[name] = at
        at += rows
    return panels, middle, places, at


def square_iotas():
    return (
        lax.broadcasted_iota(jnp.int32, (LANES, LANES), 0),
        lax.broadcasted_iota(jnp.int32, (LANES, LANES), 1),
    )


def diagonal_row(block):
    row, col = square_iotas()
    return jnp.sum(jnp.where(row == col, block, 0.0), axis=0, keepdims=True)


def two_in_one(upper, lower):
    row, col = square_iotas()
    return jnp.where(row <= col, upper, lower)


def first_of(block, turned):
    row, col = square_iotas()
    return jnp.where(row <= col, block, turned)


def second_of(block, turned, diagonal):
    row, col = square_iotas()
    return jnp.where(row > col, block, jnp.where(row == col, diagonal, turned))


def square(block):
    return jnp.pad(block, ((0, LANES - block.shape[0]), (0, LANES - block.shape[1])))


def padded_lanes(block):
    return jnp.pad(block, ((0, 0), (0, LANES - block.shape[1])))


def put(halves, at, block):
    half = halves[0].shape[0]
    done = 0
    while done < block.shape[0]:
        side, row = divmod(at + done, half)
        count = min(block.shape[0] - done, half - row)
        halves[side][row : row + count, :] = block[done : done + count, :].astype(BF16)
        done += count


def sums_kernel(
    places, rows_two, p2_ref, grad_ref, mine_ref, other_ref, done_ref, product_scr,
):
    done_ref[...] = jnp.zeros_like(done_ref)
    core = lax.axis_index("batch")
    rest = (places, rows_two, p2_ref, grad_ref, product_scr)
    pl.when(core == 0)(lambda: write_sums(*rest, (mine_ref, other_ref)))
    pl.when(core == 1)(lambda: write_sums(*rest, (other_ref, mine_ref)))


def write_sums(places, rows_two, p2_ref, grad_ref, product_scr, packed):
    panels = p2_ref.shape[0] // LANES
    used = rows_two - (panels - 1) * LANES
    lane = lax.broadcasted_iota(jnp.int32, (1, LANES), 1)
    weight_two = dot_nt(grad_ref[...], p2_ref[...])
    out_chan = weight_two.shape[0]
    last = weight_two[:, (panels - 1) * LANES :]
    spare = LANES - used
    diagonals = []
    for j in range(0, panels, 2):
        wide = min(2, panels - j)
        tall = (j + wide) * LANES
        product = product_scr.at[(j // 2) % 2]
        product[:tall, : wide * LANES] = dot_nt(p2_ref[:tall, :], p2_ref[j * LANES : tall, :])
        for k in range(wide):
            columns = slice(k * LANES, (k + 1) * LANES)
            for i in range(j + k):
                block = product[i * LANES : (i + 1) * LANES, columns]
                if j + k == panels - 1 and i * spare < used:
                    piece = pltpu.roll(last, used - i * spare, axis=1)
                    top = jnp.where(lane >= used, piece, block[:out_chan, :])
                    block = jnp.concatenate([top, block[out_chan:, :]], axis=0)
                put(packed, places["block", i, j + k], block)
        first = product[j * LANES : (j + 1) * LANES, :LANES]
        if wide == 2:
            second = product[(j + 1) * LANES : tall, LANES:]
        else:
            second = square(dot_nt(grad_ref[...], grad_ref[...]))
        diagonals.append(diagonal_row(second))
        block = two_in_one(first, second)
        if wide == 1:
            row, _ = square_iotas()
            for at, diagonal in enumerate(diagonals):
                block = jnp.where(row == used + at, diagonal, block)
        put(packed, places["pair", j // 2], block)
    for j in range(panels - 1):
        put(packed, places["weight_two", j], weight_two[:, j * LANES : (j + 1) * LANES])


def shifted_up(source, scr):
    out_chan, cells = source.shape
    side = math.isqrt(cells)
    lane = lax.broadcasted_iota(jnp.int32, (1, cells), 1)
    value = source[...].astype(F32)
    for sy in range(2):
        for sx in range(2):
            moved = value
            distance = sy * side + sx
            if distance:
                moved = pltpu.roll(value, cells - distance, axis=1)
            if sy:
                moved = jnp.where(lane < cells - side, moved, 0.0)
            if sx:
                moved = jnp.where((lane % side) != side - 1, moved, 0.0)
            at = (2 * sy + sx) * out_chan
            scr[at : at + out_chan, :] = moved.astype(BF16)


def low_kernel(
    grad_ref, back_ref, slope_ref, p1_ref, in_one_ref, done_ref,
    in_one_out, low_out, high_ref, scr,
):
    part, rows_pad, _ = p1_ref.shape
    shifted_up(grad_ref, scr)
    tall = high_ref.shape[0]
    hidden = tall // part
    grad_hidden = dot(back_ref[:, : scr.shape[0]], scr[...])
    high_ref[...] = grad_hidden[tall:, :]
    in_one = in_one_ref[...]
    total = jnp.zeros((hidden, rows_pad + hidden), F32)
    for block in range(part):
        rows = slice(block * hidden, (block + 1) * hidden)
        piece = (grad_hidden[rows, :] * slope_ref[rows, :]).astype(BF16)
        in_one += dot_nt(p1_ref[block], p1_ref[block])
        total += dot_nt(piece, jnp.concatenate([p1_ref[block], piece], axis=0))
    in_one_out[...] = in_one
    low_out[...] = total


def high_kernel(
    above_ref, back_ref, high_ref, slope_ref, p1_ref, in_one_ref, low_ref, out_ref, scr,
):
    shifted_up(above_ref, scr)
    blocks, rows_pad, _ = p1_ref.shape
    part = blocks // 2
    tall, reach = high_ref.shape[0], scr.shape[0]
    hidden = tall // part
    grad_hidden = high_ref[...] + dot(back_ref[tall:, reach:], scr[...])
    total = low_ref[...]
    for block in range(part):
        rows = slice(block * hidden, (block + 1) * hidden)
        piece = (grad_hidden[rows, :] * slope_ref[rows, :]).astype(BF16)
        total += dot_nt(piece, jnp.concatenate([p1_ref[part + block], piece], axis=0))
    weight_one, out_one = total[:, :rows_pad], total[:, rows_pad:]
    out_ref[...] = pack_small(in_one_ref[...], weight_one, out_one).astype(BF16)


SMALL_DIAGONAL = 108
SMALL_WEIGHT = 64
SMALL_REST = 112


def pack_small(in_one, weight_one, out_one):
    row, col = square_iotas()
    hidden = weight_one.shape[0]
    half = hidden // 2
    wide = padded_lanes(weight_one)
    out_square = square(out_one)
    block = jnp.where(row <= col, square(in_one), jnp.where(row < hidden, out_square, 0.0))
    block = jnp.where(row == SMALL_DIAGONAL, diagonal_row(out_square), block)
    first = jnp.pad(wide, ((SMALL_WEIGHT, LANES - SMALL_WEIGHT - hidden), (0, 0)))
    block = jnp.where((row >= SMALL_WEIGHT) & (row < SMALL_WEIGHT + hidden) & (col < SMALL_WEIGHT), first, block)
    turned = pltpu.roll(wide[half:, :], LANES - SMALL_WEIGHT, axis=1)
    lane = lax.broadcasted_iota(jnp.int32, (half, LANES), 1)
    rest = jnp.where(lane >= SMALL_WEIGHT, wide[:half, :], turned)
    return jnp.where(row >= SMALL_REST, jnp.pad(rest, ((SMALL_REST, 0), (0, 0))), block)


def unpack_small(block, rows_one, hidden):
    half = hidden // 2
    turned = block.T
    in_one = first_of(block, turned)[:rows_one, :rows_one]
    out_one = second_of(block, turned, block[SMALL_DIAGONAL : SMALL_DIAGONAL + 1, :])[:hidden, :hidden]
    rest = block[SMALL_REST:, :]
    lane = lax.broadcasted_iota(jnp.int32, (hidden, LANES), 1)
    high = jnp.concatenate([rest, pltpu.roll(rest, SMALL_WEIGHT, axis=1)], axis=0)
    weight_one = jnp.where(lane < SMALL_WEIGHT, block[SMALL_WEIGHT : SMALL_WEIGHT + hidden, :], high)
    return in_one, weight_one[:, :rows_one], out_one


def joined_kernel(mine_ref, came_ref, small_ref, *refs):
    feat_refs, out_ref = refs[:-1], refs[-1]
    owners = out_ref.shape[0]
    large, small = mine_ref.shape[0] // owners, small_ref.shape[0] // owners
    feat_rows = feat_refs[0].shape[1]
    for owner in range(owners):
        rows = slice(owner * large, (owner + 1) * large)
        out_ref[owner, :large, :] = (mine_ref[rows, :].astype(F32) + came_ref[rows, :].astype(F32)).astype(BF16)
        out_ref[owner, large : large + small, :] = small_ref[owner * small : (owner + 1) * small, :]
        for change, feat_ref in enumerate(feat_refs):
            start = large + small + change * feat_rows
            out_ref[owner, start : start + feat_rows, :] = feat_ref[walk(owners)[owner]]


def total_kernel(came_ref, out_ref, feat_ref):
    owners, chunk = came_ref.shape[0], out_ref.shape[0]
    total = came_ref[0, :chunk, :].astype(F32)
    for owner in range(1, owners):
        total += came_ref[owner, :chunk, :].astype(F32)
    out_ref[...] = total.astype(BF16)
    for owner in range(owners):
        feat_ref[owner] = came_ref[owner, chunk:, :]


def pair_kernel(mine_ref, came_ref, out_ref):
    total = (mine_ref[...].astype(F32) + came_ref[...].astype(F32)).astype(BF16)
    for owner in range(out_ref.shape[0]):
        out_ref[owner] = total


def features_kernel(owned_rows, cubes, feat_ref, out_ref, scr):
    owners, owned = out_ref.shape[1], out_ref.shape[2]
    rows = feat_ref.shape[1] // cubes
    members = owners // cubes
    cube = lax.axis_index("space") // members
    for change in range(cubes):
        for member in range(members):
            start = pl.multiple_of(((cube ^ change) * members + walk(members)[member]) * rows, 16)
            scr[pl.ds(start, rows), :] = feat_ref[member, change * rows : (change + 1) * rows, :].astype(F32)
    for i in range(owned_rows):
        block = scr[pl.ds(i, owners, stride=rows), :]
        for m in range(LANES // owned):
            out_ref[m * owned_rows + i] = block[:, m * owned : (m + 1) * owned].astype(BF16)


def gathered_half(source_ref, half_scr):
    owners = source_ref.shape[0]
    tall = half_scr.shape[0] // owners
    for owner in range(owners):
        half_scr[owner * tall : (owner + 1) * tall, :] = source_ref[owner, :tall, :]


def unit_square():
    row, col = square_iotas()
    return jnp.where(row == col, 1.0, 0.0).astype(BF16)


def first_half_copies(middle, factor, out_ref, sems):
    rows_two, split = out_ref.shape[0], middle * LANES
    spots = [(slice(0, split), slice(split, rows_two)), (slice(split, rows_two), slice(0, split))]
    return [pltpu.make_async_copy(factor.at[spot], out_ref.at[spot], sems.at[at]) for at, spot in enumerate(spots)]


def second_half_copies(middle, factor, out_ref, sems):
    rows_two, split = out_ref.shape[0], middle * LANES
    spots = [(slice(0, split), slice(0, split)), (slice(split, rows_two), slice(split, rows_two))]
    return [pltpu.make_async_copy(factor.at[spot], out_ref.at[spot], sems.at[at]) for at, spot in enumerate(spots)]


def wait_for(copies):
    for copy in copies:
        copy.wait()


def write_first_half(places, panels, middle, scale, half_scr, factor, out_ref, sems):
    copies = first_half_copies(middle, factor, out_ref, sems)
    rows_two = out_ref.shape[0]
    split = middle * LANES
    unit = unit_square()
    for j in range(middle, panels):
        wide = min(LANES, rows_two - j * LANES)
        start = places["block", 0, j]
        panel = half_scr[start : start + split, :]
        columns = slice(j * LANES, j * LANES + wide)
        factor[:split, columns] = (panel.astype(F32) * scale)[:, :wide]
        factor[columns, :split] = (dot_nt(unit, panel) * scale)[:wide, :]
    for copy in copies:
        copy.start()


def write_second_half(places, panels, middle, scale, half_scr, factor, out_ref, sems):
    copies = second_half_copies(middle, factor, out_ref, sems)
    rows_two = out_ref.shape[0]
    half = half_scr.shape[0]
    unit = unit_square()
    used = rows_two - (panels - 1) * LANES
    pairs = (panels + 1) // 2
    start = places["pair", pairs - 1] - half
    holder = half_scr[start : start + LANES, :].astype(F32)
    for j in range(panels):
        first = middle if j >= middle else 0
        if j == middle:
            copies[0].start()
        if j % 2 == 0:
            start = places["pair", j // 2] - half
            block = half_scr[start : start + LANES, :]
            turned = dot_nt(unit, block)
            block = block.astype(F32)
            wide = min(LANES, rows_two - j * LANES)
            rows = slice(j * LANES, j * LANES + wide)
            factor[rows, rows] = (first_of(block, turned) * scale)[:wide, :wide]
            if j + 1 < panels:
                rows = slice((j + 1) * LANES, (j + 2) * LANES)
                diagonal = holder[used + j // 2 : used + j // 2 + 1, :]
                factor[rows, rows] = second_of(block, turned, diagonal) * scale
        if j == first:
            continue
        wide = min(LANES, rows_two - j * LANES)
        start = places["block", first, j] - half
        panel = half_scr[start : start + (j - first) * LANES, :]
        columns, rows = slice(j * LANES, j * LANES + wide), slice(first * LANES, j * LANES)
        factor[rows, columns] = (panel.astype(F32) * scale)[:, :wide]
        factor[columns, rows] = (dot_nt(unit, panel) * scale)[:wide, :]
    copies[1].start()


def own_half_kernel(places, panels, middle, scale, mine_ref, out_ref, half_scr, factor, sems):
    gathered_half(mine_ref, half_scr)
    core = lax.axis_index("batch")
    rest = (places, panels, middle, scale, half_scr, factor, out_ref, sems)
    pl.when(core == 0)(functools.partial(write_first_half, *rest))
    pl.when(core == 1)(functools.partial(write_second_half, *rest))
    where = (middle, factor, out_ref, sems)
    pl.when(core == 0)(lambda: wait_for(first_half_copies(*where)))
    pl.when(core == 1)(lambda: wait_for(second_half_copies(*where)))


def unpack_kernel(
    places, panels, middle, scale_one, scale_two, begun_ref, mine_ref, came_ref,
    in_one_out, in_two_ref, out_one_out, out_two_out, weight_one_out, weight_two_out,
    packed, small, factor, in_one_ref, out_one_ref, out_two_ref, weight_one_ref, weight_two_ref, sems,
):
    core = lax.axis_index("batch")
    gathered_half(mine_ref, packed.at[core])
    gathered_half(came_ref, packed.at[1 - core])
    rest = (places, panels, middle, scale_two)
    pl.when(core == 1)(functools.partial(write_first_half, *rest, packed.at[0], factor, in_two_ref, sems))
    pl.when(core == 0)(functools.partial(write_second_half, *rest, packed.at[1], factor, in_two_ref, sems))
    out_chan, rows_two = weight_two_ref.shape
    hidden, rows_one = weight_one_ref.shape
    owners = mine_ref.shape[0]
    tall_large, tall_small = packed.shape[1] // owners, small.shape[0] // owners
    for owner in range(owners):
        rows = slice(tall_large, tall_large + tall_small)
        small[owner * tall_small : (owner + 1) * tall_small, :] = mine_ref[owner, rows, :].astype(F32) + came_ref[
            owner, rows, :
        ].astype(F32)
    half = packed.shape[1]

    def get(name, count):
        side, row = divmod(places[name], half)
        return packed[side, row : row + count, :].astype(F32)

    used = rows_two - (panels - 1) * LANES
    spare = LANES - used
    lane = lax.broadcasted_iota(jnp.int32, (1, LANES), 1)
    last = jnp.zeros((out_chan, LANES), F32)
    for i in range(-(-used // spare)):
        piece = pltpu.roll(get(("block", i, panels - 1), out_chan), LANES - (used - i * spare), axis=1)
        last = jnp.where((lane >= i * spare) & (lane < (i + 1) * spare), piece, last)
    for j in range(panels - 1):
        weight_two_ref[:, j * LANES : (j + 1) * LANES] = get(("weight_two", j), out_chan)
    weight_two_ref[:, (panels - 1) * LANES :] = last[:, :used]
    copies = [pltpu.make_async_copy(weight_two_ref, weight_two_out, sems.at[2])]
    copies[0].start()
    pairs = (panels + 1) // 2
    block = get(("pair", pairs - 1), LANES)
    diagonal = block[used + pairs - 1 : used + pairs, :]
    out_two_ref[...] = second_of(block, block.T, diagonal)[:out_chan, :out_chan]
    in_one, weight_one, out_one = unpack_small(small[...], rows_one, hidden)
    in_one_ref[...] = in_one * scale_one
    weight_one_ref[...] = weight_one
    out_one_ref[...] = out_one
    results = ((in_one_ref, in_one_out), (out_one_ref, out_one_out), (out_two_ref, out_two_out))
    for at, (here, there) in enumerate(results + ((weight_one_ref, weight_one_out),)):
        copies.append(pltpu.make_async_copy(here, there, sems.at[3 + at]))
        copies[-1].start()
    wait_for(copies)
    where = (middle, factor, in_two_ref, sems)
    pl.when(core == 1)(lambda: wait_for(first_half_copies(*where)))
    pl.when(core == 0)(lambda: wait_for(second_half_copies(*where)))


def cube_size(space):
    return 8 if space % 8 == 0 else space


def walk(size):
    return [at ^ (at >> 1) for at in range(size)]


def exchange(parts, size):
    space = lax.axis_size("space")
    groups = [[base + at for at in walk(size)] for base in range(0, space, size)]
    return lax.all_to_all(parts, "space", split_axis=0, concat_axis=0, axis_index_groups=groups)


def from_partner(block, stride):
    return lax.ppermute(block, "space", [(i, i ^ stride) for i in range(lax.axis_size("space"))])


def call(kernel, out_shape, scratch=(), micros=3, mib=24, **more):
    return pl.pallas_call(
        kernel,
        out_shape=out_shape,
        scratch_shapes=list(scratch),
        cost_estimate=pl.CostEstimate(flops=int(micros * 1.1e9), bytes_accessed=1 << 20, transcendentals=0),
        compiler_params=pltpu.CompilerParams(vmem_limit_bytes=mib * MIB),
        **more,
    )


def passed_along(block, axis, distance):
    devices = range(lax.axis_size(axis))
    route = [(i - distance, i) for i in devices if i - distance in devices]
    return lax.ppermute(block, axis, route)


def swapped(block):
    return lax.ppermute(block, "batch", [(0, 1), (1, 0)])


def like(shape, kind=BF16):
    return jax.ShapeDtypeStruct(shape, kind)


def split_scratch(count, plane):
    return [
        pltpu.VMEM((count * (plane + 8) + 16, plane), F32),
        pltpu.VMEM((count * 40, 4 * plane), BF16),
        pltpu.VMEM((8 * up_to(25 * count, 16) + 8, LANES), F32),
    ]


def local(volume, kernel_one, kernel_two, cotangent):
    channels, _, own, plane, _ = volume.shape
    rows_one, hidden = kernel_one.shape
    rows_two, out_chan = kernel_two.shape
    cells = cotangent.shape[3]
    side = math.isqrt(cells)
    space = lax.axis_size("space")
    devices_all = space * lax.axis_size("batch")
    total_one = devices_all * 8 * cells
    total_two = devices_all * cells
    rows_pad = up_to(rows_one, 16)
    halo = own - 1
    halo_width = up_to(25 * channels * halo, 16)
    own_width = up_to(25 * channels * own, 16)
    tall = 4 * hidden

    vol = volume.reshape(channels, own, plane, plane)
    halo_block = passed_along(vol[:, own - halo :], "space", 1)
    halo_rows = jnp.asarray(patch_rows(channels, 0, halo, (0, 1), rows_pad), BF16)
    own_rows = jnp.asarray(patch_rows(channels, halo, own, (1, 2), rows_pad), BF16)
    split = jnp.asarray(split_columns(plane, side), BF16)
    halo_wide, own_wide, back = call(
        prepare_kernel,
        (like((2 * tall, halo_width)), like((2 * tall, own_width)), like((2 * tall, 8 * out_chan))),
        [pltpu.VMEM((rows_two + 32, LANES), F32)],
        micros=3,
    )(kernel_one.T, kernel_two.T, halo_rows, own_rows)
    part, act_high, slope_high, p1, in_one_part = call(
        own_kernel,
        (
            like((tall, cells), F32),
            like((tall, cells), F32),
            like((tall, cells), F32),
            like((8, rows_pad, cells)),
            like((rows_pad, rows_pad), F32),
        ),
        split_scratch(channels * own, plane) + [pltpu.VMEM((own_width, cells), BF16)],
        micros=6,
    )(vol, own_wide, split, own_rows)
    panels, middle, places, large_rows = large_places(rows_two, out_chan)
    feat_rows = out_chan * cells // space // LANES
    feat_tall = up_to(feat_rows, 16)
    cube = cube_size(space)
    cubes = space // cube
    grad_two, p2, slope_low, p1_low, *feats = call(
        functools.partial(forward_kernel, 1.0 / math.sqrt(total_two)),
        (
            like((out_chan, cells)),
            like((panels * LANES, cells)),
            like((tall, cells), F32),
            like((4, rows_pad, cells)),
        )
        + (like((cube, feat_tall, LANES)),) * cubes,
        split_scratch(channels * halo, plane)
        + [pltpu.VMEM((halo_width, cells), BF16)]
        + [pltpu.VMEM((rows_two * (cells // LANES) + 32, LANES), F32), pltpu.VMEM((space, feat_tall, LANES), BF16)],
        micros=5,
    )(halo_block, halo_wide, split, part, act_high, kernel_two.T, cotangent.reshape(out_chan, cells), halo_rows[4:], p1)
    feats = feats[:1] + [from_partner(feats[change], change * cube) for change in range(1, cubes)]
    above = passed_along(grad_two, "space", -1)
    feats, above = lax.optimization_barrier((feats, above))

    half = large_rows // 2
    small_rows = LANES
    chunk = (half + small_rows) // cube
    mine, other, done = call(
        functools.partial(sums_kernel, places, rows_two),
        (like((half, LANES)), like((half, LANES)), like((8, LANES), F32)),
        [pltpu.VMEM((2, panels * LANES, 2 * LANES), F32)],
        micros=0.1,
    )(p2, grad_two)
    came = swapped(other)
    in_one_low, low, high = call(
        low_kernel,
        (like((rows_pad, rows_pad), F32), like((hidden, rows_pad + hidden), F32), like((tall, cells), F32)),
        [pltpu.VMEM((4 * out_chan, cells), BF16)],
        micros=0.1,
    )(grad_two, back, slope_low, p1_low, in_one_part, done)
    small = call(
        high_kernel,
        like((small_rows, LANES)),
        [pltpu.VMEM((4 * out_chan, cells), BF16)],
        micros=12,
    )(above, back, high, slope_high, p1, in_one_low, low)
    joined = call(joined_kernel, like((cube, chunk + cubes * feat_tall, LANES)), micros=1)(mine, came, small, *feats)
    total, feat = call(
        total_kernel, (like((chunk, LANES)), like((cube, cubes * feat_tall, LANES))), micros=1
    )(exchange(joined, cube))
    stride = cube
    while 2 * stride < space:
        total = (total.astype(F32) + from_partner(total, stride).astype(F32)).astype(BF16)
        stride *= 2
    features = call(
        functools.partial(features_kernel, feat_rows, cubes),
        like((out_chan, space, cells // space)),
        [pltpu.VMEM(((space + 1) * feat_tall, LANES), F32)],
        micros=1,
    )(feat)
    other = from_partner(total, stride) if stride < space else jnp.zeros_like(total)
    other, features = lax.optimization_barrier((other, features))
    copies = call(pair_kernel, like((cube, chunk, LANES)), micros=1)(total, other)
    mine = exchange(copies, cube)
    came = swapped(mine)
    anywhere = pl.BlockSpec(memory_space=pl.ANY)
    begun = call(
        functools.partial(own_half_kernel, places, panels, middle, 1.0 / total_two),
        like((rows_two, rows_two), F32),
        [
            pltpu.VMEM((half, LANES), BF16),
            pltpu.VMEM((rows_two, rows_two), F32),
            pltpu.SemaphoreType.DMA((2,)),
        ],
        micros=2,
        out_specs=anywhere,
    )(mine)
    kinds = [
        like(shape, F32)
        for shape in (
            (rows_one, rows_one),
            (rows_two, rows_two),
            (hidden, hidden),
            (out_chan, out_chan),
            (hidden, rows_one),
            (out_chan, rows_two),
        )
    ]
    in_one, in_two, out_one, out_two, weight_one, weight_two = call(
        functools.partial(unpack_kernel, places, panels, middle, 1.0 / total_one, 1.0 / total_two),
        tuple(kinds),
        [
            pltpu.VMEM((2, half, LANES), BF16),
            pltpu.VMEM((small_rows, LANES), F32),
            pltpu.VMEM((rows_two, rows_two), F32),
        ]
        + [pltpu.VMEM(kind.shape, F32) for at, kind in enumerate(kinds) if at != 1]
        + [pltpu.SemaphoreType.DMA((7,))],
        micros=2,
        in_specs=[anywhere, pl.BlockSpec(memory_space=pltpu.VMEM), pl.BlockSpec(memory_space=pltpu.VMEM)],
        out_specs=(anywhere,) * 6,
        input_output_aliases={0: 1},
    )(begun, mine, came)
    features = features.reshape(out_chan, 1, space, cells // space)
    return features, in_one, in_two, out_one, out_two, weight_one.T, weight_two.T


def solution(mesh):
    placed = (P(None, "batch", "space", None, None), P(), P(), P(None, "batch", "space", None))
    return jax.shard_map(
        local,
        mesh=mesh,
        in_specs=placed,
        out_specs=(P(None, "batch", None, "space"), P(), P(), P(), P(), P(), P()),
        check_vma=False,
    )
```

```python
import functools
import math

import jax
import jax.numpy as jnp
import numpy as np
from jax import lax
from jax.experimental import pallas as pl
from jax.experimental.pallas import tpu as pltpu
from jax.sharding import PartitionSpec as P

F32 = jnp.float32
BF16 = jnp.bfloat16
LANES = 128
TAPS = 27
MIB = 1024 * 1024


def up_to(count, unit):
    return -(-count // unit) * unit


def split_columns(plane, quarter):
    table = np.zeros((4, plane, 5, 4, quarter), np.float32)
    for group in range(4):
        for q in range(5):
            for cell in range(quarter):
                x = 4 * cell + q - 1
                if 0 <= x < plane:
                    table[group, x, q, group, cell] = 1.0
    return table.reshape(4 * plane, 5 * 4 * quarter)


def patch_rows(channels, first, planes, hidden_planes, rows):
    width = up_to(25 * channels * planes, 16)
    table = np.zeros((len(hidden_planes), 2, 2, rows, width), np.float32)
    for at, j in enumerate(hidden_planes):
        for a in range(3):
            plane = 2 * j + a - first
            if not 0 <= plane < planes:
                continue
            for py, px, c, b, e in np.ndindex(2, 2, channels, 3, 3):
                source = (((2 * px + e) * channels + c) * planes + plane) * 5 + 2 * py + b
                table[at, py, px, c * TAPS + a * 9 + b * 3 + e, source] = 1.0
    return table.reshape(len(hidden_planes) * 4, rows, width)


def dot(first, second):
    return jnp.dot(first, second, preferred_element_type=F32)


def dot_nt(first, second):
    return lax.dot_general(first, second, (((1,), (1,)), ((), ())), preferred_element_type=F32)


def gelu_parts(value):
    square = value * value
    tangent = jnp.tanh(0.7978845608028654 * (value + 0.044715 * value * square))
    half = 0.5 * (1.0 + tangent)
    return value * half, half, tangent, square


def gelu_and_slope(value):
    act, half, tangent, square = gelu_parts(value)
    slope = half + 0.5 * value * (1.0 - tangent * tangent) * (
        0.7978845608028654 * (1.0 + 3.0 * 0.044715 * square)
    )
    return act, slope


def prepare_kernel(k1t_ref, k2t_ref, halo_rows_ref, own_rows_ref, halo_wide_ref, own_wide_ref, back_ref, k2_rows):
    hidden, rows_one = k1t_ref.shape
    rows_pad = halo_rows_ref.shape[1]
    k1t = jnp.pad(k1t_ref[...].astype(F32), ((0, 0), (0, rows_pad - rows_one))).astype(BF16)
    for rows_ref, wide_ref in ((halo_rows_ref, halo_wide_ref), (own_rows_ref, own_wide_ref)):
        for block in range(rows_ref.shape[0]):
            wide_ref[block * hidden : (block + 1) * hidden, :] = dot(k1t, rows_ref[block]).astype(BF16)
    out_chan, rows_two = k2t_ref.shape
    for at in range(0, rows_two, LANES):
        tall = min(LANES, rows_two - at)
        block = k2t_ref[:, at : at + tall].astype(F32)
        if tall < LANES:
            block = jnp.pad(block, ((0, 0), (0, LANES - tall)))
        k2_rows[at : at + tall, :out_chan] = block.T[:tall, :]
    taps = [k2_rows[pl.ds(tap, hidden, stride=TAPS), :][:, :out_chan] for tap in range(TAPS)]
    nothing = jnp.zeros_like(taps[0])

    def tap_for(parity, shift):
        if parity == 0:
            return 1 if shift == 0 else None
        return 2 if shift == 0 else 0

    for j in (1, 2):
        for py in range(2):
            for px in range(2):
                blocks = []
                for above in range(2):
                    a = {(1, 0): 1, (2, 0): 2, (2, 1): 0}.get((j, above))
                    for sy in range(2):
                        for sx in range(2):
                            b, e = tap_for(py, sy), tap_for(px, sx)
                            there = a is not None and b is not None and e is not None
                            blocks.append(taps[a * 9 + b * 3 + e] if there else nothing)
                start = ((j - 1) * 4 + py * 2 + px) * hidden
                back_ref[start : start + hidden, :] = jnp.concatenate(blocks, axis=1).astype(BF16)


def split_cells(planes, split_ref, cells_ref, rows_scr, lhs_scr, cells_scr):
    plane = planes[0].shape[0]
    pitch = plane + 8
    for at, source in enumerate(planes):
        start = at * pitch
        rows_scr[start : start + 8, :] = jnp.zeros((8, plane), F32)
        rows_scr[start + 8 : start + pitch, :] = source[...].astype(F32)
    for pair in range(len(planes) // 2):
        pieces = []
        for member in range(2):
            start = (pair * 2 + member) * pitch + 8
            tiles = [rows_scr[pl.ds(start + t, 8, stride=16), :] for t in range(-1, 16)]
            for q in range(5):
                pieces.append(jnp.concatenate([tiles[4 * group + q] for group in range(4)], axis=1))
        lhs_scr[pair * 80 : (pair + 1) * 80, :] = jnp.concatenate(pieces, axis=0).astype(BF16)
    total_rows = len(planes) * 40
    chunk = 160
    for part in range(total_rows // chunk):
        product = dot(lhs_scr[part * chunk : (part + 1) * chunk, :], split_ref[...])
        for q in range(5):
            start = q * total_rows + part * chunk
            cells_scr[start : start + chunk, :] = product[:, q * LANES : (q + 1) * LANES]
    filled = 5 * total_rows
    width = cells_ref.shape[0]
    if filled < 8 * width:
        cells_scr[filled : 8 * width, :] = jnp.zeros((8 * width - filled, LANES), F32)
    for yh in range(8):
        cells_ref[:, yh * LANES : (yh + 1) * LANES] = cells_scr[pl.ds(yh, width, stride=8), :].astype(BF16)


def own_kernel(
    vol_ref, wide_ref, split_ref, rows_ref,
    part_ref, act_ref, slope_ref, p1_ref, in_one_ref, rows_scr, lhs_scr, cells_scr, cells_ref,
):
    channels, own = vol_ref.shape[0], vol_ref.shape[1]
    planes = [vol_ref.at[c, z] for c in range(channels) for z in range(own)]
    split_cells(planes, split_ref, cells_ref, rows_scr, lhs_scr, cells_scr)
    pre = dot(wide_ref[...], cells_ref[...])
    tall = part_ref.shape[0]
    part_ref[...] = pre[:tall, :]
    quarter = tall // 4
    for at in range(0, tall, quarter):
        act, slope = gelu_and_slope(pre[tall + at : tall + at + quarter, :])
        act_ref[at : at + quarter, :] = act
        slope_ref[at : at + quarter, :] = slope
    blocks, rows_pad, width = rows_ref.shape
    p1 = dot(rows_ref[...].reshape(blocks * rows_pad, width), cells_ref[...]).astype(BF16)
    total = jnp.zeros((rows_pad, rows_pad), F32)
    for block in range(blocks):
        piece = p1[block * rows_pad : (block + 1) * rows_pad, :]
        p1_ref[block] = piece
        if block >= blocks // 2:
            total += dot_nt(piece, piece)
    in_one_ref[...] = total


def forward_kernel(
    scale, halo_ref, wide_ref, split_ref, part_ref, act_ref, k2t_ref, cot_ref, rows_ref, p1_ref,
    grad_ref, p2_ref, slope_ref, low_ref, *rest,
):
    feat_refs, (rows_scr, lhs_scr, cells_scr, cells_ref, p2_scr, feat_scr) = rest[:-6], rest[-6:]
    channels, halo = halo_ref.shape[0], halo_ref.shape[1]
    planes = [halo_ref.at[c, z] for c in range(channels) for z in range(halo)]
    split_cells(planes, split_ref, cells_ref, rows_scr, lhs_scr, cells_scr)
    cells = cells_ref.shape[1]
    lane = lax.broadcasted_iota(jnp.int32, (1, cells), 1)
    side = math.isqrt(cells)
    not_left = (lane % side) != 0
    not_top = lane >= side
    tall = part_ref.shape[0]
    hidden = tall // 4
    rows_two = hidden * TAPS
    part, rows_pad, width = rows_ref.shape
    both = jnp.concatenate([wide_ref[...], rows_ref[...].reshape(part * rows_pad, width)], axis=0)
    product = dot(both, cells_ref[...])
    for at in range(part):
        start = 2 * tall + at * rows_pad
        low_ref[at] = (product[start : start + rows_pad, :] + p1_ref[at].astype(F32)).astype(BF16)
    for j in (2, 1, 0):
        if j < 2:
            pre = product[j * tall : (j + 1) * tall, :]
            if j == 1:
                pre = pre + part_ref[...]
        for parity in range(4):
            rows = slice(parity * hidden, (parity + 1) * hidden)
            if j == 2:
                act = act_ref[rows, :]
            elif j == 1:
                act, slope = gelu_and_slope(pre[rows, :])
                slope_ref[rows, :] = slope
            else:
                act = gelu_parts(pre[rows, :])[0]
            py, px = parity // 2, parity % 2
            for b in ((1,) if py == 0 else (2, 0)):
                for e in ((1,) if px == 0 else (2, 0)):
                    moved = act
                    distance = (side if b == 0 else 0) + (1 if e == 0 else 0)
                    if distance:
                        moved = pltpu.roll(act, distance, axis=1)
                    if b == 0:
                        moved = jnp.where(not_top, moved, 0.0)
                    if e == 0:
                        moved = jnp.where(not_left, moved, 0.0)
                    for k in range(cells // LANES):
                        start = k * rows_two + j * 9 + b * 3 + e
                        p2_scr[pl.ds(start, hidden, stride=TAPS), :] = moved[:, k * LANES : (k + 1) * LANES]
    for k in range(cells // LANES):
        p2_ref[:rows_two, k * LANES : (k + 1) * LANES] = p2_scr[k * rows_two : (k + 1) * rows_two, :].astype(BF16)
    p2_ref[rows_two:, :] = jnp.zeros((p2_ref.shape[0] - rows_two, cells), BF16)
    act, slope = gelu_and_slope(dot(k2t_ref[...], p2_ref[:rows_two, :]))
    grad_ref[...] = (cot_ref[...].astype(F32) * scale * slope).astype(BF16)
    owned = cells // feat_scr.shape[0]
    rows = act.shape[0] * owned // LANES
    count = LANES // owned
    place = lax.broadcasted_iota(jnp.int32, (1, LANES), 1) // owned
    for k in range(cells // LANES):
        tile = act[:, k * LANES : (k + 1) * LANES]
        for u in range(count):
            total = jnp.zeros((rows, LANES), F32)
            for m in range(count):
                block = tile[m * rows : (m + 1) * rows, :]
                if m != u:
                    block = pltpu.roll(block, ((m - u) * owned) % LANES, axis=1)
                total = jnp.where(place == m, block, total)
            if rows < feat_scr.shape[1]:
                total = jnp.pad(total, ((0, feat_scr.shape[1] - rows), (0, 0)))
            feat_scr[k * count + u] = total.astype(BF16)
    owners = feat_refs[0].shape[0]
    cube = lax.axis_index("space") // owners
    for change, feat_ref in enumerate(feat_refs):
        feat_ref[...] = feat_scr[pl.ds((cube ^ change) * owners, owners)]


def large_places(rows_two, out_chan):
    panels = -(-rows_two // LANES)
    pairs = (panels + 1) // 2
    middle = pairs // 2 * 2
    names = [("block", i, j) for j in range(middle, panels) for i in range(middle)]
    names += [("block", i, j) for j in range(middle) for i in range(j)]
    names += [("block", i, j) for j in range(middle, panels) for i in range(middle, j)]
    names += [("pair", p) for p in range(pairs)]
    cross = middle * (panels - middle)
    weights = [("weight_two", j) for j in range(panels - 1)]
    half = (len(names) * LANES + len(weights) * out_chan) // 2
    early = (half - cross * LANES) // out_chan
    order = [(name, LANES) for name in names[:cross]] + [(name, out_chan) for name in weights[:early]]
    order += [(name, LANES) for name in names[cross:]] + [(name, out_chan) for name in weights[early:]]
    places, at = {}, 0
    for name, rows in order:
        places[name] = at
        at += rows
    return panels, middle, places, at


def square_iotas():
    return (
        lax.broadcasted_iota(jnp.int32, (LANES, LANES), 0),
        lax.broadcasted_iota(jnp.int32, (LANES, LANES), 1),
    )


def diagonal_row(block):
    row, col = square_iotas()
    return jnp.sum(jnp.where(row == col, block, 0.0), axis=0, keepdims=True)


def two_in_one(upper, lower):
    row, col = square_iotas()
    return jnp.where(row <= col, upper, lower)


def first_of(block, turned):
    row, col = square_iotas()
    return jnp.where(row <= col, block, turned)


def second_of(block, turned, diagonal):
    row, col = square_iotas()
    return jnp.where(row > col, block, jnp.where(row == col, diagonal, turned))


def square(block):
    return jnp.pad(block, ((0, LANES - block.shape[0]), (0, LANES - block.shape[1])))


def padded_lanes(block):
    return jnp.pad(block, ((0, 0), (0, LANES - block.shape[1])))


def put(halves, at, block):
    half = halves[0].shape[0]
    done = 0
    while done < block.shape[0]:
        side, row = divmod(at + done, half)
        count = min(block.shape[0] - done, half - row)
        halves[side][row : row + count, :] = block[done : done + count, :].astype(BF16)
        done += count


def sums_kernel(
    places, rows_two, p2_ref, grad_ref, mine_ref, other_ref, done_ref, product_scr,
):
    done_ref[...] = jnp.zeros_like(done_ref)
    core = lax.axis_index("batch")
    rest = (places, rows_two, p2_ref, grad_ref, product_scr)
    pl.when(core == 0)(lambda: write_sums(*rest, (mine_ref, other_ref)))
    pl.when(core == 1)(lambda: write_sums(*rest, (other_ref, mine_ref)))


def write_sums(places, rows_two, p2_ref, grad_ref, product_scr, packed):
    panels = p2_ref.shape[0] // LANES
    used = rows_two - (panels - 1) * LANES
    lane = lax.broadcasted_iota(jnp.int32, (1, LANES), 1)
    weight_two = dot_nt(grad_ref[...], p2_ref[...])
    out_chan = weight_two.shape[0]
    last = weight_two[:, (panels - 1) * LANES :]
    spare = LANES - used
    diagonals = []
    for j in range(0, panels, 2):
        wide = min(2, panels - j)
        tall = (j + wide) * LANES
        product = product_scr.at[(j // 2) % 2]
        product[:tall, : wide * LANES] = dot_nt(p2_ref[:tall, :], p2_ref[j * LANES : tall, :])
        for k in range(wide):
            columns = slice(k * LANES, (k + 1) * LANES)
            for i in range(j + k):
                block = product[i * LANES : (i + 1) * LANES, columns]
                if j + k == panels - 1 and i * spare < used:
                    piece = pltpu.roll(last, used - i * spare, axis=1)
                    top = jnp.where(lane >= used, piece, block[:out_chan, :])
                    block = jnp.concatenate([top, block[out_chan:, :]], axis=0)
                put(packed, places["block", i, j + k], block)
        first = product[j * LANES : (j + 1) * LANES, :LANES]
        if wide == 2:
            second = product[(j + 1) * LANES : tall, LANES:]
        else:
            second = square(dot_nt(grad_ref[...], grad_ref[...]))
        diagonals.append(diagonal_row(second))
        block = two_in_one(first, second)
        if wide == 1:
            row, _ = square_iotas()
            for at, diagonal in enumerate(diagonals):
                block = jnp.where(row == used + at, diagonal, block)
        put(packed, places["pair", j // 2], block)
    for j in range(panels - 1):
        put(packed, places["weight_two", j], weight_two[:, j * LANES : (j + 1) * LANES])


def shifted_up(source, scr):
    out_chan, cells = source.shape
    side = math.isqrt(cells)
    lane = lax.broadcasted_iota(jnp.int32, (1, cells), 1)
    value = source[...].astype(F32)
    for sy in range(2):
        for sx in range(2):
            moved = value
            distance = sy * side + sx
            if distance:
                moved = pltpu.roll(value, cells - distance, axis=1)
            if sy:
                moved = jnp.where(lane < cells - side, moved, 0.0)
            if sx:
                moved = jnp.where((lane % side) != side - 1, moved, 0.0)
            at = (2 * sy + sx) * out_chan
            scr[at : at + out_chan, :] = moved.astype(BF16)


def low_kernel(
    grad_ref, back_ref, slope_ref, p1_ref, in_one_ref, done_ref,
    in_one_out, low_out, high_ref, scr,
):
    part, rows_pad, _ = p1_ref.shape
    shifted_up(grad_ref, scr)
    tall = high_ref.shape[0]
    hidden = tall // part
    grad_hidden = dot(back_ref[:, : scr.shape[0]], scr[...])
    high_ref[...] = grad_hidden[tall:, :]
    in_one = in_one_ref[...]
    total = jnp.zeros((hidden, rows_pad + hidden), F32)
    for block in range(part):
        rows = slice(block * hidden, (block + 1) * hidden)
        piece = (grad_hidden[rows, :] * slope_ref[rows, :]).astype(BF16)
        in_one += dot_nt(p1_ref[block], p1_ref[block])
        total += dot_nt(piece, jnp.concatenate([p1_ref[block], piece], axis=0))
    in_one_out[...] = in_one
    low_out[...] = total


def high_kernel(
    above_ref, back_ref, high_ref, slope_ref, p1_ref, in_one_ref, low_ref, out_ref, scr,
):
    shifted_up(above_ref, scr)
    blocks, rows_pad, _ = p1_ref.shape
    part = blocks // 2
    tall, reach = high_ref.shape[0], scr.shape[0]
    hidden = tall // part
    grad_hidden = high_ref[...] + dot(back_ref[tall:, reach:], scr[...])
    total = low_ref[...]
    for block in range(part):
        rows = slice(block * hidden, (block + 1) * hidden)
        piece = (grad_hidden[rows, :] * slope_ref[rows, :]).astype(BF16)
        total += dot_nt(piece, jnp.concatenate([p1_ref[part + block], piece], axis=0))
    weight_one, out_one = total[:, :rows_pad], total[:, rows_pad:]
    out_ref[...] = pack_small(in_one_ref[...], weight_one, out_one).astype(BF16)


SMALL_DIAGONAL = 108
SMALL_WEIGHT = 64
SMALL_REST = 112


def pack_small(in_one, weight_one, out_one):
    row, col = square_iotas()
    hidden = weight_one.shape[0]
    half = hidden // 2
    wide = padded_lanes(weight_one)
    out_square = square(out_one)
    block = jnp.where(row <= col, square(in_one), jnp.where(row < hidden, out_square, 0.0))
    block = jnp.where(row == SMALL_DIAGONAL, diagonal_row(out_square), block)
    first = jnp.pad(wide, ((SMALL_WEIGHT, LANES - SMALL_WEIGHT - hidden), (0, 0)))
    block = jnp.where((row >= SMALL_WEIGHT) & (row < SMALL_WEIGHT + hidden) & (col < SMALL_WEIGHT), first, block)
    turned = pltpu.roll(wide[half:, :], LANES - SMALL_WEIGHT, axis=1)
    lane = lax.broadcasted_iota(jnp.int32, (half, LANES), 1)
    rest = jnp.where(lane >= SMALL_WEIGHT, wide[:half, :], turned)
    return jnp.where(row >= SMALL_REST, jnp.pad(rest, ((SMALL_REST, 0), (0, 0))), block)


def unpack_small(block, rows_one, hidden):
    half = hidden // 2
    turned = block.T
    in_one = first_of(block, turned)[:rows_one, :rows_one]
    out_one = second_of(block, turned, block[SMALL_DIAGONAL : SMALL_DIAGONAL + 1, :])[:hidden, :hidden]
    rest = block[SMALL_REST:, :]
    lane = lax.broadcasted_iota(jnp.int32, (hidden, LANES), 1)
    high = jnp.concatenate([rest, pltpu.roll(rest, SMALL_WEIGHT, axis=1)], axis=0)
    weight_one = jnp.where(lane < SMALL_WEIGHT, block[SMALL_WEIGHT : SMALL_WEIGHT + hidden, :], high)
    return in_one, weight_one[:, :rows_one], out_one


def tail_kernel(small_ref, *refs):
    feat_refs, out_ref = refs[:-1], refs[-1]
    owners = out_ref.shape[0]
    small = small_ref.shape[0] // owners
    feat_rows = feat_refs[0].shape[1]
    for owner in range(owners):
        out_ref[owner, :small, :] = small_ref[owner * small : (owner + 1) * small, :]
        for change, feat_ref in enumerate(feat_refs):
            start = small + change * feat_rows
            out_ref[owner, start : start + feat_rows, :] = feat_ref[walk(owners)[owner]]


def joined_kernel(mine_ref, came_ref, tail_ref, out_ref):
    owners = out_ref.shape[0]
    large = mine_ref.shape[0] // owners
    for owner in range(owners):
        rows = slice(owner * large, (owner + 1) * large)
        out_ref[owner, :large, :] = (mine_ref[rows, :].astype(F32) + came_ref[rows, :].astype(F32)).astype(BF16)
        out_ref[owner, large:, :] = tail_ref[owner]


def total_kernel(came_ref, out_ref, feat_ref):
    owners, chunk = came_ref.shape[0], out_ref.shape[0]
    total = came_ref[0, :chunk, :].astype(F32)
    for owner in range(1, owners):
        total += came_ref[owner, :chunk, :].astype(F32)
    out_ref[...] = total.astype(BF16)
    for owner in range(owners):
        feat_ref[owner] = came_ref[owner, chunk:, :]


def pair_kernel(mine_ref, came_ref, out_ref):
    total = (mine_ref[...].astype(F32) + came_ref[...].astype(F32)).astype(BF16)
    for owner in range(out_ref.shape[0]):
        out_ref[owner] = total


def features_kernel(owned_rows, cubes, feat_ref, out_ref, scr):
    owners, owned = out_ref.shape[1], out_ref.shape[2]
    rows = feat_ref.shape[1] // cubes
    members = owners // cubes
    cube = lax.axis_index("space") // members
    for change in range(cubes):
        for member in range(members):
            start = pl.multiple_of(((cube ^ change) * members + walk(members)[member]) * rows, 16)
            scr[pl.ds(start, rows), :] = feat_ref[member, change * rows : (change + 1) * rows, :].astype(F32)
    for i in range(owned_rows):
        block = scr[pl.ds(i, owners, stride=rows), :]
        for m in range(LANES // owned):
            out_ref[m * owned_rows + i] = block[:, m * owned : (m + 1) * owned].astype(BF16)


def gathered_half(source_ref, half_scr):
    owners = source_ref.shape[0]
    tall = half_scr.shape[0] // owners
    for owner in range(owners):
        half_scr[owner * tall : (owner + 1) * tall, :] = source_ref[owner, :tall, :]


def unit_square():
    row, col = square_iotas()
    return jnp.where(row == col, 1.0, 0.0).astype(BF16)


def first_half_copies(middle, factor, out_ref, sems):
    rows_two, split = out_ref.shape[0], middle * LANES
    spots = [(slice(0, split), slice(split, rows_two)), (slice(split, rows_two), slice(0, split))]
    return [pltpu.make_async_copy(factor.at[spot], out_ref.at[spot], sems.at[at]) for at, spot in enumerate(spots)]


def second_half_copies(middle, factor, out_ref, sems):
    rows_two, split = out_ref.shape[0], middle * LANES
    spots = [(slice(0, split), slice(0, split)), (slice(split, rows_two), slice(split, rows_two))]
    return [pltpu.make_async_copy(factor.at[spot], out_ref.at[spot], sems.at[at]) for at, spot in enumerate(spots)]


def wait_for(copies):
    for copy in copies:
        copy.wait()


def write_first_half(places, panels, middle, scale, half_scr, factor, out_ref, sems):
    copies = first_half_copies(middle, factor, out_ref, sems)
    rows_two = out_ref.shape[0]
    split = middle * LANES
    unit = unit_square()
    for j in range(middle, panels):
        wide = min(LANES, rows_two - j * LANES)
        start = places["block", 0, j]
        panel = half_scr[start : start + split, :]
        columns = slice(j * LANES, j * LANES + wide)
        factor[:split, columns] = (panel.astype(F32) * scale)[:, :wide]
        factor[columns, :split] = (dot_nt(unit, panel) * scale)[:wide, :]
    for copy in copies:
        copy.start()


def write_second_half(places, panels, middle, scale, half_scr, factor, out_ref, sems):
    copies = second_half_copies(middle, factor, out_ref, sems)
    rows_two = out_ref.shape[0]
    half = half_scr.shape[0]
    unit = unit_square()
    used = rows_two - (panels - 1) * LANES
    pairs = (panels + 1) // 2
    start = places["pair", pairs - 1] - half
    holder = half_scr[start : start + LANES, :].astype(F32)
    for j in range(panels):
        first = middle if j >= middle else 0
        if j == middle:
            copies[0].start()
        if j % 2 == 0:
            start = places["pair", j // 2] - half
            block = half_scr[start : start + LANES, :]
            turned = dot_nt(unit, block)
            block = block.astype(F32)
            wide = min(LANES, rows_two - j * LANES)
            rows = slice(j * LANES, j * LANES + wide)
            factor[rows, rows] = (first_of(block, turned) * scale)[:wide, :wide]
            if j + 1 < panels:
                rows = slice((j + 1) * LANES, (j + 2) * LANES)
                diagonal = holder[used + j // 2 : used + j // 2 + 1, :]
                factor[rows, rows] = second_of(block, turned, diagonal) * scale
        if j == first:
            continue
        wide = min(LANES, rows_two - j * LANES)
        start = places["block", first, j] - half
        panel = half_scr[start : start + (j - first) * LANES, :]
        columns, rows = slice(j * LANES, j * LANES + wide), slice(first * LANES, j * LANES)
        factor[rows, columns] = (panel.astype(F32) * scale)[:, :wide]
        factor[columns, rows] = (dot_nt(unit, panel) * scale)[:wide, :]
    copies[1].start()


def own_half_kernel(places, panels, middle, scale, mine_ref, out_ref, half_scr, factor, sems):
    gathered_half(mine_ref, half_scr)
    core = lax.axis_index("batch")
    rest = (places, panels, middle, scale, half_scr, factor, out_ref, sems)
    pl.when(core == 0)(functools.partial(write_first_half, *rest))
    pl.when(core == 1)(functools.partial(write_second_half, *rest))
    where = (middle, factor, out_ref, sems)
    pl.when(core == 0)(lambda: wait_for(first_half_copies(*where)))
    pl.when(core == 1)(lambda: wait_for(second_half_copies(*where)))


def unpack_kernel(
    places, panels, middle, scale_one, scale_two, begun_ref, mine_ref, came_ref,
    in_one_out, in_two_ref, out_one_out, out_two_out, weight_one_out, weight_two_out,
    packed, small, factor, in_one_ref, out_one_ref, out_two_ref, weight_one_ref, weight_two_ref, sems,
):
    core = lax.axis_index("batch")
    gathered_half(mine_ref, packed.at[core])
    gathered_half(came_ref, packed.at[1 - core])
    rest = (places, panels, middle, scale_two)
    pl.when(core == 1)(functools.partial(write_first_half, *rest, packed.at[0], factor, in_two_ref, sems))
    pl.when(core == 0)(functools.partial(write_second_half, *rest, packed.at[1], factor, in_two_ref, sems))
    out_chan, rows_two = weight_two_ref.shape
    hidden, rows_one = weight_one_ref.shape
    owners = mine_ref.shape[0]
    tall_large, tall_small = packed.shape[1] // owners, small.shape[0] // owners
    for owner in range(owners):
        rows = slice(tall_large, tall_large + tall_small)
        small[owner * tall_small : (owner + 1) * tall_small, :] = mine_ref[owner, rows, :].astype(F32) + came_ref[
            owner, rows, :
        ].astype(F32)
    half = packed.shape[1]

    def get(name, count):
        side, row = divmod(places[name], half)
        return packed[side, row : row + count, :].astype(F32)

    used = rows_two - (panels - 1) * LANES
    spare = LANES - used
    lane = lax.broadcasted_iota(jnp.int32, (1, LANES), 1)
    last = jnp.zeros((out_chan, LANES), F32)
    for i in range(-(-used // spare)):
        piece = pltpu.roll(get(("block", i, panels - 1), out_chan), LANES - (used - i * spare), axis=1)
        last = jnp.where((lane >= i * spare) & (lane < (i + 1) * spare), piece, last)
    for j in range(panels - 1):
        weight_two_ref[:, j * LANES : (j + 1) * LANES] = get(("weight_two", j), out_chan)
    weight_two_ref[:, (panels - 1) * LANES :] = last[:, :used]
    copies = [pltpu.make_async_copy(weight_two_ref, weight_two_out, sems.at[2])]
    copies[0].start()
    pairs = (panels + 1) // 2
    block = get(("pair", pairs - 1), LANES)
    diagonal = block[used + pairs - 1 : used + pairs, :]
    out_two_ref[...] = second_of(block, block.T, diagonal)[:out_chan, :out_chan]
    in_one, weight_one, out_one = unpack_small(small[...], rows_one, hidden)
    in_one_ref[...] = in_one * scale_one
    weight_one_ref[...] = weight_one
    out_one_ref[...] = out_one
    results = ((in_one_ref, in_one_out), (out_one_ref, out_one_out), (out_two_ref, out_two_out))
    for at, (here, there) in enumerate(results + ((weight_one_ref, weight_one_out),)):
        copies.append(pltpu.make_async_copy(here, there, sems.at[3 + at]))
        copies[-1].start()
    wait_for(copies)
    where = (middle, factor, in_two_ref, sems)
    pl.when(core == 1)(lambda: wait_for(first_half_copies(*where)))
    pl.when(core == 0)(lambda: wait_for(second_half_copies(*where)))


def cube_size(space):
    return 8 if space % 8 == 0 else space


def walk(size):
    return [at ^ (at >> 1) for at in range(size)]


def exchange(parts, size):
    space = lax.axis_size("space")
    groups = [[base + at for at in walk(size)] for base in range(0, space, size)]
    return lax.all_to_all(parts, "space", split_axis=0, concat_axis=0, axis_index_groups=groups)


def from_partner(block, stride):
    return lax.ppermute(block, "space", [(i, i ^ stride) for i in range(lax.axis_size("space"))])


def call(kernel, out_shape, scratch=(), micros=3, mib=24, **more):
    return pl.pallas_call(
        kernel,
        out_shape=out_shape,
        scratch_shapes=list(scratch),
        cost_estimate=pl.CostEstimate(flops=int(micros * 1.1e9), bytes_accessed=1 << 20, transcendentals=0),
        compiler_params=pltpu.CompilerParams(vmem_limit_bytes=mib * MIB),
        **more,
    )


def passed_along(block, axis, distance):
    devices = range(lax.axis_size(axis))
    route = [(i - distance, i) for i in devices if i - distance in devices]
    return lax.ppermute(block, axis, route)


def swapped(block):
    return lax.ppermute(block, "batch", [(0, 1), (1, 0)])


def like(shape, kind=BF16):
    return jax.ShapeDtypeStruct(shape, kind)


def split_scratch(count, plane):
    return [
        pltpu.VMEM((count * (plane + 8) + 16, plane), F32),
        pltpu.VMEM((count * 40, 4 * plane), BF16),
        pltpu.VMEM((8 * up_to(25 * count, 16) + 8, LANES), F32),
    ]


def local(volume, kernel_one, kernel_two, cotangent):
    channels, _, own, plane, _ = volume.shape
    rows_one, hidden = kernel_one.shape
    rows_two, out_chan = kernel_two.shape
    cells = cotangent.shape[3]
    side = math.isqrt(cells)
    space = lax.axis_size("space")
    devices_all = space * lax.axis_size("batch")
    total_one = devices_all * 8 * cells
    total_two = devices_all * cells
    rows_pad = up_to(rows_one, 16)
    halo = own - 1
    halo_width = up_to(25 * channels * halo, 16)
    own_width = up_to(25 * channels * own, 16)
    tall = 4 * hidden

    vol = volume.reshape(channels, own, plane, plane)
    halo_block = passed_along(vol[:, own - halo :], "space", 1)
    halo_rows = jnp.asarray(patch_rows(channels, 0, halo, (0, 1), rows_pad), BF16)
    own_rows = jnp.asarray(patch_rows(channels, halo, own, (1, 2), rows_pad), BF16)
    split = jnp.asarray(split_columns(plane, side), BF16)
    halo_wide, own_wide, back = call(
        prepare_kernel,
        (like((2 * tall, halo_width)), like((2 * tall, own_width)), like((2 * tall, 8 * out_chan))),
        [pltpu.VMEM((rows_two + 32, LANES), F32)],
        micros=3,
    )(kernel_one.T, kernel_two.T, halo_rows, own_rows)
    part, act_high, slope_high, p1, in_one_part = call(
        own_kernel,
        (
            like((tall, cells), F32),
            like((tall, cells), F32),
            like((tall, cells), F32),
            like((8, rows_pad, cells)),
            like((rows_pad, rows_pad), F32),
        ),
        split_scratch(channels * own, plane) + [pltpu.VMEM((own_width, cells), BF16)],
        micros=6,
    )(vol, own_wide, split, own_rows)
    panels, middle, places, large_rows = large_places(rows_two, out_chan)
    feat_rows = out_chan * cells // space // LANES
    feat_tall = up_to(feat_rows, 16)
    cube = cube_size(space)
    cubes = space // cube
    grad_two, p2, slope_low, p1_low, *feats = call(
        functools.partial(forward_kernel, 1.0 / math.sqrt(total_two)),
        (
            like((out_chan, cells)),
            like((panels * LANES, cells)),
            like((tall, cells), F32),
            like((4, rows_pad, cells)),
        )
        + (like((cube, feat_tall, LANES)),) * cubes,
        split_scratch(channels * halo, plane)
        + [pltpu.VMEM((halo_width, cells), BF16)]
        + [pltpu.VMEM((rows_two * (cells // LANES) + 32, LANES), F32), pltpu.VMEM((space, feat_tall, LANES), BF16)],
        micros=5,
    )(halo_block, halo_wide, split, part, act_high, kernel_two.T, cotangent.reshape(out_chan, cells), halo_rows[4:], p1)
    feats = feats[:1] + [from_partner(feats[change], change * cube) for change in range(1, cubes)]
    above = passed_along(grad_two, "space", -1)

    half = large_rows // 2
    small_rows = LANES
    chunk = (half + small_rows) // cube
    mine, other, done = call(
        functools.partial(sums_kernel, places, rows_two),
        (like((half, LANES)), like((half, LANES)), like((8, LANES), F32)),
        [pltpu.VMEM((2, panels * LANES, 2 * LANES), F32)],
        micros=0.1,
    )(p2, grad_two)
    came = swapped(other)
    in_one_low, low, high = call(
        low_kernel,
        (like((rows_pad, rows_pad), F32), like((hidden, rows_pad + hidden), F32), like((tall, cells), F32)),
        [pltpu.VMEM((4 * out_chan, cells), BF16)],
        micros=0.1,
    )(grad_two, back, slope_low, p1_low, in_one_part, done)
    small = call(
        high_kernel,
        like((small_rows, LANES)),
        [pltpu.VMEM((4 * out_chan, cells), BF16)],
        micros=0.1,
    )(above, back, high, slope_high, p1, in_one_low, low)
    tail = call(
        tail_kernel, like((cube, small_rows // cube + cubes * feat_tall, LANES)), micros=12
    )(small, *feats)
    joined = call(joined_kernel, like((cube, chunk + cubes * feat_tall, LANES)), micros=1)(mine, came, tail)
    total, feat = call(
        total_kernel, (like((chunk, LANES)), like((cube, cubes * feat_tall, LANES))), micros=1
    )(exchange(joined, cube))
    stride = cube
    while 2 * stride < space:
        total = (total.astype(F32) + from_partner(total, stride).astype(F32)).astype(BF16)
        stride *= 2
    features = call(
        functools.partial(features_kernel, feat_rows, cubes),
        like((out_chan, space, cells // space)),
        [pltpu.VMEM(((space + 1) * feat_tall, LANES), F32)],
        micros=1,
    )(feat)
    other = from_partner(total, stride) if stride < space else jnp.zeros_like(total)
    other, features = lax.optimization_barrier((other, features))
    copies = call(pair_kernel, like((cube, chunk, LANES)), micros=1)(total, other)
    mine = exchange(copies, cube)
    came = swapped(mine)
    anywhere = pl.BlockSpec(memory_space=pl.ANY)
    begun = call(
        functools.partial(own_half_kernel, places, panels, middle, 1.0 / total_two),
        like((rows_two, rows_two), F32),
        [
            pltpu.VMEM((half, LANES), BF16),
            pltpu.VMEM((rows_two, rows_two), F32),
            pltpu.SemaphoreType.DMA((2,)),
        ],
        micros=2,
        out_specs=anywhere,
    )(mine)
    kinds = [
        like(shape, F32)
        for shape in (
            (rows_one, rows_one),
            (rows_two, rows_two),
            (hidden, hidden),
            (out_chan, out_chan),
            (hidden, rows_one),
            (out_chan, rows_two),
        )
    ]
    in_one, in_two, out_one, out_two, weight_one, weight_two = call(
        functools.partial(unpack_kernel, places, panels, middle, 1.0 / total_one, 1.0 / total_two),
        tuple(kinds),
        [
            pltpu.VMEM((2, half, LANES), BF16),
            pltpu.VMEM((small_rows, LANES), F32),
            pltpu.VMEM((rows_two, rows_two), F32),
        ]
        + [pltpu.VMEM(kind.shape, F32) for at, kind in enumerate(kinds) if at != 1]
        + [pltpu.SemaphoreType.DMA((7,))],
        micros=2,
        in_specs=[anywhere, pl.BlockSpec(memory_space=pltpu.VMEM), pl.BlockSpec(memory_space=pltpu.VMEM)],
        out_specs=(anywhere,) * 6,
        input_output_aliases={0: 1},
    )(begun, mine, came)
    features = features.reshape(out_chan, 1, space, cells // space)
    return features, in_one, in_two, out_one, out_two, weight_one.T, weight_two.T


def solution(mesh):
    placed = (P(None, "batch", "space", None, None), P(), P(), P(None, "batch", "space", None))
    return jax.shard_map(
        local,
        mesh=mesh,
        in_specs=placed,
        out_specs=(P(None, "batch", None, "space"), P(), P(), P(), P(), P(), P()),
        check_vma=False,
    )
```

```python
import functools
import math

import jax
import jax.numpy as jnp
import numpy as np
from jax import lax
from jax.experimental import pallas as pl
from jax.experimental.pallas import tpu as pltpu
from jax.sharding import PartitionSpec as P

F32 = jnp.float32
BF16 = jnp.bfloat16
LANES = 128
TAPS = 27
MIB = 1024 * 1024


def up_to(count, unit):
    return -(-count // unit) * unit


def split_columns(plane, quarter):
    table = np.zeros((4, plane, 5, 4, quarter), np.float32)
    for group in range(4):
        for q in range(5):
            for cell in range(quarter):
                x = 4 * cell + q - 1
                if 0 <= x < plane:
                    table[group, x, q, group, cell] = 1.0
    return table.reshape(4 * plane, 5 * 4 * quarter)


def patch_rows(channels, first, planes, hidden_planes, rows):
    width = up_to(25 * channels * planes, 16)
    table = np.zeros((len(hidden_planes), 2, 2, rows, width), np.float32)
    for at, j in enumerate(hidden_planes):
        for a in range(3):
            plane = 2 * j + a - first
            if not 0 <= plane < planes:
                continue
            for py, px, c, b, e in np.ndindex(2, 2, channels, 3, 3):
                source = (((2 * px + e) * channels + c) * planes + plane) * 5 + 2 * py + b
                table[at, py, px, c * TAPS + a * 9 + b * 3 + e, source] = 1.0
    return table.reshape(len(hidden_planes) * 4, rows, width)


def dot(first, second):
    return jnp.dot(first, second, preferred_element_type=F32)


def dot_nt(first, second):
    return lax.dot_general(first, second, (((1,), (1,)), ((), ())), preferred_element_type=F32)


def gelu_parts(value):
    square = value * value
    tangent = jnp.tanh(0.7978845608028654 * (value + 0.044715 * value * square))
    half = 0.5 * (1.0 + tangent)
    return value * half, half, tangent, square


def gelu_and_slope(value):
    act, half, tangent, square = gelu_parts(value)
    slope = half + 0.5 * value * (1.0 - tangent * tangent) * (
        0.7978845608028654 * (1.0 + 3.0 * 0.044715 * square)
    )
    return act, slope


def prepare_kernel(k1t_ref, k2t_ref, halo_rows_ref, own_rows_ref, halo_wide_ref, own_wide_ref, back_ref, k2_rows):
    hidden, rows_one = k1t_ref.shape
    rows_pad = halo_rows_ref.shape[1]
    k1t = jnp.pad(k1t_ref[...].astype(F32), ((0, 0), (0, rows_pad - rows_one))).astype(BF16)
    for rows_ref, wide_ref in ((halo_rows_ref, halo_wide_ref), (own_rows_ref, own_wide_ref)):
        for block in range(rows_ref.shape[0]):
            wide_ref[block * hidden : (block + 1) * hidden, :] = dot(k1t, rows_ref[block]).astype(BF16)
    out_chan, rows_two = k2t_ref.shape
    for at in range(0, rows_two, LANES):
        tall = min(LANES, rows_two - at)
        block = k2t_ref[:, at : at + tall].astype(F32)
        if tall < LANES:
            block = jnp.pad(block, ((0, 0), (0, LANES - tall)))
        k2_rows[at : at + tall, :out_chan] = block.T[:tall, :]
    taps = [k2_rows[pl.ds(tap, hidden, stride=TAPS), :][:, :out_chan] for tap in range(TAPS)]
    nothing = jnp.zeros_like(taps[0])

    def tap_for(parity, shift):
        if parity == 0:
            return 1 if shift == 0 else None
        return 2 if shift == 0 else 0

    for j in (1, 2):
        for py in range(2):
            for px in range(2):
                blocks = []
                for above in range(2):
                    a = {(1, 0): 1, (2, 0): 2, (2, 1): 0}.get((j, above))
                    for sy in range(2):
                        for sx in range(2):
                            b, e = tap_for(py, sy), tap_for(px, sx)
                            there = a is not None and b is not None and e is not None
                            blocks.append(taps[a * 9 + b * 3 + e] if there else nothing)
                start = ((j - 1) * 4 + py * 2 + px) * hidden
                back_ref[start : start + hidden, :] = jnp.concatenate(blocks, axis=1).astype(BF16)


def split_cells(planes, split_ref, cells_ref, rows_scr, lhs_scr, cells_scr):
    plane = planes[0].shape[0]
    pitch = plane + 8
    for at, source in enumerate(planes):
        start = at * pitch
        rows_scr[start : start + 8, :] = jnp.zeros((8, plane), F32)
        rows_scr[start + 8 : start + pitch, :] = source[...].astype(F32)
    for pair in range(len(planes) // 2):
        pieces = []
        for member in range(2):
            start = (pair * 2 + member) * pitch + 8
            tiles = [rows_scr[pl.ds(start + t, 8, stride=16), :] for t in range(-1, 16)]
            for q in range(5):
                pieces.append(jnp.concatenate([tiles[4 * group + q] for group in range(4)], axis=1))
        lhs_scr[pair * 80 : (pair + 1) * 80, :] = jnp.concatenate(pieces, axis=0).astype(BF16)
    total_rows = len(planes) * 40
    chunk = total_rows
    for part in range(total_rows // chunk):
        product = dot(lhs_scr[part * chunk : (part + 1) * chunk, :], split_ref[...])
        for q in range(5):
            start = q * total_rows + part * chunk
            cells_scr[start : start + chunk, :] = product[:, q * LANES : (q + 1) * LANES]
    filled = 5 * total_rows
    width = cells_ref.shape[0]
    if filled < 8 * width:
        cells_scr[filled : 8 * width, :] = jnp.zeros((8 * width - filled, LANES), F32)
    for yh in range(8):
        cells_ref[:, yh * LANES : (yh + 1) * LANES] = cells_scr[pl.ds(yh, width, stride=8), :].astype(BF16)


def own_kernel(
    vol_ref, wide_ref, split_ref, rows_ref,
    part_ref, act_ref, slope_ref, p1_ref, in_one_ref, rows_scr, lhs_scr, cells_scr, cells_ref,
):
    channels, own = vol_ref.shape[0], vol_ref.shape[1]
    planes = [vol_ref.at[c, z] for c in range(channels) for z in range(own)]
    split_cells(planes, split_ref, cells_ref, rows_scr, lhs_scr, cells_scr)
    pre = dot(wide_ref[...], cells_ref[...])
    tall = part_ref.shape[0]
    part_ref[...] = pre[:tall, :]
    quarter = tall // 4
    for at in range(0, tall, quarter):
        act, slope = gelu_and_slope(pre[tall + at : tall + at + quarter, :])
        act_ref[at : at + quarter, :] = act
        slope_ref[at : at + quarter, :] = slope
    blocks, rows_pad, width = rows_ref.shape
    p1 = dot(rows_ref[...].reshape(blocks * rows_pad, width), cells_ref[...]).astype(BF16)
    total = jnp.zeros((rows_pad, rows_pad), F32)
    for block in range(blocks):
        piece = p1[block * rows_pad : (block + 1) * rows_pad, :]
        p1_ref[block] = piece
        if block >= blocks // 2:
            total += dot_nt(piece, piece)
    in_one_ref[...] = total


def forward_kernel(
    scale, halo_ref, wide_ref, split_ref, part_ref, act_ref, k2t_ref, cot_ref, rows_ref, p1_ref,
    grad_ref, p2_ref, slope_ref, low_ref, *rest,
):
    feat_refs, (rows_scr, lhs_scr, cells_scr, cells_ref, p2_scr, feat_scr) = rest[:-6], rest[-6:]
    channels, halo = halo_ref.shape[0], halo_ref.shape[1]
    planes = [halo_ref.at[c, z] for c in range(channels) for z in range(halo)]
    split_cells(planes, split_ref, cells_ref, rows_scr, lhs_scr, cells_scr)
    cells = cells_ref.shape[1]
    lane = lax.broadcasted_iota(jnp.int32, (1, cells), 1)
    side = math.isqrt(cells)
    not_left = (lane % side) != 0
    not_top = lane >= side
    tall = part_ref.shape[0]
    hidden = tall // 4
    rows_two = hidden * TAPS
    part, rows_pad, width = rows_ref.shape
    both = jnp.concatenate([wide_ref[...], rows_ref[...].reshape(part * rows_pad, width)], axis=0)
    product = dot(both, cells_ref[...])
    for at in range(part):
        start = 2 * tall + at * rows_pad
        low_ref[at] = (product[start : start + rows_pad, :] + p1_ref[at].astype(F32)).astype(BF16)
    for j in (2, 1, 0):
        if j < 2:
            pre = product[j * tall : (j + 1) * tall, :]
            if j == 1:
                pre = pre + part_ref[...]
        for parity in range(4):
            rows = slice(parity * hidden, (parity + 1) * hidden)
            if j == 2:
                act = act_ref[rows, :]
            elif j == 1:
                act, slope = gelu_and_slope(pre[rows, :])
                slope_ref[rows, :] = slope
            else:
                act = gelu_parts(pre[rows, :])[0]
            py, px = parity // 2, parity % 2
            for b in ((1,) if py == 0 else (2, 0)):
                for e in ((1,) if px == 0 else (2, 0)):
                    moved = act
                    distance = (side if b == 0 else 0) + (1 if e == 0 else 0)
                    if distance:
                        moved = pltpu.roll(act, distance, axis=1)
                    if b == 0:
                        moved = jnp.where(not_top, moved, 0.0)
                    if e == 0:
                        moved = jnp.where(not_left, moved, 0.0)
                    for k in range(cells // LANES):
                        start = k * rows_two + j * 9 + b * 3 + e
                        p2_scr[pl.ds(start, hidden, stride=TAPS), :] = moved[:, k * LANES : (k + 1) * LANES]
    for k in range(cells // LANES):
        p2_ref[:rows_two, k * LANES : (k + 1) * LANES] = p2_scr[k * rows_two : (k + 1) * rows_two, :].astype(BF16)
    p2_ref[rows_two:, :] = jnp.zeros((p2_ref.shape[0] - rows_two, cells), BF16)
    act, slope = gelu_and_slope(dot(k2t_ref[...], p2_ref[:rows_two, :]))
    grad_ref[...] = (cot_ref[...].astype(F32) * scale * slope).astype(BF16)
    owned = cells // feat_scr.shape[0]
    rows = act.shape[0] * owned // LANES
    count = LANES // owned
    place = lax.broadcasted_iota(jnp.int32, (1, LANES), 1) // owned
    for k in range(cells // LANES):
        tile = act[:, k * LANES : (k + 1) * LANES]
        for u in range(count):
            total = jnp.zeros((rows, LANES), F32)
            for m in range(count):
                block = tile[m * rows : (m + 1) * rows, :]
                if m != u:
                    block = pltpu.roll(block, ((m - u) * owned) % LANES, axis=1)
                total = jnp.where(place == m, block, total)
            if rows < feat_scr.shape[1]:
                total = jnp.pad(total, ((0, feat_scr.shape[1] - rows), (0, 0)))
            feat_scr[k * count + u] = total.astype(BF16)
    owners = feat_refs[0].shape[0]
    cube = lax.axis_index("space") // owners
    for change, feat_ref in enumerate(feat_refs):
        feat_ref[...] = feat_scr[pl.ds((cube ^ change) * owners, owners)]


def large_places(rows_two, out_chan):
    panels = -(-rows_two // LANES)
    pairs = (panels + 1) // 2
    middle = pairs // 2 * 2
    names = [("block", i, j) for j in range(middle, panels) for i in range(middle)]
    names += [("block", i, j) for j in range(middle) for i in range(j)]
    names += [("block", i, j) for j in range(middle, panels) for i in range(middle, j)]
    names += [("pair", p) for p in range(pairs)]
    cross = middle * (panels - middle)
    weights = [("weight_two", j) for j in range(panels - 1)]
    half = (len(names) * LANES + len(weights) * out_chan) // 2
    early = (half - cross * LANES) // out_chan
    order = [(name, LANES) for name in names[:cross]] + [(name, out_chan) for name in weights[:early]]
    order += [(name, LANES) for name in names[cross:]] + [(name, out_chan) for name in weights[early:]]
    places, at = {}, 0
    for name, rows in order:
        places[name] = at
        at += rows
    return panels, middle, places, at


def square_iotas():
    return (
        lax.broadcasted_iota(jnp.int32, (LANES, LANES), 0),
        lax.broadcasted_iota(jnp.int32, (LANES, LANES), 1),
    )


def diagonal_row(block):
    row, col = square_iotas()
    return jnp.sum(jnp.where(row == col, block, 0.0), axis=0, keepdims=True)


def two_in_one(upper, lower):
    row, col = square_iotas()
    return jnp.where(row <= col, upper, lower)


def first_of(block, turned):
    row, col = square_iotas()
    return jnp.where(row <= col, block, turned)


def second_of(block, turned, diagonal):
    row, col = square_iotas()
    return jnp.where(row > col, block, jnp.where(row == col, diagonal, turned))


def square(block):
    return jnp.pad(block, ((0, LANES - block.shape[0]), (0, LANES - block.shape[1])))


def padded_lanes(block):
    return jnp.pad(block, ((0, 0), (0, LANES - block.shape[1])))


def put(halves, at, block):
    half = halves[0].shape[0]
    done = 0
    while done < block.shape[0]:
        side, row = divmod(at + done, half)
        count = min(block.shape[0] - done, half - row)
        halves[side][row : row + count, :] = block[done : done + count, :].astype(BF16)
        done += count


def sums_kernel(
    places, rows_two, p2_ref, grad_ref, mine_ref, other_ref, done_ref, product_scr,
):
    done_ref[...] = jnp.zeros_like(done_ref)
    core = lax.axis_index("batch")
    rest = (places, rows_two, p2_ref, grad_ref, product_scr)
    pl.when(core == 0)(lambda: write_sums(*rest, (mine_ref, other_ref)))
    pl.when(core == 1)(lambda: write_sums(*rest, (other_ref, mine_ref)))


def write_sums(places, rows_two, p2_ref, grad_ref, product_scr, packed):
    panels = p2_ref.shape[0] // LANES
    used = rows_two - (panels - 1) * LANES
    lane = lax.broadcasted_iota(jnp.int32, (1, LANES), 1)
    weight_two = dot_nt(grad_ref[...], p2_ref[...])
    out_chan = weight_two.shape[0]
    last = weight_two[:, (panels - 1) * LANES :]
    spare = LANES - used
    diagonals = []
    for j in range(0, panels, 2):
        wide = min(2, panels - j)
        tall = (j + wide) * LANES
        product = product_scr.at[(j // 2) % 2]
        product[:tall, : wide * LANES] = dot_nt(p2_ref[:tall, :], p2_ref[j * LANES : tall, :])
        for k in range(wide):
            columns = slice(k * LANES, (k + 1) * LANES)
            for i in range(j + k):
                block = product[i * LANES : (i + 1) * LANES, columns]
                if j + k == panels - 1 and i * spare < used:
                    piece = pltpu.roll(last, used - i * spare, axis=1)
                    top = jnp.where(lane >= used, piece, block[:out_chan, :])
                    block = jnp.concatenate([top, block[out_chan:, :]], axis=0)
                put(packed, places["block", i, j + k], block)
        first = product[j * LANES : (j + 1) * LANES, :LANES]
        if wide == 2:
            second = product[(j + 1) * LANES : tall, LANES:]
        else:
            second = square(dot_nt(grad_ref[...], grad_ref[...]))
        diagonals.append(diagonal_row(second))
        block = two_in_one(first, second)
        if wide == 1:
            row, _ = square_iotas()
            for at, diagonal in enumerate(diagonals):
                block = jnp.where(row == used + at, diagonal, block)
        put(packed, places["pair", j // 2], block)
    for j in range(panels - 1):
        put(packed, places["weight_two", j], weight_two[:, j * LANES : (j + 1) * LANES])


def shifted_up(source, scr):
    out_chan, cells = source.shape
    side = math.isqrt(cells)
    lane = lax.broadcasted_iota(jnp.int32, (1, cells), 1)
    value = source[...].astype(F32)
    for sy in range(2):
        for sx in range(2):
            moved = value
            distance = sy * side + sx
            if distance:
                moved = pltpu.roll(value, cells - distance, axis=1)
            if sy:
                moved = jnp.where(lane < cells - side, moved, 0.0)
            if sx:
                moved = jnp.where((lane % side) != side - 1, moved, 0.0)
            at = (2 * sy + sx) * out_chan
            scr[at : at + out_chan, :] = moved.astype(BF16)


def low_kernel(
    grad_ref, back_ref, slope_ref, p1_ref, in_one_ref, done_ref,
    in_one_out, low_out, high_ref, scr,
):
    part, rows_pad, _ = p1_ref.shape
    shifted_up(grad_ref, scr)
    tall = high_ref.shape[0]
    hidden = tall // part
    grad_hidden = dot(back_ref[:, : scr.shape[0]], scr[...])
    high_ref[...] = grad_hidden[tall:, :]
    in_one = in_one_ref[...]
    total = jnp.zeros((hidden, rows_pad + hidden), F32)
    for block in range(part):
        rows = slice(block * hidden, (block + 1) * hidden)
        piece = (grad_hidden[rows, :] * slope_ref[rows, :]).astype(BF16)
        in_one += dot_nt(p1_ref[block], p1_ref[block])
        total += dot_nt(piece, jnp.concatenate([p1_ref[block], piece], axis=0))
    in_one_out[...] = in_one
    low_out[...] = total


def high_kernel(
    above_ref, back_ref, high_ref, slope_ref, p1_ref, in_one_ref, low_ref, out_ref, scr,
):
    shifted_up(above_ref, scr)
    blocks, rows_pad, _ = p1_ref.shape
    part = blocks // 2
    tall, reach = high_ref.shape[0], scr.shape[0]
    hidden = tall // part
    grad_hidden = high_ref[...] + dot(back_ref[tall:, reach:], scr[...])
    total = low_ref[...]
    for block in range(part):
        rows = slice(block * hidden, (block + 1) * hidden)
        piece = (grad_hidden[rows, :] * slope_ref[rows, :]).astype(BF16)
        total += dot_nt(piece, jnp.concatenate([p1_ref[part + block], piece], axis=0))
    weight_one, out_one = total[:, :rows_pad], total[:, rows_pad:]
    out_ref[...] = pack_small(in_one_ref[...], weight_one, out_one).astype(BF16)


SMALL_DIAGONAL = 108
SMALL_WEIGHT = 64
SMALL_REST = 112


def pack_small(in_one, weight_one, out_one):
    row, col = square_iotas()
    hidden = weight_one.shape[0]
    half = hidden // 2
    wide = padded_lanes(weight_one)
    out_square = square(out_one)
    block = jnp.where(row <= col, square(in_one), jnp.where(row < hidden, out_square, 0.0))
    block = jnp.where(row == SMALL_DIAGONAL, diagonal_row(out_square), block)
    first = jnp.pad(wide, ((SMALL_WEIGHT, LANES - SMALL_WEIGHT - hidden), (0, 0)))
    block = jnp.where((row >= SMALL_WEIGHT) & (row < SMALL_WEIGHT + hidden) & (col < SMALL_WEIGHT), first, block)
    turned = pltpu.roll(wide[half:, :], LANES - SMALL_WEIGHT, axis=1)
    lane = lax.broadcasted_iota(jnp.int32, (half, LANES), 1)
    rest = jnp.where(lane >= SMALL_WEIGHT, wide[:half, :], turned)
    return jnp.where(row >= SMALL_REST, jnp.pad(rest, ((SMALL_REST, 0), (0, 0))), block)


def unpack_small(block, rows_one, hidden):
    half = hidden // 2
    turned = block.T
    in_one = first_of(block, turned)[:rows_one, :rows_one]
    out_one = second_of(block, turned, block[SMALL_DIAGONAL : SMALL_DIAGONAL + 1, :])[:hidden, :hidden]
    rest = block[SMALL_REST:, :]
    lane = lax.broadcasted_iota(jnp.int32, (hidden, LANES), 1)
    high = jnp.concatenate([rest, pltpu.roll(rest, SMALL_WEIGHT, axis=1)], axis=0)
    weight_one = jnp.where(lane < SMALL_WEIGHT, block[SMALL_WEIGHT : SMALL_WEIGHT + hidden, :], high)
    return in_one, weight_one[:, :rows_one], out_one


def joined_kernel(mine_ref, came_ref, small_ref, *refs):
    feat_refs, out_ref = refs[:-1], refs[-1]
    owners = out_ref.shape[0]
    large, small = mine_ref.shape[0] // owners, small_ref.shape[0] // owners
    feat_rows = feat_refs[0].shape[1]
    for owner in range(owners):
        rows = slice(owner * large, (owner + 1) * large)
        out_ref[owner, :large, :] = (mine_ref[rows, :].astype(F32) + came_ref[rows, :].astype(F32)).astype(BF16)
        out_ref[owner, large : large + small, :] = small_ref[owner * small : (owner + 1) * small, :]
        for change, feat_ref in enumerate(feat_refs):
            start = large + small + change * feat_rows
            out_ref[owner, start : start + feat_rows, :] = feat_ref[walk(owners)[owner]]


def total_kernel(came_ref, out_ref, feat_ref):
    owners, chunk = came_ref.shape[0], out_ref.shape[0]
    total = came_ref[0, :chunk, :].astype(F32)
    for owner in range(1, owners):
        total += came_ref[owner, :chunk, :].astype(F32)
    out_ref[...] = total.astype(BF16)
    for owner in range(owners):
        feat_ref[owner] = came_ref[owner, chunk:, :]


def pair_kernel(mine_ref, came_ref, out_ref):
    total = (mine_ref[...].astype(F32) + came_ref[...].astype(F32)).astype(BF16)
    for owner in range(out_ref.shape[0]):
        out_ref[owner] = total


def features_kernel(owned_rows, cubes, feat_ref, out_ref, scr):
    owners, owned = out_ref.shape[1], out_ref.shape[2]
    rows = feat_ref.shape[1] // cubes
    members = owners // cubes
    cube = lax.axis_index("space") // members
    for change in range(cubes):
        for member in range(members):
            start = pl.multiple_of(((cube ^ change) * members + walk(members)[member]) * rows, 16)
            scr[pl.ds(start, rows), :] = feat_ref[member, change * rows : (change + 1) * rows, :].astype(F32)
    for i in range(owned_rows):
        block = scr[pl.ds(i, owners, stride=rows), :]
        for m in range(LANES // owned):
            out_ref[m * owned_rows + i] = block[:, m * owned : (m + 1) * owned].astype(BF16)


def gathered_half(source_ref, half_scr):
    owners = source_ref.shape[0]
    tall = half_scr.shape[0] // owners
    for owner in range(owners):
        half_scr[owner * tall : (owner + 1) * tall, :] = source_ref[owner, :tall, :]


def unit_square():
    row, col = square_iotas()
    return jnp.where(row == col, 1.0, 0.0).astype(BF16)


def first_half_copies(middle, factor, out_ref, sems):
    rows_two, split = out_ref.shape[0], middle * LANES
    spots = [(slice(0, split), slice(split, rows_two)), (slice(split, rows_two), slice(0, split))]
    return [pltpu.make_async_copy(factor.at[spot], out_ref.at[spot], sems.at[at]) for at, spot in enumerate(spots)]


def second_half_copies(middle, factor, out_ref, sems):
    rows_two, split = out_ref.shape[0], middle * LANES
    spots = [(slice(0, split), slice(0, split)), (slice(split, rows_two), slice(split, rows_two))]
    return [pltpu.make_async_copy(factor.at[spot], out_ref.at[spot], sems.at[at]) for at, spot in enumerate(spots)]


def wait_for(copies):
    for copy in copies:
        copy.wait()


def write_first_half(places, panels, middle, scale, half_scr, factor, out_ref, sems):
    copies = first_half_copies(middle, factor, out_ref, sems)
    rows_two = out_ref.shape[0]
    split = middle * LANES
    unit = unit_square()
    for j in range(middle, panels):
        wide = min(LANES, rows_two - j * LANES)
        start = places["block", 0, j]
        panel = half_scr[start : start + split, :]
        columns = slice(j * LANES, j * LANES + wide)
        factor[:split, columns] = (panel.astype(F32) * scale)[:, :wide]
        factor[columns, :split] = (dot_nt(unit, panel) * scale)[:wide, :]
    for copy in copies:
        copy.start()


def write_second_half(places, panels, middle, scale, half_scr, factor, out_ref, sems):
    copies = second_half_copies(middle, factor, out_ref, sems)
    rows_two = out_ref.shape[0]
    half = half_scr.shape[0]
    unit = unit_square()
    used = rows_two - (panels - 1) * LANES
    pairs = (panels + 1) // 2
    start = places["pair", pairs - 1] - half
    holder = half_scr[start : start + LANES, :].astype(F32)
    for j in range(panels):
        first = middle if j >= middle else 0
        if j == middle:
            copies[0].start()
        if j % 2 == 0:
            start = places["pair", j // 2] - half
            block = half_scr[start : start + LANES, :]
            turned = dot_nt(unit, block)
            block = block.astype(F32)
            wide = min(LANES, rows_two - j * LANES)
            rows = slice(j * LANES, j * LANES + wide)
            factor[rows, rows] = (first_of(block, turned) * scale)[:wide, :wide]
            if j + 1 < panels:
                rows = slice((j + 1) * LANES, (j + 2) * LANES)
                diagonal = holder[used + j // 2 : used + j // 2 + 1, :]
                factor[rows, rows] = second_of(block, turned, diagonal) * scale
        if j == first:
            continue
        wide = min(LANES, rows_two - j * LANES)
        start = places["block", first, j] - half
        panel = half_scr[start : start + (j - first) * LANES, :]
        columns, rows = slice(j * LANES, j * LANES + wide), slice(first * LANES, j * LANES)
        factor[rows, columns] = (panel.astype(F32) * scale)[:, :wide]
        factor[columns, rows] = (dot_nt(unit, panel) * scale)[:wide, :]
    copies[1].start()


def own_half_kernel(places, panels, middle, scale, mine_ref, out_ref, half_scr, factor, sems):
    gathered_half(mine_ref, half_scr)
    core = lax.axis_index("batch")
    rest = (places, panels, middle, scale, half_scr, factor, out_ref, sems)
    pl.when(core == 0)(functools.partial(write_first_half, *rest))
    pl.when(core == 1)(functools.partial(write_second_half, *rest))
    where = (middle, factor, out_ref, sems)
    pl.when(core == 0)(lambda: wait_for(first_half_copies(*where)))
    pl.when(core == 1)(lambda: wait_for(second_half_copies(*where)))


def unpack_kernel(
    places, panels, middle, scale_one, scale_two, begun_ref, mine_ref, came_ref,
    in_one_out, in_two_ref, out_one_out, out_two_out, weight_one_out, weight_two_out,
    packed, small, factor, in_one_ref, out_one_ref, out_two_ref, weight_one_ref, weight_two_ref, sems,
):
    core = lax.axis_index("batch")
    gathered_half(mine_ref, packed.at[core])
    gathered_half(came_ref, packed.at[1 - core])
    rest = (places, panels, middle, scale_two)
    pl.when(core == 1)(functools.partial(write_first_half, *rest, packed.at[0], factor, in_two_ref, sems))
    pl.when(core == 0)(functools.partial(write_second_half, *rest, packed.at[1], factor, in_two_ref, sems))
    out_chan, rows_two = weight_two_ref.shape
    hidden, rows_one = weight_one_ref.shape
    owners = mine_ref.shape[0]
    tall_large, tall_small = packed.shape[1] // owners, small.shape[0] // owners
    for owner in range(owners):
        rows = slice(tall_large, tall_large + tall_small)
        small[owner * tall_small : (owner + 1) * tall_small, :] = mine_ref[owner, rows, :].astype(F32) + came_ref[
            owner, rows, :
        ].astype(F32)
    half = packed.shape[1]

    def get(name, count):
        side, row = divmod(places[name], half)
        return packed[side, row : row + count, :].astype(F32)

    used = rows_two - (panels - 1) * LANES
    spare = LANES - used
    lane = lax.broadcasted_iota(jnp.int32, (1, LANES), 1)
    last = jnp.zeros((out_chan, LANES), F32)
    for i in range(-(-used // spare)):
        piece = pltpu.roll(get(("block", i, panels - 1), out_chan), LANES - (used - i * spare), axis=1)
        last = jnp.where((lane >= i * spare) & (lane < (i + 1) * spare), piece, last)
    for j in range(panels - 1):
        weight_two_ref[:, j * LANES : (j + 1) * LANES] = get(("weight_two", j), out_chan)
    weight_two_ref[:, (panels - 1) * LANES :] = last[:, :used]
    copies = [pltpu.make_async_copy(weight_two_ref, weight_two_out, sems.at[2])]
    copies[0].start()
    pairs = (panels + 1) // 2
    block = get(("pair", pairs - 1), LANES)
    diagonal = block[used + pairs - 1 : used + pairs, :]
    out_two_ref[...] = second_of(block, block.T, diagonal)[:out_chan, :out_chan]
    in_one, weight_one, out_one = unpack_small(small[...], rows_one, hidden)
    in_one_ref[...] = in_one * scale_one
    weight_one_ref[...] = weight_one
    out_one_ref[...] = out_one
    results = ((in_one_ref, in_one_out), (out_one_ref, out_one_out), (out_two_ref, out_two_out))
    for at, (here, there) in enumerate(results + ((weight_one_ref, weight_one_out),)):
        copies.append(pltpu.make_async_copy(here, there, sems.at[3 + at]))
        copies[-1].start()
    wait_for(copies)
    where = (middle, factor, in_two_ref, sems)
    pl.when(core == 1)(lambda: wait_for(first_half_copies(*where)))
    pl.when(core == 0)(lambda: wait_for(second_half_copies(*where)))


def cube_size(space):
    return 8 if space % 8 == 0 else space


def walk(size):
    return [at ^ (at >> 1) for at in range(size)]


def exchange(parts, size):
    space = lax.axis_size("space")
    groups = [[base + at for at in walk(size)] for base in range(0, space, size)]
    return lax.all_to_all(parts, "space", split_axis=0, concat_axis=0, axis_index_groups=groups)


def from_partner(block, stride):
    return lax.ppermute(block, "space", [(i, i ^ stride) for i in range(lax.axis_size("space"))])


def call(kernel, out_shape, scratch=(), micros=3, mib=24, **more):
    return pl.pallas_call(
        kernel,
        out_shape=out_shape,
        scratch_shapes=list(scratch),
        cost_estimate=pl.CostEstimate(flops=int(micros * 1.1e9), bytes_accessed=1 << 20, transcendentals=0),
        compiler_params=pltpu.CompilerParams(vmem_limit_bytes=mib * MIB),
        **more,
    )


def passed_along(block, axis, distance):
    devices = range(lax.axis_size(axis))
    route = [(i - distance, i) for i in devices if i - distance in devices]
    return lax.ppermute(block, axis, route)


def swapped(block):
    return lax.ppermute(block, "batch", [(0, 1), (1, 0)])


def like(shape, kind=BF16):
    return jax.ShapeDtypeStruct(shape, kind)


def split_scratch(count, plane):
    return [
        pltpu.VMEM((count * (plane + 8) + 16, plane), F32),
        pltpu.VMEM((count * 40, 4 * plane), BF16),
        pltpu.VMEM((8 * up_to(25 * count, 16) + 8, LANES), F32),
    ]


def local(volume, kernel_one, kernel_two, cotangent):
    channels, _, own, plane, _ = volume.shape
    rows_one, hidden = kernel_one.shape
    rows_two, out_chan = kernel_two.shape
    cells = cotangent.shape[3]
    side = math.isqrt(cells)
    space = lax.axis_size("space")
    devices_all = space * lax.axis_size("batch")
    total_one = devices_all * 8 * cells
    total_two = devices_all * cells
    rows_pad = up_to(rows_one, 16)
    halo = own - 1
    halo_width = up_to(25 * channels * halo, 16)
    own_width = up_to(25 * channels * own, 16)
    tall = 4 * hidden

    vol = volume.reshape(channels, own, plane, plane)
    halo_block = passed_along(vol[:, own - halo :], "space", 1)
    halo_rows = jnp.asarray(patch_rows(channels, 0, halo, (0, 1), rows_pad), BF16)
    own_rows = jnp.asarray(patch_rows(channels, halo, own, (1, 2), rows_pad), BF16)
    split = jnp.asarray(split_columns(plane, side), BF16)
    halo_wide, own_wide, back = call(
        prepare_kernel,
        (like((2 * tall, halo_width)), like((2 * tall, own_width)), like((2 * tall, 8 * out_chan))),
        [pltpu.VMEM((rows_two + 32, LANES), F32)],
        micros=3,
    )(kernel_one.T, kernel_two.T, halo_rows, own_rows)
    part, act_high, slope_high, p1, in_one_part = call(
        own_kernel,
        (
            like((tall, cells), F32),
            like((tall, cells), F32),
            like((tall, cells), F32),
            like((8, rows_pad, cells)),
            like((rows_pad, rows_pad), F32),
        ),
        split_scratch(channels * own, plane) + [pltpu.VMEM((own_width, cells), BF16)],
        micros=6,
    )(vol, own_wide, split, own_rows)
    panels, middle, places, large_rows = large_places(rows_two, out_chan)
    feat_rows = out_chan * cells // space // LANES
    feat_tall = up_to(feat_rows, 16)
    cube = cube_size(space)
    cubes = space // cube
    grad_two, p2, slope_low, p1_low, *feats = call(
        functools.partial(forward_kernel, 1.0 / math.sqrt(total_two)),
        (
            like((out_chan, cells)),
            like((panels * LANES, cells)),
            like((tall, cells), F32),
            like((4, rows_pad, cells)),
        )
        + (like((cube, feat_tall, LANES)),) * cubes,
        split_scratch(channels * halo, plane)
        + [pltpu.VMEM((halo_width, cells), BF16)]
        + [pltpu.VMEM((rows_two * (cells // LANES) + 32, LANES), F32), pltpu.VMEM((space, feat_tall, LANES), BF16)],
        micros=5,
    )(halo_block, halo_wide, split, part, act_high, kernel_two.T, cotangent.reshape(out_chan, cells), halo_rows[4:], p1)
    feats = feats[:1] + [from_partner(feats[change], change * cube) for change in range(1, cubes)]
    above = passed_along(grad_two, "space", -1)
    feats, above = lax.optimization_barrier((feats, above))

    half = large_rows // 2
    small_rows = LANES
    chunk = (half + small_rows) // cube
    mine, other, done = call(
        functools.partial(sums_kernel, places, rows_two),
        (like((half, LANES)), like((half, LANES)), like((8, LANES), F32)),
        [pltpu.VMEM((2, panels * LANES, 2 * LANES), F32)],
        micros=0.1,
    )(p2, grad_two)
    came = swapped(other)
    in_one_low, low, high = call(
        low_kernel,
        (like((rows_pad, rows_pad), F32), like((hidden, rows_pad + hidden), F32), like((tall, cells), F32)),
        [pltpu.VMEM((4 * out_chan, cells), BF16)],
        micros=0.1,
    )(grad_two, back, slope_low, p1_low, in_one_part, done)
    small = call(
        high_kernel,
        like((small_rows, LANES)),
        [pltpu.VMEM((4 * out_chan, cells), BF16)],
        micros=12,
    )(above, back, high, slope_high, p1, in_one_low, low)
    joined = call(joined_kernel, like((cube, chunk + cubes * feat_tall, LANES)), micros=1)(mine, came, small, *feats)
    total, feat = call(
        total_kernel, (like((chunk, LANES)), like((cube, cubes * feat_tall, LANES))), micros=1
    )(exchange(joined, cube))
    stride = cube
    while 2 * stride < space:
        total = (total.astype(F32) + from_partner(total, stride).astype(F32)).astype(BF16)
        stride *= 2
    features = call(
        functools.partial(features_kernel, feat_rows, cubes),
        like((out_chan, space, cells // space)),
        [pltpu.VMEM(((space + 1) * feat_tall, LANES), F32)],
        micros=1,
    )(feat)
    other = from_partner(total, stride) if stride < space else jnp.zeros_like(total)
    other, features = lax.optimization_barrier((other, features))
    copies = call(pair_kernel, like((cube, chunk, LANES)), micros=1)(total, other)
    mine = exchange(copies, cube)
    came = swapped(mine)
    anywhere = pl.BlockSpec(memory_space=pl.ANY)
    begun = call(
        functools.partial(own_half_kernel, places, panels, middle, 1.0 / total_two),
        like((rows_two, rows_two), F32),
        [
            pltpu.VMEM((half, LANES), BF16),
            pltpu.VMEM((rows_two, rows_two), F32),
            pltpu.SemaphoreType.DMA((2,)),
        ],
        micros=2,
        out_specs=anywhere,
    )(mine)
    kinds = [
        like(shape, F32)
        for shape in (
            (rows_one, rows_one),
            (rows_two, rows_two),
            (hidden, hidden),
            (out_chan, out_chan),
            (hidden, rows_one),
            (out_chan, rows_two),
        )
    ]
    in_one, in_two, out_one, out_two, weight_one, weight_two = call(
        functools.partial(unpack_kernel, places, panels, middle, 1.0 / total_one, 1.0 / total_two),
        tuple(kinds),
        [
            pltpu.VMEM((2, half, LANES), BF16),
            pltpu.VMEM((small_rows, LANES), F32),
            pltpu.VMEM((rows_two, rows_two), F32),
        ]
        + [pltpu.VMEM(kind.shape, F32) for at, kind in enumerate(kinds) if at != 1]
        + [pltpu.SemaphoreType.DMA((7,))],
        micros=2,
        in_specs=[anywhere, pl.BlockSpec(memory_space=pltpu.VMEM), pl.BlockSpec(memory_space=pltpu.VMEM)],
        out_specs=(anywhere,) * 6,
        input_output_aliases={0: 1},
    )(begun, mine, came)
    features = features.reshape(out_chan, 1, space, cells // space)
    return features, in_one, in_two, out_one, out_two, weight_one.T, weight_two.T


def solution(mesh):
    placed = (P(None, "batch", "space", None, None), P(), P(), P(None, "batch", "space", None))
    return jax.shard_map(
        local,
        mesh=mesh,
        in_specs=placed,
        out_specs=(P(None, "batch", None, "space"), P(), P(), P(), P(), P(), P()),
        check_vma=False,
    )
```
